32 devices in a mesh: rep: 8 (over y, x, core), fsdp: 4 (over z).
Axes of the slice: x: 2, y: 2, z: 4, core: 2. Of those that a mesh axis runs over, the one named last changes fastest.
Arguments:
- tokens: bfloat16 [16384, 1536], P(('rep', 'fsdp')), may hold values from -6 to 6
- gain_attn: bfloat16 [1536], P('fsdp'), may hold values from 0.5 to 1.5
- w_query: bfloat16 [1536, 1536], P('fsdp'), may hold values from -0.15625 to 0.15625
- w_key: bfloat16 [1536, 768], P('fsdp'), may hold values from -0.15625 to 0.15625
- w_value: bfloat16 [1536, 768], P('fsdp'), may hold values from -0.15625 to 0.15625
- w_out: bfloat16 [1536, 1536], P('fsdp'), may hold values from -1.25 to 1.25
- gain_ffn: bfloat16 [1536], P('fsdp'), may hold values from 0.5 to 1.5
- w_gate: bfloat16 [1536, 4096], P('fsdp'), may hold values from -0.15625 to 0.15625
- w_up: bfloat16 [1536, 4096], P('fsdp'), may hold values from -0.15625 to 0.15625
- w_down: bfloat16 [4096, 1536], P('fsdp'), may hold values from -0.09375 to 0.09375
- cotangent: bfloat16 [16384, 1536], P(('rep', 'fsdp')), may hold values from -6 to 6
Outputs:
- output: bfloat16 [16384, 1536], P(('rep', 'fsdp'))
- input_grad: float32 [16384, 1536], P(('rep', 'fsdp'))
- grad_gain_attn: float32 [1536], P('fsdp')
- grad_query: float32 [1536, 1536], P('fsdp')
- grad_key: float32 [1536, 768], P('fsdp')
- grad_value: float32 [1536, 768], P('fsdp')
- grad_out: float32 [1536, 1536], P('fsdp')
- grad_gain_ffn: float32 [1536], P('fsdp')
- grad_gate: float32 [1536, 4096], P('fsdp')
- grad_up: float32 [1536, 4096], P('fsdp')
- grad_down: float32 [4096, 1536], P('fsdp')
The draws below stay inside these ranges and needn't reach their ends.
All inputs are finite; a program needn't handle non-finite values.
Results may differ from the reference program's by a relative error of at most 0.02.
Values may be sent and summed in bfloat16 or wider, within the bound.
No kernel may reach another device: no remote copies, remote signals or barrier semaphores. Data moves between devices by JAX's collectives and lax.ppermute only.
A program may use at most 320 MiB of HBM per device.

```python
import math
import jax
import jax.numpy as jnp
from jax import lax

D = 1536
HEADS = 16
KV = 8
HD = 96
FF = 4096
TOK_DEV = 512
TOKENS = 16384


def with_spikes(values, own_key, source, target, shards_of, factor):
    owner, partner = [(jnp.arange(values.shape[axis_at]) // (values.shape[axis_at] // shards_of)).reshape([-1 if axis == axis_at else 1 for axis in range(values.ndim)]) for axis_at in (source, target)]
    chosen = jax.random.permutation(own_key, shards_of)[partner]
    strong = (owner == chosen) | (owner == (partner + shards_of // 2) % shards_of)
    return jnp.where(strong, factor * values, values)


def level_of(own_key, shape, split, smallest, high):
    def one(dim, blocks):
        draws = jax.random.uniform(jax.random.fold_in(jax.random.fold_in(own_key, 6), dim), (blocks,), jnp.float32, smallest / len(split), high / len(split))
        return jnp.repeat(jnp.exp(draws), shape[dim] // blocks).reshape((-1,) + (1,) * (len(shape) - dim - 1))

    gain = one(*split[0])
    for cut in split[1:]:
        gain = gain * one(*cut)
    return gain


def noise(own_key, shape, deviation, reach, shards=(), held_as=jnp.bfloat16):
    values = jax.random.normal(own_key, shape, jnp.float32) * deviation
    if len(shards) > 0:
        values = level_of(own_key, shape, shards, -0.22, 0.18) * values
    return jnp.clip(values, min=-reach, max=reach).astype(held_as)


def bell_draw_with(stream_key, shape, spread, bound, cuts, heavy, dtype=jnp.bfloat16):
    array = spread * jax.random.normal(stream_key, shape, jnp.float32)
    if cuts:
        array = array * level_of(stream_key, shape, cuts, -0.22, 0.18)
    return jnp.clip(with_spikes(array, jax.random.fold_in(stream_key, 3), *heavy), -bound, bound).astype(dtype)


def setup_inputs(seed: int = 0) -> dict:
    key_of = jax.random.split(jax.random.key(seed), 12)
    return {
        "tokens": noise(key_of[0], (TOKENS, D), 1.0, 6.0, ((0, 32),)),
        "gain_attn": jnp.clip(1.0 + 0.1 * jax.random.normal(key_of[1], (D,), jnp.float32), 0.5, 1.5).astype(jnp.bfloat16),
        "w_query": noise(key_of[2], (D, D), D ** -0.5, 0.15625, ((0, 4),)),
        "w_key": noise(key_of[3], (D, KV * HD), D ** -0.5, 0.15625, ((0, 4),)),
        "w_value": noise(key_of[4], (D, KV * HD), D ** -0.5, 0.15625, ((0, 4),)),
        "w_out": noise(key_of[5], (D, D), (D // 64) ** -0.5, 1.25, ((0, 4),)),
        "gain_ffn": jnp.clip(1.0 + 0.1 * jax.random.normal(key_of[6], (D,), jnp.float32), 0.5, 1.5).astype(jnp.bfloat16),
        "w_gate": noise(key_of[7], (D, FF), D ** -0.5, 0.15625, ((0, 4),)),
        "w_up": noise(key_of[8], (D, FF), D ** -0.5, 0.15625, ((0, 4),)),
        "w_down": noise(key_of[9], (FF, D), FF ** -0.5, 0.09375, ((0, 4),)),
        "cotangent": bell_draw_with(key_of[10], (TOKENS, D), 1.0, 6.0, ((0, 32),), (0, 1, 32, 2.75)),
    }


@jax.custom_vjp
def low(v):
    return lax.optimization_barrier(v.astype(jnp.bfloat16)).astype(jnp.float32)

@jax.custom_vjp
def low_back(v):
    return v

def low_keep(v):
    return (low(v), None)

def low_pass(kept, grad):
    return (grad,)

def back_keep(v):
    return (v, None)

def back_low(kept, grad):
    return (low(grad),)
low.defvjp(low_keep, low_pass)
low_back.defvjp(back_keep, back_low)

def rotate(values, cosine, sine):
    half = values.shape[-1] // 2
    turned = jnp.concatenate([-values[..., half:], values[..., :half]], axis=-1)
    return values * cosine + turned * sine

def tables(length, size):
    freq = 10000.0 ** (-jnp.arange(0, size, 2).astype(jnp.float32) / size)
    angle = jnp.arange(length).astype(jnp.float32)[:, None] * freq[None, :]
    angle = jnp.concatenate([angle, angle], axis=-1)
    return (jnp.cos(angle)[:, None, :], jnp.sin(angle)[:, None, :])

def scaled_rms(values):
    return values * lax.rsqrt(lax.optimization_barrier(jnp.mean(values * values, axis=-1, keepdims=True)) + 1e-05)

def attend(pieces):
    queries, keys, values = pieces
    highest = lax.Precision.HIGHEST
    cosine, sine = tables(TOK_DEV, HD)
    q_rot = low(rotate(queries, cosine, sine))
    k_rot = low(rotate(keys, cosine, sine))
    v_low = low(values)
    batch = queries.shape[0]
    grouped = q_rot.reshape(batch, TOK_DEV, KV, HEADS // KV, HD)
    scores = jnp.einsum('bqhgd,bkhd->bhgqk', grouped, k_rot, precision=highest) / math.sqrt(HD)
    scores = low_back(scores)
    rows = jnp.arange(TOK_DEV)
    allowed = rows[:, None] >= rows[None, :]
    scores = jnp.where(allowed, scores, -1e+30)
    probs = jax.nn.softmax(scores, axis=-1)
    mixed = jnp.einsum('bhgqk,bkhd->bqhgd', low(probs), v_low, precision=highest)
    return mixed.reshape(batch, TOK_DEV, D)

def forward(x_in, gain_one, wq, wk, wv, wo, gain_two, wg, wu, wd):
    highest = lax.Precision.HIGHEST
    count = x_in.shape[0] // TOK_DEV
    group = math.gcd(count, max(1, 4096 // TOK_DEV))
    n_one = low(scaled_rms(x_in) * gain_one)
    q_pre = low_back(jnp.dot(n_one, wq, precision=highest))
    k_pre = low_back(jnp.dot(n_one, wk, precision=highest))
    v_pre = low_back(jnp.dot(n_one, wv, precision=highest))
    q_seq = q_pre.reshape(count // group, group, TOK_DEV, HEADS, HD)
    k_seq = k_pre.reshape(count // group, group, TOK_DEV, KV, HD)
    v_seq = v_pre.reshape(count // group, group, TOK_DEV, KV, HD)
    mixed = lax.map(jax.checkpoint(attend), (q_seq, k_seq, v_seq))
    mixed = low(low_back(mixed.reshape(-1, D)))
    hidden = x_in + low_back(jnp.dot(mixed, wo, precision=highest))
    n_two = low(scaled_rms(hidden) * gain_two)
    gate = low_back(jnp.dot(n_two, wg, precision=highest))
    upper = low_back(jnp.dot(n_two, wu, precision=highest))
    act = low(jax.nn.silu(gate) * upper)
    return hidden + low_back(jnp.dot(act, wd, precision=highest))

def reference(tokens, gain_attn, w_query, w_key, w_value, w_out, gain_ffn, w_gate, w_up, w_down, cotangent):
    inputs = [tokens, gain_attn, w_query, w_key, w_value, w_out, gain_ffn, w_gate, w_up, w_down]
    inputs = [item.astype(jnp.float32) for item in inputs]
    result, pullback = jax.vjp(forward, *inputs)
    grads = pullback(cotangent.astype(jnp.float32))
    return (result.astype(jnp.bfloat16), grads[0], grads[1], grads[2], grads[3], grads[4], grads[5], grads[6], grads[7], grads[8], grads[9])
```

```python
import functools
import math

import jax
import jax.numpy as jnp
from jax import lax
from jax.experimental import pallas as pl
from jax.experimental.pallas import tpu as pltpu
from jax.sharding import PartitionSpec as P

D = 1536
HEADS = 16
KV = 8
HD = 96
BF = jnp.bfloat16
F32 = jnp.float32
MiB = 1024 * 1024
ANY = pl.BlockSpec(memory_space=pl.ANY)
WHOLE = pl.BlockSpec(memory_space=pltpu.VMEM)
SCALARS = pl.BlockSpec(memory_space=pltpu.SMEM)
QUADS = 4


def turn(values):
    half = values.shape[-1] // 2
    return jnp.concatenate([-values[..., half:], values[..., :half]], axis=-1)


def tables(length, size):
    freq = 10000.0 ** (-jnp.arange(0, size, 2).astype(F32) / size)
    angle = jnp.arange(length).astype(F32)[:, None] * freq[None, :]
    angle = jnp.concatenate([angle, angle], axis=-1)
    return (jnp.cos(angle)[:, None, :], jnp.sin(angle)[:, None, :])


def norm_back(upstream, normed, factor, gain):
    scaled = upstream * gain
    return factor * (scaled - normed * jnp.mean(scaled * normed, axis=-1, keepdims=True))


def nt(a, b):
    return lax.dot_general(a, b, (((1,), (1,)), ((), ())), preferred_element_type=F32)


def tn(a, b):
    return lax.dot_general(a, b, (((0,), (0,)), ((), ())), preferred_element_type=F32)


def nn(a, b):
    return jnp.dot(a, b, preferred_element_type=F32)


class Links:
    def __init__(self, reps, depth):
        self.reps, self.depth = reps, depth

    def swap(self, value, bit):
        return lax.ppermute(value, "rep", [(i, i ^ bit) for i in range(self.reps)])

    def shift(self, value, by):
        return lax.ppermute(value, "fsdp", [(i, (i + by) % self.depth) for i in range(self.depth)])

    def spread(self, piece, cut):
        got = [self.shift(piece, by) for by in range(1, self.depth)]
        along_x = [self.swap(item, 2) for item in got]
        along_y = [self.swap(item, 4) for item in got]
        corner = [
            (self.swap(item_y[:cut], 2), self.swap(item_x[cut:], 4))
            for item_x, item_y in zip(along_x, along_y)
        ]
        return [[(i,) for i in got], [(i,) for i in along_x], [(i,) for i in along_y], corner]

    def collect(self, blocks, z):
        own, along_x, along_y, corner = blocks
        half = self.depth // 2
        from_x = self.swap(corner[:half], 2)
        from_y = self.swap(corner[half:], 4)
        x_low = self.swap(along_x[:half], 2)
        y_high = self.swap(along_y[half:], 4)
        x_high = self.swap((along_x[half:].astype(F32) + from_y.astype(F32)).astype(BF), 2)
        y_low = self.swap((along_y[:half].astype(F32) + from_x.astype(F32)).astype(BF), 4)
        low = own[:half].astype(F32) + x_low.astype(F32) + y_low.astype(F32)
        high = own[half:].astype(F32) + x_high.astype(F32) + y_high.astype(F32)
        total = jnp.concatenate([low, high], axis=0).astype(BF)
        result = lax.dynamic_index_in_dim(total, z, 0, keepdims=False).astype(F32)
        for by in range(1, self.depth):
            send = lax.dynamic_index_in_dim(total, (z + by) % self.depth, 0, keepdims=False)
            result = result + self.shift(send, by).astype(F32)
        result = result.astype(BF)
        if self.reps > 2 * QUADS:
            cells = [
                [cell * 2 * QUADS + i for cell in range(self.reps // (2 * QUADS))]
                for i in range(2 * QUADS)
            ]
            result = lax.psum(result, "rep", axis_index_groups=cells)
        return result

    def share(self, quarter, cut):
        along_x = self.swap(quarter, 2)
        along_y = self.swap(quarter, 4)
        corner = jnp.concatenate(
            [self.swap(along_y[:cut], 2), self.swap(along_x[cut:], 4)], axis=0
        )
        mine = [quarter, along_x, along_y, corner]
        return mine + [self.swap(item, 1) for item in mine]


def depth_offsets(z, depth, rows):
    return [lax.rem(z + depth - by, depth) * rows for by in range(1, depth)]


def run_copies(copies, sems):
    started = []
    for i, (source, target) in enumerate(copies):
        copy = pltpu.make_async_copy(source, target, sems.at[i])
        copy.start()
        started.append(copy)
    for copy in started:
        copy.wait()


def assemble(pos, own, pieces, rows, depth):
    flat, plan = [], []
    for rel in range(QUADS):
        for by, parts in enumerate(pieces[rel]):
            start = 0
            for part in parts:
                plan.append((rel, by, start, part.shape[0]))
                flat.append(part)
                start += part.shape[0]
    quarter = rows // QUADS
    width = own.shape[1]

    def kernel(pos_ref, own_ref, *refs):
        part_refs, out_ref, sems = refs[:-2], refs[-2], refs[-1]
        z, k = pos_ref[0], pos_ref[1]
        starts = depth_offsets(z, depth, rows)
        copies = [(own_ref, out_ref.at[pl.ds(pl.multiple_of(z * rows, 16), rows), :])]
        for ref, (rel, by, start, size) in zip(part_refs, plan):
            row = starts[by] + (k ^ rel) * quarter + start
            copies.append((ref, out_ref.at[pl.ds(pl.multiple_of(row, 16), size), :]))
        run_copies(copies, sems)

    return pl.pallas_call(
        kernel,
        out_shape=jax.ShapeDtypeStruct((rows * depth, width), BF),
        in_specs=[SCALARS] + [ANY] * (1 + len(flat)),
        out_specs=ANY,
        scratch_shapes=[pltpu.SemaphoreType.DMA((1 + len(flat),))],
        cost_estimate=pl.CostEstimate(
            flops=0, bytes_accessed=4 * rows * depth * width, transcendentals=0
        ),
    )(pos, own, *flat)


def ffn_block(pos, rel, n_two, d_out, shard_gate, shard_up, shard_down, gate, up, down, depth):
    rows = shard_gate.shape[0]
    cols = gate[0][0].shape[1]
    d_rows = down[0][0].shape[0] if len(down[0]) == 1 else sum(i.shape[0] for i in down[0])
    tokens = n_two[0].shape[0] * 2
    width = n_two[0].shape[1]
    seg = cols // depth
    flat, plan = [], []
    for which, pieces in enumerate((gate, up, down)):
        for by, parts in enumerate(pieces):
            start = 0
            for part in parts:
                plan.append((which, by, start, part.shape[0]))
                flat.append(part)
                start += part.shape[0]
    n_copies = 4 + 2 * depth + 1 + len(flat)
    tile = 256

    def kernel(pos_ref, na, nb, ya, yb, sg_ref, su_ref, sd_ref, *refs):
        parts = refs[: len(flat)]
        (act, dgu, g_gate, g_up, g_down, w_gate, w_up, w_down, n_all, y_all, sems) = refs[
            len(flat) :
        ]
        z, k, c = pos_ref[0], pos_ref[1], pos_ref[2]
        j = k ^ rel
        half = tokens // 2
        copies = [
            (na, n_all.at[pl.ds(0, half), :]),
            (nb, n_all.at[pl.ds(half, half), :]),
            (ya, y_all.at[pl.ds(0, half), :]),
            (yb, y_all.at[pl.ds(half, half), :]),
        ]
        for source, target in ((sg_ref, w_gate), (su_ref, w_up)):
            for s in range(depth):
                col = pl.multiple_of((s * 2 + c) * (QUADS * seg) + j * seg, 128)
                copies.append(
                    (
                        source.at[:, pl.ds(col, seg)],
                        target.at[pl.ds(pl.multiple_of(z * rows, 16), rows), pl.ds(s * seg, seg)],
                    )
                )
        row = pl.multiple_of((c * QUADS + j) * d_rows, 16)
        copies.append(
            (
                sd_ref.at[pl.ds(row, d_rows), :],
                w_down.at[pl.ds(pl.multiple_of(z * d_rows, 16), d_rows), :],
            )
        )
        targets = (w_gate, w_up, w_down)
        for ref, (which, by, start, size) in zip(parts, plan):
            base = depth_offsets(z, depth, rows if which < 2 else d_rows)[by] + start
            copies.append((ref, targets[which].at[pl.ds(pl.multiple_of(base, 16), size), :]))
        run_copies(copies, sems)

        def forward(i, _):
            at = pl.ds(pl.multiple_of(i * tile, tile), tile)
            normed, grad = n_all[at, :], y_all[at, :]
            gated = nn(normed, w_gate[...])
            upper = nn(normed, w_up[...])
            d_act = nt(grad, w_down[...])
            sig = 1.0 / (1.0 + jnp.exp(-gated))
            silu = gated * sig
            act[at, :] = (silu * upper).astype(BF)
            dgu[at, :cols] = (d_act * upper * sig * (1.0 + gated * (1.0 - sig))).astype(BF)
            dgu[at, cols:] = (d_act * silu).astype(BF)
            return 0

        lax.fori_loop(0, tokens // tile, forward, 0)

        def back_in(i, _):
            at = pl.ds(pl.multiple_of(i * tile, tile), tile)
            grads = tn(n_all[:, at], dgu[...])
            g_gate[at, :] = grads[:, :cols].astype(BF)
            g_up[at, :] = grads[:, cols:].astype(BF)
            return 0

        lax.fori_loop(0, width // tile, back_in, 0)

        def back_out(i, _):
            at = pl.ds(pl.multiple_of(i * tile, tile), tile)
            g_down[at, :] = tn(act[:, at], y_all[...]).astype(BF)
            return 0

        lax.fori_loop(0, cols // tile, back_out, 0)

    shapes = [
        (tokens, cols),
        (tokens, 2 * cols),
        (width, cols),
        (width, cols),
        (cols, width),
        (width, cols),
        (width, cols),
        (cols, width),
    ]
    return pl.pallas_call(
        kernel,
        out_shape=[jax.ShapeDtypeStruct(shape, BF) for shape in shapes],
        in_specs=[SCALARS] + [ANY] * (7 + len(flat)),
        out_specs=[WHOLE] * len(shapes),
        scratch_shapes=[
            pltpu.VMEM((tokens, width), BF),
            pltpu.VMEM((tokens, width), BF),
            pltpu.SemaphoreType.DMA((n_copies,)),
        ],
        compiler_params=pltpu.CompilerParams(vmem_limit_bytes=48 * MiB),
        cost_estimate=pl.CostEstimate(
            flops=12 * tokens * width * cols,
            bytes_accessed=2 * sum(a * b for a, b in shapes),
            transcendentals=tokens * cols,
        ),
    )(pos, *n_two, *d_out, shard_gate, shard_up, shard_down, *flat)


def rows_product(lefts, rights, half, transposed, dtype):
    rows = lefts[0].shape[0] // 2
    tile = 256
    per = len(rights) // len(lefts)
    width = rights[0].shape[0] if transposed else rights[0].shape[1]
    depth = rights[0].shape[1] if transposed else rights[0].shape[0]
    steps = rows // tile

    def kernel(*refs):
        left, right, out = refs[: len(lefts)], refs[len(lefts) : -1], refs[-1]
        total = None
        for i, ref in enumerate(right):
            part = left[i // per][:, (i % per) * depth : (i % per + 1) * depth]
            term = (nt if transposed else nn)(part, ref[...])
            total = term if total is None else total + term
        out[...] = total.astype(dtype)

    return pl.pallas_call(
        kernel,
        grid=(steps,),
        out_shape=jax.ShapeDtypeStruct((rows, width), dtype),
        in_specs=[
            pl.BlockSpec((tile, left.shape[1]), lambda i: (i + half * steps, 0)) for left in lefts
        ]
        + [pl.BlockSpec(right.shape, lambda i: (0, 0)) for right in rights],
        out_specs=pl.BlockSpec((tile, width), lambda i: (i, 0)),
        compiler_params=pltpu.CompilerParams(vmem_limit_bytes=56 * MiB),
        cost_estimate=pl.CostEstimate(
            flops=2 * rows * width * depth * len(rights),
            bytes_accessed=2 * len(rights) * width * depth,
            transcendentals=0,
        ),
    )(*lefts, *rights)


def unpack_columns(pos, parts, depth):
    rows, cols = parts[0].shape
    seg = cols // depth
    width = cols * 2 * QUADS

    def kernel(pos_ref, *refs):
        out = refs[-1]
        k, c = pos_ref[1], pos_ref[2]
        for i, ref in enumerate(refs[:-1]):
            block = (c if i < QUADS else 1 - c) * QUADS + (k ^ (i % QUADS))
            for s in range(depth):
                at = pl.multiple_of((s * 2 * QUADS + block) * seg, 128)
                out[:, pl.ds(at, seg)] = ref[:, s * seg : (s + 1) * seg].astype(F32)

    tile = 128
    return pl.pallas_call(
        kernel,
        grid=(rows // tile,),
        out_shape=jax.ShapeDtypeStruct((rows, width), F32),
        in_specs=[SCALARS] + [pl.BlockSpec((tile, cols), lambda i: (i, 0))] * len(parts),
        out_specs=pl.BlockSpec((tile, width), lambda i: (i, 0)),
        compiler_params=pltpu.CompilerParams(vmem_limit_bytes=32 * MiB),
        cost_estimate=pl.CostEstimate(
            flops=rows * width, bytes_accessed=6 * rows * width, transcendentals=0
        ),
    )(pos, *parts)


def unpack_rows(pos, parts):
    rows, width = parts[0].shape

    def kernel(pos_ref, *refs):
        out = refs[-1]
        k, c = pos_ref[1], pos_ref[2]
        for i, ref in enumerate(refs[:-1]):
            block = (c if i < QUADS else 1 - c) * QUADS + (k ^ (i % QUADS))
            out[pl.ds(pl.multiple_of(block * rows, 8), rows), :] = ref[...].astype(F32)

    tile = 512
    return pl.pallas_call(
        kernel,
        grid=(width // tile,),
        out_shape=jax.ShapeDtypeStruct((rows * 2 * QUADS, width), F32),
        in_specs=[SCALARS] + [pl.BlockSpec((rows, tile), lambda i: (0, i))] * len(parts),
        out_specs=pl.BlockSpec((rows * 2 * QUADS, tile), lambda i: (0, i)),
        compiler_params=pltpu.CompilerParams(vmem_limit_bytes=32 * MiB),
        cost_estimate=pl.CostEstimate(
            flops=rows * width, bytes_accessed=48 * rows * width, transcendentals=0
        ),
    )(pos, *parts)


def on_device(
    reps,
    depth,
    tokens,
    gain_attn,
    w_query,
    w_key,
    w_value,
    w_out,
    gain_ffn,
    w_gate,
    w_up,
    w_down,
    cotangent,
):
    links = Links(reps, depth)
    z = lax.axis_index("fsdp")
    r = lax.axis_index("rep")
    c = r % 2
    k = (r // 2) % QUADS
    pos = jnp.stack([z, k, c]).astype(jnp.int32)
    length = tokens.shape[0]
    ratio = HEADS // KV
    kv = KV // 2
    scale = 1.0 / math.sqrt(HD)
    rows = w_query.shape[0]
    quarter = rows // QUADS
    inner = D // 2
    narrow = inner // ratio

    def core_columns(weight):
        split = weight.reshape(rows, depth, 2, weight.shape[1] // (2 * depth))
        return lax.dynamic_index_in_dim(split, c, 2, keepdims=False).reshape(rows, -1)

    shard_qkv = jnp.concatenate([core_columns(i) for i in (w_query, w_key, w_value)], axis=1)
    shard_out = lax.dynamic_slice_in_dim(w_out, c * (rows // 2), rows // 2, 0)
    piece_qkv = lax.dynamic_slice_in_dim(shard_qkv, k * quarter, quarter, 0)
    piece_out = lax.dynamic_slice_in_dim(shard_out, k * (quarter // 2), quarter // 2, 0)
    seg = w_gate.shape[1] // (depth * 2 * QUADS)
    d_rows = w_down.shape[0] // (2 * QUADS)

    def block_columns(weight):
        return jnp.concatenate(
            [
                lax.dynamic_slice_in_dim(weight, ((s * 2 + c) * QUADS + k) * seg, seg, 1)
                for s in range(depth)
            ],
            axis=1,
        )

    piece_gate, piece_up = block_columns(w_gate), block_columns(w_up)
    piece_down = lax.dynamic_slice_in_dim(w_down, (c * QUADS + k) * d_rows, d_rows, 0)

    gains = jnp.stack([gain_attn, gain_ffn])
    gains = jnp.stack([gains] + [links.shift(gains, by) for by in range(1, depth)])
    gains = jnp.take(gains, (z - jnp.arange(depth)) % depth, axis=0)
    g_one = gains[:, 0].reshape(-1).astype(F32)
    g_two = gains[:, 1].reshape(-1).astype(F32)
    other_tokens = links.swap(tokens, 1)
    other_cotangent = links.swap(cotangent, 1)

    got_qkv = links.spread(piece_qkv, quarter // 2)
    got_out = links.spread(piece_out, quarter // 3)
    got_gate = links.spread(piece_gate, rows // 2)
    got_up = links.spread(piece_up, rows // 2)
    got_down = links.spread(piece_down, d_rows // 2)

    cosine, sine = tables(length, HD)
    order = jnp.arange(length)
    allowed = order[:, None] >= order[None, :]

    def normed_of(values):
        factor = lax.rsqrt(jnp.mean(values * values, axis=-1, keepdims=True) + 1e-05)
        return values * factor, factor

    x_in = tokens.astype(F32)
    normed_one, factor_one = normed_of(x_in)
    normed_other, _ = normed_of(other_tokens.astype(F32))
    n_one = jnp.concatenate(
        [(normed_one * g_one).astype(BF), (normed_other * g_one).astype(BF)], axis=0
    )
    wqkv = assemble(pos, shard_qkv, got_qkv, rows, depth)
    qkv = nn(n_one, wqkv)
    q_pre = qkv[:, :inner].reshape(2, length, 2 * kv, HD)
    k_pre = qkv[:, inner : inner + narrow].reshape(2, length, kv, HD)
    v_low = qkv[:, inner + narrow :].astype(BF).reshape(2, length, kv, HD)
    q_rot = (q_pre * cosine + turn(q_pre) * sine).astype(BF).reshape(2, length, kv, ratio, HD)
    k_rot = (k_pre * cosine + turn(k_pre) * sine).astype(BF)

    def scores_of(queries, keys):
        raw = jnp.einsum("bqhgd,bkhd->bhgqk", queries, keys, preferred_element_type=F32) * scale
        return jnp.where(allowed, raw, -1e30)

    scores = scores_of(q_rot, k_rot)
    peak = jnp.max(scores, axis=-1, keepdims=True)
    log_total = peak + jnp.log(jnp.sum(jnp.exp(scores - peak), axis=-1, keepdims=True))
    probs = jnp.exp(scores - log_total)
    mixed = jnp.einsum(
        "bhgqk,bkhd->bqhgd", probs.astype(BF), v_low, preferred_element_type=F32
    )
    mixed = mixed.reshape(2 * length, inner).astype(BF)
    wo = assemble(pos, shard_out, got_out, rows // 2, depth)
    out_part = nn(mixed, wo)
    hidden = (
        x_in + out_part[:length] + links.swap(out_part[length:].astype(BF), 1).astype(F32)
    )

    normed_two, factor_two = normed_of(hidden)
    n_two = (normed_two * g_two).astype(BF)
    n_two = (n_two, links.swap(n_two, 1))
    d_pair = (cotangent, other_cotangent)
    blocks = [None] * QUADS
    for rel in (3, 1, 2, 0):
        blocks[rel] = ffn_block(
            pos,
            rel,
            n_two,
            d_pair,
            w_gate,
            w_up,
            w_down,
            got_gate[rel],
            got_up[rel],
            got_down[rel],
            depth,
        )
    sums_gate = links.collect([b[2].reshape(depth, rows, -1) for b in blocks], z)
    sums_up = links.collect([b[3].reshape(depth, rows, -1) for b in blocks], z)
    sums_down = links.collect([b[4].reshape(depth, d_rows, -1) for b in blocks], z)

    lefts = [b[1] for b in blocks]
    rights = [w for b in blocks for w in (b[5], b[6])]
    to_other = rows_product(lefts, rights, 1, True, BF)
    mine = rows_product(lefts, rights, 0, True, F32)
    d_norm_two = mine + links.swap(to_other, 1).astype(F32)
    acts, downs = [b[0] for b in blocks], [b[7] for b in blocks]
    out_other = rows_product(acts, downs, 1, False, BF)
    out_mine = rows_product(acts, downs, 0, False, F32)
    result = (hidden + out_mine + links.swap(out_other, 1).astype(F32)).astype(BF)

    grad_g_two = jnp.sum(d_norm_two * normed_two, axis=0)
    d_hidden = cotangent.astype(F32) + norm_back(d_norm_two, normed_two, factor_two, g_two)

    low = d_hidden.astype(BF)
    d_low = jnp.concatenate([low, links.swap(low, 1)], axis=0)
    grad_o = tn(mixed, d_low).astype(BF)
    d_mixed = nt(d_low, wo).astype(BF).reshape(2, length, kv, ratio, HD)
    again = jnp.exp(scores_of(q_rot, k_rot) - log_total)
    d_value = jnp.einsum(
        "bhgqk,bqhgd->bkhd", again.astype(BF), d_mixed, preferred_element_type=F32
    )
    d_probs = jnp.einsum("bqhgd,bkhd->bhgqk", d_mixed, v_low, preferred_element_type=F32)
    centre = jnp.sum(again * d_probs, axis=-1, keepdims=True)
    d_scores = (again * (d_probs - centre)).astype(BF)
    d_query = (
        jnp.einsum("bhgqk,bkhd->bqhgd", d_scores, k_rot, preferred_element_type=F32) * scale
    ).reshape(2, length, 2 * kv, HD)
    d_key = (
        jnp.einsum("bhgqk,bqhgd->bkhd", d_scores, q_rot, preferred_element_type=F32) * scale
    )
    d_query = (d_query * cosine - turn(d_query * sine)).reshape(2 * length, inner).astype(BF)
    d_key = (d_key * cosine - turn(d_key * sine)).reshape(2 * length, narrow).astype(BF)
    d_value = d_value.reshape(2 * length, narrow).astype(BF)
    d_qkv = jnp.concatenate([d_query, d_key, d_value], axis=1)
    grad_qkv = tn(n_one, d_qkv).astype(BF)
    d_one_other = nt(d_qkv[length:], wqkv).astype(BF)
    d_norm_one = nt(d_qkv[:length], wqkv) + links.swap(d_one_other, 1).astype(F32)
    grad_g_one = jnp.sum(d_norm_one * normed_one, axis=0)
    input_grad = d_hidden + norm_back(d_norm_one, normed_one, factor_one, g_one)

    def quarters(grads, size):
        split = grads.reshape(depth, QUADS, size, -1)
        return [lax.dynamic_index_in_dim(split, k ^ rel, 1, keepdims=False) for rel in range(QUADS)]

    sums_qkv = links.collect(quarters(grad_qkv, quarter), z)
    sums_out = links.collect(quarters(grad_o, quarter // 2), z)

    share_gate = unpack_columns(pos, links.share(sums_gate, rows // 2), depth)
    share_up = unpack_columns(pos, links.share(sums_up, rows // 2), depth)
    share_down = unpack_rows(pos, links.share(sums_down, d_rows // 2))
    share_out = unpack_rows(pos, links.share(sums_out, quarter // 3))
    qkv_rows = unpack_rows(pos, links.share(sums_qkv, quarter // 2)).reshape(2, rows, -1)

    def both_cores(start, width):
        part = qkv_rows[:, :, start : start + width].reshape(2, rows, depth, width // depth)
        return part.transpose(1, 2, 0, 3).reshape(rows, 2 * width)

    share_q = both_cores(0, inner)
    share_k = both_cores(inner, narrow)
    share_v = both_cores(inner + narrow, narrow)

    sums = lax.psum(jnp.stack([grad_g_one, grad_g_two]), ("rep", "fsdp"))
    sums = lax.dynamic_slice_in_dim(sums, z * rows, rows, 1)
    return (
        result,
        input_grad,
        sums[0],
        share_q,
        share_k,
        share_v,
        share_out,
        sums[1],
        share_gate,
        share_up,
        share_down,
    )


def solution(mesh):
    tokens = P(("rep", "fsdp"), None)
    gain, weight = P("fsdp"), P("fsdp", None)
    return jax.shard_map(
        functools.partial(on_device, mesh.shape["rep"], mesh.shape["fsdp"]),
        mesh=mesh,
        in_specs=(tokens, gain, *[weight] * 4, gain, *[weight] * 3, tokens),
        out_specs=(tokens, tokens, gain, *[weight] * 4, gain, *[weight] * 3),
        check_vma=False,
    )
```

```python
import functools
import math

import jax
import jax.numpy as jnp
from jax import lax
from jax.experimental import pallas as pl
from jax.experimental.pallas import tpu as pltpu
from jax.sharding import PartitionSpec as P

D = 1536
HEADS = 16
KV = 8
HD = 96
BF = jnp.bfloat16
F32 = jnp.float32
MiB = 1024 * 1024
ANY = pl.BlockSpec(memory_space=pl.ANY)
WHOLE = pl.BlockSpec(memory_space=pltpu.VMEM)
SCALARS = pl.BlockSpec(memory_space=pltpu.SMEM)
QUADS = 4
TILE = 256
SCALE = 1.0 / math.sqrt(HD)


def nt(a, b):
    return lax.dot_general(a, b, (((1,), (1,)), ((), ())), preferred_element_type=F32)


def tn(a, b):
    return lax.dot_general(a, b, (((0,), (0,)), ((), ())), preferred_element_type=F32)


def nn(a, b):
    return jnp.dot(a, b, preferred_element_type=F32)


def rms(values):
    return lax.rsqrt(jnp.mean(values * values, axis=-1, keepdims=True) + 1e-05)


def tile_at(i, size):
    return pl.ds(pl.multiple_of(i * size, size), size)


def call(kernel, out_shape, *args, scratch=(), vmem=48, grid=(), in_specs=None, out_specs=None):
    return pl.pallas_call(
        kernel,
        grid=grid,
        out_shape=out_shape,
        in_specs=in_specs,
        out_specs=out_specs,
        scratch_shapes=list(scratch),
        compiler_params=pltpu.CompilerParams(vmem_limit_bytes=vmem * MiB),
        cost_estimate=pl.CostEstimate(flops=0, bytes_accessed=1024, transcendentals=0),
    )(*args)


def shaped(shape, dtype=BF):
    return jax.ShapeDtypeStruct(shape, dtype)


class Links:
    def __init__(self, reps, depth):
        self.reps, self.depth = reps, depth

    def swap(self, value, bit):
        return lax.ppermute(value, "rep", [(i, i ^ bit) for i in range(self.reps)])

    def shift(self, value, by):
        return lax.ppermute(value, "fsdp", [(i, (i + by) % self.depth) for i in range(self.depth)])

    def cells(self, value):
        if self.reps == 2 * QUADS:
            return value
        groups = [
            [cell * 2 * QUADS + i for cell in range(self.reps // (2 * QUADS))]
            for i in range(2 * QUADS)
        ]
        return lax.psum(value, "rep", axis_index_groups=groups)

    def spread(self, pos, piece, cut):
        return Gathered(self, pos, piece, cut)

    def collect(self, blocks):
        own, along_x, along_y, corner = blocks
        from_x = self.swap(corner[0], 2)
        from_y = self.swap(corner[1], 4)
        x_low = self.swap(along_x[0], 2)
        y_high = self.swap(along_y[1], 4)
        y_low = self.swap((along_y[0].astype(F32) + from_x.astype(F32)).astype(BF), 4)
        x_high = self.swap((along_x[1].astype(F32) + from_y.astype(F32)).astype(BF), 2)
        low = own[0].astype(F32) + x_low.astype(F32) + y_low.astype(F32)
        high = own[1].astype(F32) + x_high.astype(F32) + y_high.astype(F32)
        return tuple(
            self.cells(
                lax.psum_scatter(i.astype(BF), "fsdp", scatter_dimension=0, tiled=True)[0]
            )
            for i in (low, high)
        )

    def share(self, low, high):
        x_low, x_high = self.swap(low, 2), self.swap(high, 2)
        y_low, y_high = self.swap(low, 4), self.swap(high, 4)
        mine_low = jnp.stack([low, x_low, y_low, self.swap(y_low, 2)])
        mine_high = jnp.stack([high, x_high, y_high, self.swap(x_high, 4)])
        return mine_low, self.swap(mine_low, 1), mine_high, self.swap(mine_high, 1)


class Gathered:
    def __init__(self, links, pos, piece, cut):
        self.rows, self.cut, self.depth = piece.shape[0], cut, links.depth
        n, m, depth = piece.shape[0], piece.shape[1], links.depth
        self.own = lax.all_gather(piece, "fsdp", axis=0, tiled=True)

        def kernel(pos_ref, in_ref, out_ref):
            out_ref[...] = in_ref[...]

        remote = pl.pallas_call(
            kernel,
            grid_spec=pltpu.PrefetchScalarGridSpec(
                num_scalar_prefetch=1,
                grid=(depth - 1,),
                in_specs=[pl.BlockSpec((n, m), lambda i, at: (lax.rem(at[0] + 1 + i, depth), 0))],
                out_specs=pl.BlockSpec((n, m), lambda i, at: (i, 0)),
            ),
            out_shape=shaped(((depth - 1) * n, m)),
            cost_estimate=pl.CostEstimate(flops=0, bytes_accessed=1024, transcendentals=0),
        )(pos, self.own)
        self.x = links.swap(remote, 2)
        self.y = links.swap(remote, 4)
        self.corner = links.swap(self.y[:cut], 2), links.swap(self.x[cut:], 4)

    def arrays(self, rel):
        return [(self.own,), (self.x,), (self.y,), self.corner][rel]

    def segments(self, rel):
        n = self.rows
        if rel == 0:
            return [(0, i, None, n, 0) for i in range(self.depth - 1)]
        if rel < 3:
            return [(0, i, i * n, n, 0) for i in range(self.depth - 1)]
        found = []
        for i in range(self.depth - 1):
            first, last = i * n, (i + 1) * n
            if first < self.cut:
                found.append((0, i, first, min(last, self.cut) - first, 0))
            if last > self.cut:
                begin = max(first, self.cut)
                found.append((1, i, begin - self.cut, last - begin, begin - first))
        return found

    def copies(self, rel, refs, z, target, stride, base):
        out = []
        for which, i, row, count, offset in self.segments(rel):
            shard = lax.rem(z + 1 + i, self.depth)
            source = pl.multiple_of(shard * self.rows, 16) if row is None else row
            at = pl.multiple_of(shard * stride + base + offset, 16)
            out.append((refs[which].at[pl.ds(source, count), :], target.at[pl.ds(at, count), :]))
        return out


def start(copies, sems, first=0):
    made = [
        pltpu.make_async_copy(source, target, sems.at[first + i])
        for i, (source, target) in enumerate(copies)
    ]
    for copy in made:
        copy.start()
    return made


def all_parts(got):
    return [array for rel in range(QUADS) for array in got.arrays(rel)]


def whole_copies(got, refs, z, k, target, stride):
    out, at = [], 0
    for rel in range(QUADS):
        size = len(got.arrays(rel))
        out += got.copies(rel, refs[at : at + size], z, target, stride, (k ^ rel) * got.rows)
        at += size
    return out


def n_copies(got, rels=range(QUADS)):
    return sum(len(got.segments(rel)) for rel in rels)


def tables(length):
    freq = 10000.0 ** (-jnp.arange(0, HD, 2).astype(F32) / HD)
    angle = jnp.arange(length).astype(F32)[:, None] * freq[None, :]
    cosine, sine = jnp.cos(angle), jnp.sin(angle)
    none = jnp.zeros_like(sine)

    def four(a, b):
        return jnp.concatenate([a, b] * 4, axis=1)

    return four(cosine, cosine), four(-sine, none), four(none, sine)


def rotated(u, cosine, right, left, sign):
    width = u.shape[1]
    turned = pltpu.roll(u, width - HD // 2, 1) * right + pltpu.roll(u, HD // 2, 1) * left
    return u * cosine + sign * turned


def project(pos, pair, gain, got, shard, turns):
    length, width = pair[0].shape
    cols = shard.shape[1]
    rows = shard.shape[0]
    parts = all_parts(got)
    narrow = cols // 4
    copies_in = 3 + n_copies(got)

    def kernel(pos_ref, gain_ref, cos_ref, right_ref, left_ref, ta, tb, shard_ref, *refs):
        part_refs = refs[: len(parts)]
        normed, q, key, value, weight, toks, sems = refs[len(parts) :]
        z, k = pos_ref[0], pos_ref[1]
        first = start(
            [(ta, toks.at[pl.ds(0, length), :]), (tb, toks.at[pl.ds(length, length), :])], sems
        )
        second = start(
            [(shard_ref, weight.at[pl.ds(pl.multiple_of(z * rows, 16), rows), :])]
            + whole_copies(got, part_refs, z, k, weight, rows),
            sems,
            2,
        )
        for copy in first:
            copy.wait()

        def norm(i, _):
            at = tile_at(i, TILE)
            x = toks[at, :].astype(F32)
            normed[at, :] = (x * rms(x) * gain_ref[...]).astype(BF)
            return 0

        lax.fori_loop(0, 2 * length // TILE, norm, 0)
        for copy in second:
            copy.wait()

        def body(i, _):
            at = tile_at(i, TILE)
            place = tile_at(lax.rem(i, length // TILE), TILE)
            out = nn(normed[at, :], weight[...])
            cosine, right, left = cos_ref[place, :], right_ref[place, :], left_ref[place, :]
            for t in range(2):
                u = out[:, t * narrow : (t + 1) * narrow]
                q[at, t * narrow : (t + 1) * narrow] = rotated(
                    u, cosine, right, left, 1.0
                ).astype(BF)
            key[at, :] = rotated(
                out[:, 2 * narrow : 3 * narrow], cosine, right, left, 1.0
            ).astype(BF)
            value[at, :] = out[:, 3 * narrow :].astype(BF)
            return 0

        lax.fori_loop(0, 2 * length // TILE, body, 0)

    return call(
        kernel,
        [
            shaped((2 * length, width)),
            shaped((2 * length, 2 * narrow)),
            shaped((2 * length, narrow)),
            shaped((2 * length, narrow)),
            shaped((width, cols)),
        ],
        pos,
        gain,
        *turns,
        *pair,
        shard,
        *parts,
        in_specs=[SCALARS] + [WHOLE] * 4 + [ANY] * (3 + len(parts)),
        out_specs=[WHOLE] * 5,
        scratch=[pltpu.VMEM((2 * length, width), BF), pltpu.SemaphoreType.DMA((copies_in,))],
    )


def masked(scores, first):
    keys = lax.broadcasted_iota(jnp.int32, scores.shape, 0)
    queries = lax.broadcasted_iota(jnp.int32, scores.shape, 1) + first
    return jnp.where(keys <= queries, scores, -1e30)


def attend(q, key, value):
    length = q.shape[0] // 2
    heads, groups = q.shape[1] // HD, key.shape[1] // HD

    def kernel(q_ref, k_ref, v_ref, o_ref, lse_ref):
        for g in range(groups):
            keys = k_ref[:, g * HD : (g + 1) * HD]
            turned = v_ref[:, g * HD : (g + 1) * HD].T
            for j in range(g * heads // groups, (g + 1) * heads // groups):
                for t in range(length // TILE):
                    at = slice(t * TILE, (t + 1) * TILE)
                    reach = (t + 1) * TILE
                    s = nt(keys[:reach], q_ref[at, j * HD : (j + 1) * HD]) * SCALE
                    s = masked(s, t * TILE)
                    peak = jnp.max(s, axis=0, keepdims=True)
                    e = jnp.exp(s - peak)
                    total = jnp.sum(e, axis=0, keepdims=True)
                    lse = peak + jnp.log(total)
                    p = (e * (1.0 / total)).astype(BF)
                    lse_ref[0, j : j + 1, at] = lse
                    o_ref[at, j * HD : (j + 1) * HD] = nn(turned[:, :reach], p).T.astype(BF)

    return call(
        kernel,
        [shaped(q.shape), shaped((2, heads, length), F32)],
        q,
        key,
        value,
        grid=(2,),
        in_specs=[
            pl.BlockSpec((length, q.shape[1]), lambda i: (i, 0)),
            pl.BlockSpec((length, key.shape[1]), lambda i: (i, 0)),
            pl.BlockSpec((length, key.shape[1]), lambda i: (i, 0)),
        ],
        out_specs=[
            pl.BlockSpec((length, q.shape[1]), lambda i: (i, 0)),
            pl.BlockSpec((1, heads, length), lambda i: (i, 0, 0)),
        ],
    )


def attend_back(q, key, value, lse, d_mixed, turns):
    length = q.shape[0] // 2
    heads, groups = q.shape[1] // HD, key.shape[1] // HD
    inner, narrow = q.shape[1], key.shape[1]

    def kernel(q_ref, k_ref, v_ref, lse_ref, do_ref, cos_ref, right_ref, left_ref, out, dq, dk):
        for g in range(groups):
            keys = k_ref[:, g * HD : (g + 1) * HD]
            values = v_ref[:, g * HD : (g + 1) * HD]
            turned = keys.T
            d_key = [jnp.zeros((TILE, HD), F32) for _ in range(length // TILE)]
            d_value = [jnp.zeros((TILE, HD), F32) for _ in range(length // TILE)]
            for j in range(g * heads // groups, (g + 1) * heads // groups):
                for t in range(length // TILE):
                    at = slice(t * TILE, (t + 1) * TILE)
                    reach = (t + 1) * TILE
                    queries = q_ref[at, j * HD : (j + 1) * HD]
                    upstream = do_ref[at, j * HD : (j + 1) * HD]
                    s = masked(nt(keys[:reach], queries) * SCALE, t * TILE)
                    p = jnp.exp(s - lse_ref[0, j : j + 1, at])
                    dp = nt(values[:reach], upstream)
                    centre = jnp.sum(p * dp, axis=0, keepdims=True)
                    ds = (p * (dp - centre)).astype(BF)
                    from_values = nn(p.astype(BF), upstream)
                    from_keys = nn(ds, queries)
                    for i in range(t + 1):
                        rows = slice(i * TILE, (i + 1) * TILE)
                        d_value[i] = d_value[i] + from_values[rows]
                        d_key[i] = d_key[i] + from_keys[rows]
                    dq[at, j * HD : (j + 1) * HD] = nn(turned[:, :reach], ds).T * SCALE
            for i in range(length // TILE):
                rows = slice(i * TILE, (i + 1) * TILE)
                dk[rows, g * HD : (g + 1) * HD] = d_key[i] * SCALE
                first = inner + narrow + g * HD
                out[rows, first : first + HD] = d_value[i].astype(BF)
        cosine, right, left = cos_ref[...], right_ref[...], left_ref[...]
        for t in range(inner // narrow):
            cols = slice(t * narrow, (t + 1) * narrow)
            out[:, cols] = rotated(dq[:, cols], cosine, right, left, -1.0).astype(BF)
        out[:, inner : inner + narrow] = rotated(dk[...], cosine, right, left, -1.0).astype(BF)

    def block(cols):
        return pl.BlockSpec((length, cols), lambda i: (i, 0))

    table = pl.BlockSpec(turns[0].shape, lambda i: (0, 0))
    return call(
        kernel,
        shaped((2 * length, inner + 2 * narrow)),
        q,
        key,
        value,
        lse,
        d_mixed,
        *turns,
        grid=(2,),
        in_specs=[
            block(inner),
            block(narrow),
            block(narrow),
            pl.BlockSpec((1, heads, length), lambda i: (i, 0, 0)),
            block(inner),
            table,
            table,
            table,
        ],
        out_specs=block(inner + 2 * narrow),
        scratch=[pltpu.VMEM((length, inner), F32), pltpu.VMEM((length, narrow), F32)],
    )


def mix(pos, mixed, got, shard):
    tokens, inner = mixed.shape
    width = shard.shape[1]
    rows = shard.shape[0]
    parts = all_parts(got)

    def kernel(pos_ref, mixed_ref, shard_ref, *refs):
        part_refs = refs[: len(parts)]
        other, mine, weight, sems = refs[len(parts) :]
        z, k = pos_ref[0], pos_ref[1]
        copies = start(
            [(shard_ref, weight.at[pl.ds(pl.multiple_of(z * rows, 16), rows), :])]
            + whole_copies(got, part_refs, z, k, weight, rows),
            sems,
        )
        for copy in copies:
            copy.wait()
        for i in range(tokens // 2 // TILE):
            at = slice(i * TILE, (i + 1) * TILE)
            low = slice(tokens // 2 + i * TILE, tokens // 2 + (i + 1) * TILE)
            other[at, :] = nn(mixed_ref[low, :], weight[...]).astype(BF)
            mine[at, :] = nn(mixed_ref[at, :], weight[...])

    return call(
        kernel,
        [
            shaped((tokens // 2, width)),
            shaped((tokens // 2, width), F32),
            shaped((inner, width)),
        ],
        pos,
        mixed,
        shard,
        *parts,
        in_specs=[SCALARS, WHOLE] + [ANY] * (1 + len(parts)),
        out_specs=[WHOLE] * 3,
        scratch=[pltpu.SemaphoreType.DMA((1 + n_copies(got),))],
    )


def residual_norm(tokens, mine, received, gain):
    length, width = tokens.shape

    def kernel(x, a, b, gain_ref, hidden, normed):
        h = x[...].astype(F32) + a[...] + b[...].astype(F32)
        hidden[...] = h
        normed[...] = (h * rms(h) * gain_ref[...]).astype(BF)

    block = pl.BlockSpec((TILE, width), lambda i: (i, 0))
    return call(
        kernel,
        [shaped((length, width), F32), shaped((length, width))],
        tokens,
        mine,
        received,
        gain,
        grid=(length // TILE,),
        in_specs=[block, block, block, pl.BlockSpec((1, width), lambda i: (0, 0))],
        out_specs=[block, block],
    )


def norm_back(mine, received, values, residual, gain, rounded):
    length, width = values.shape

    def kernel(a, b, values_ref, residual_ref, gain_ref, grad, gain_grad, *low):
        x = values_ref[...].astype(F32)
        factor = rms(x)
        normed = x * factor
        upstream = a[...] + b[...].astype(F32)
        part = jnp.sum(upstream * normed, axis=0, keepdims=True)

        @pl.when(pl.program_id(0) == 0)
        def _():
            gain_grad[...] = part

        @pl.when(pl.program_id(0) > 0)
        def _():
            gain_grad[...] += part

        scaled = upstream * gain_ref[...]
        inside = scaled - normed * jnp.mean(scaled * normed, axis=-1, keepdims=True)
        total = residual_ref[...].astype(F32) + factor * inside
        grad[...] = total
        if low:
            low[0][...] = total.astype(BF)

    block = pl.BlockSpec((TILE, width), lambda i: (i, 0))
    line = pl.BlockSpec((1, width), lambda i: (0, 0))
    return call(
        kernel,
        [shaped((length, width), F32), shaped((1, width), F32)]
        + [shaped((length, width))] * rounded,
        mine,
        received,
        values,
        residual,
        gain,
        grid=(length // TILE,),
        in_specs=[block] * 4 + [line],
        out_specs=[block, line] + [block] * rounded,
    )


def ffn_block(pos, rel, n_two, d_out, shards, gots):
    depth = gots[0].depth
    rows, d_rows = shards[0].shape[0], gots[2].rows
    cols = gots[0].own.shape[1]
    length, width = n_two[0].shape
    tokens = 2 * length
    seg = cols // depth
    parts = [array for got in gots for array in got.arrays(rel)]
    counts = [len(got.arrays(rel)) for got in gots]
    total = 4 + 3 + 2 * depth + sum(n_copies(got, [rel]) for got in gots)
    half = d_rows // 2

    def kernel(pos_ref, na, nb, ya, yb, sg_ref, su_ref, sd_ref, *refs):
        part_refs, refs = refs[: len(parts)], refs[len(parts) :]
        act, dgu, g_gate, g_up, g_low, g_high, w_gate, w_up, w_down, n_all, y_all, sems = refs
        targets = (w_gate, w_up, w_down)
        z, k, c = pos_ref[0], pos_ref[1], pos_ref[2]
        copies = [
            (na, n_all.at[pl.ds(0, length), :]),
            (nb, n_all.at[pl.ds(length, length), :]),
            (ya, y_all.at[pl.ds(0, length), :]),
            (yb, y_all.at[pl.ds(length, length), :]),
        ]
        if rel == 0:
            copies += list(zip(part_refs, targets))
        else:
            j = k ^ rel
            for source, target in ((sg_ref, w_gate), (su_ref, w_up)):
                for s in range(depth):
                    col = pl.multiple_of(((s * 2 + c) * QUADS + j) * seg, 128)
                    at = pl.ds(pl.multiple_of(z * rows, 16), rows)
                    copies.append(
                        (source.at[:, pl.ds(col, seg)], target.at[at, pl.ds(s * seg, seg)])
                    )
            row = pl.multiple_of((c * QUADS + j) * d_rows, 16)
            at = pl.ds(pl.multiple_of(z * d_rows, 16), d_rows)
            copies.append((sd_ref.at[pl.ds(row, d_rows), :], w_down.at[at, :]))
            first = 0
            for got, target, count in zip(gots, targets, counts):
                copies += got.copies(
                    rel, part_refs[first : first + count], z, target, got.rows, 0
                )
                first += count
        for copy in start(copies, sems):
            copy.wait()

        def forward(i, _):
            at = tile_at(i, TILE)
            normed, grad = n_all[at, :], y_all[at, :]
            gated = nn(normed, w_gate[...])
            upper = nn(normed, w_up[...])
            d_act = nt(grad, w_down[...])
            sig = 1.0 / (1.0 + jnp.exp(-gated))
            silu = gated * sig
            act[at, :] = (silu * upper).astype(BF)
            dgu[at, :cols] = (d_act * upper * sig * (1.0 + gated * (1.0 - sig))).astype(BF)
            dgu[at, cols:] = (d_act * silu).astype(BF)
            return 0

        lax.fori_loop(0, tokens // TILE, forward, 0)

        def back_in(s, _):
            grads = tn(n_all[:, tile_at(s, rows)], dgu[...])
            g_gate[s] = grads[:, :cols].astype(BF)
            g_up[s] = grads[:, cols:].astype(BF)
            return 0

        lax.fori_loop(0, depth, back_in, 0)

        def back_out(s, _):
            grads = tn(act[:, tile_at(s, d_rows)], y_all[...]).astype(BF)
            g_low[s] = grads[:half]
            g_high[s] = grads[half:]
            return 0

        lax.fori_loop(0, depth, back_out, 0)

    outs = [
        shaped((tokens, cols)),
        shaped((tokens, 2 * cols)),
        shaped((depth, rows, cols)),
        shaped((depth, rows, cols)),
        shaped((depth, half, width)),
        shaped((depth, half, width)),
    ]
    weights = [(width, cols), (width, cols), (cols, width)]
    scratch = [
        pltpu.VMEM((tokens, width), BF),
        pltpu.VMEM((tokens, width), BF),
        pltpu.SemaphoreType.DMA((total,)),
    ]
    if rel == 0:
        scratch = [pltpu.VMEM(shape, BF) for shape in weights] + scratch
    else:
        outs += [shaped(shape) for shape in weights]
    made = call(
        kernel,
        outs,
        pos,
        *n_two,
        *d_out,
        *shards,
        *parts,
        in_specs=[SCALARS] + [ANY] * (7 + len(parts)),
        out_specs=[WHOLE] * len(outs),
        scratch=scratch,
    )
    return made if rel else [*made, *(got.own for got in gots)]


def rows_product(lefts, rights, half, transposed, dtype):
    rows = lefts[0].shape[0] // 2
    per = len(rights) // len(lefts)
    width = rights[0].shape[0] if transposed else rights[0].shape[1]
    depth = rights[0].shape[1] if transposed else rights[0].shape[0]
    steps = rows // TILE

    def kernel(*refs):
        left, right, out = refs[: len(lefts)], refs[len(lefts) : -1], refs[-1]
        total = None
        for i, ref in enumerate(right):
            part = left[i // per][:, (i % per) * depth : (i % per + 1) * depth]
            term = (nt if transposed else nn)(part, ref[...])
            total = term if total is None else total + term
        out[...] = total.astype(dtype)

    return call(
        kernel,
        shaped((rows, width), dtype),
        *lefts,
        *rights,
        grid=(steps,),
        in_specs=[
            pl.BlockSpec((TILE, left.shape[1]), lambda i: (i + half * steps, 0)) for left in lefts
        ]
        + [pl.BlockSpec(right.shape, lambda i: (0, 0)) for right in rights],
        out_specs=pl.BlockSpec((TILE, width), lambda i: (i, 0)),
        vmem=56,
    )


def mix_back(low, other, mixed, weight):
    length, width = low.shape
    inner = mixed.shape[1]

    def kernel(a, b, mixed_ref, weight_ref, d_mixed, grad):
        for i in range(2 * length // TILE):
            at = slice(i * TILE, (i + 1) * TILE)
            part = a if i < length // TILE else b
            first = i * TILE % length
            d_mixed[at, :] = nt(part[first : first + TILE, :], weight_ref[...]).astype(BF)

        def body(i, _):
            at = tile_at(i, TILE)
            grad[at, :] = (
                tn(mixed_ref[:length, at], a[...]) + tn(mixed_ref[length:, at], b[...])
            ).astype(BF)
            return 0

        lax.fori_loop(0, inner // TILE, body, 0)

    return call(
        kernel,
        [shaped((2 * length, inner)), shaped((inner, width))],
        low,
        other,
        mixed,
        weight,
        in_specs=[WHOLE] * 4,
        out_specs=[WHOLE] * 2,
    )


def attention_grads(pos, normed, d_qkv, grad_out, depth, rows, low):
    width, cols = normed.shape[1], d_qkv.shape[1]
    quarter = rows // QUADS
    small = quarter // 2
    high = quarter - low + small

    def kernel(pos_ref, normed_ref, d_ref, out_ref, *refs):
        k = pos_ref[1]
        tile = refs[-1]

        def body(s, _):
            tile[...] = tn(normed_ref[:, tile_at(s, rows)], d_ref[...]).astype(BF)
            for rel in range(QUADS):
                j = k ^ rel
                first = pl.multiple_of(j * quarter, 16)
                refs[2 * rel][s] = tile[pl.ds(first, low), :]
                refs[2 * rel + 1][s, : quarter - low] = tile[pl.ds(first + low, quarter - low), :]
                at = pl.multiple_of(s * (rows // 2) + j * small, 16)
                refs[2 * rel + 1][s, quarter - low :] = out_ref[pl.ds(at, small), :]
            return 0

        lax.fori_loop(0, depth, body, 0)

    made = call(
        kernel,
        [shaped((depth, n, cols)) for _ in range(QUADS) for n in (low, high)],
        pos,
        normed,
        d_qkv,
        grad_out,
        in_specs=[SCALARS] + [WHOLE] * 3,
        out_specs=[WHOLE] * (2 * QUADS),
        scratch=[pltpu.VMEM((rows, cols), BF)],
    )
    return [(made[2 * rel], made[2 * rel + 1]) for rel in range(QUADS)]


def unpack_columns(pos, mine, other, depth):
    _, rows, cols = mine.shape
    seg = cols // depth
    width = cols * 2 * QUADS
    tile = 128

    def kernel(pos_ref, a, b, out):
        k, c = pos_ref[1], pos_ref[2]
        for ref, core in ((a, c), (b, 1 - c)):
            for rel in range(QUADS):
                block = core * QUADS + (k ^ rel)
                for s in range(depth):
                    at = pl.multiple_of((s * 2 * QUADS + block) * seg, 128)
                    out[:, pl.ds(at, seg)] = ref[rel, :, s * seg : (s + 1) * seg].astype(F32)

    spec = pl.BlockSpec((QUADS, tile, cols), lambda i: (0, i, 0))
    return call(
        kernel,
        shaped((rows, width), F32),
        pos,
        mine,
        other,
        grid=(rows // tile,),
        in_specs=[SCALARS, spec, spec],
        out_specs=pl.BlockSpec((tile, width), lambda i: (i, 0)),
    )


def unpack_rows(pos, parts, plans, heights, width):
    tile = 512

    def kernel(pos_ref, *refs):
        k, c = pos_ref[1], pos_ref[2]
        ins, outs = refs[: len(parts)], refs[len(parts) :]
        for i, plan in enumerate(plans):
            for ref, core in ((ins[2 * i], c), (ins[2 * i + 1], 1 - c)):
                for rel in range(QUADS):
                    block = core * QUADS + (k ^ rel)
                    for which, count, there, here in plan:
                        at = pl.multiple_of(block * heights[which] + there, 8)
                        outs[which][pl.ds(at, count), :] = ref[
                            rel, here : here + count, :
                        ].astype(F32)

    return call(
        kernel,
        [shaped((2 * QUADS * height, width), F32) for height in heights],
        pos,
        *parts,
        grid=(width // tile,),
        in_specs=[SCALARS]
        + [pl.BlockSpec((QUADS, i.shape[1], tile), lambda i: (0, 0, i)) for i in parts],
        out_specs=[
            pl.BlockSpec((2 * QUADS * height, tile), lambda i: (0, i)) for height in heights
        ],
    )


def on_device(
    reps,
    depth,
    tokens,
    gain_attn,
    w_query,
    w_key,
    w_value,
    w_out,
    gain_ffn,
    w_gate,
    w_up,
    w_down,
    cotangent,
):
    links = Links(reps, depth)
    z = lax.axis_index("fsdp")
    r = lax.axis_index("rep")
    c = r % 2
    k = (r // 2) % QUADS
    pos = jnp.stack([z, k, c]).astype(jnp.int32)
    length = tokens.shape[0]
    rows = w_query.shape[0]
    quarter = rows // QUADS
    small = quarter // 2
    inner = D // 2
    narrow = inner // (HEADS // KV)

    def core_columns(weight):
        split = weight.reshape(rows, depth, 2, weight.shape[1] // (2 * depth))
        return lax.dynamic_index_in_dim(split, c, 2, keepdims=False).reshape(rows, -1)

    shard_qkv = jnp.concatenate([core_columns(i) for i in (w_query, w_key, w_value)], axis=1)
    shard_out = lax.dynamic_slice_in_dim(w_out, c * (rows // 2), rows // 2, 0)
    piece_qkv = lax.dynamic_slice_in_dim(shard_qkv, k * quarter, quarter, 0)
    piece_out = lax.dynamic_slice_in_dim(shard_out, k * small, small, 0)
    seg = w_gate.shape[1] // (depth * 2 * QUADS)
    d_rows = w_down.shape[0] // (2 * QUADS)

    def block_columns(weight):
        return jnp.concatenate(
            [
                lax.dynamic_slice_in_dim(weight, ((s * 2 + c) * QUADS + k) * seg, seg, 1)
                for s in range(depth)
            ],
            axis=1,
        )

    piece_gate, piece_up = block_columns(w_gate), block_columns(w_up)
    piece_down = lax.dynamic_slice_in_dim(w_down, (c * QUADS + k) * d_rows, d_rows, 0)

    got_qkv = links.spread(pos, piece_qkv, 3 * quarter // 2)
    got_out = links.spread(pos, piece_out, 80)
    got_gate = links.spread(pos, piece_gate, 3 * rows // 2)
    got_up = links.spread(pos, piece_up, 3 * rows // 2)
    got_down = links.spread(pos, piece_down, 3 * d_rows // 2)

    gains = jnp.stack([gain_attn, gain_ffn])
    gains = jnp.stack([gains] + [links.shift(gains, by) for by in range(1, depth)])
    gains = jnp.take(gains, (z - jnp.arange(depth)) % depth, axis=0)
    g_one = gains[:, 0].reshape(1, -1).astype(F32)
    g_two = gains[:, 1].reshape(1, -1).astype(F32)
    token_pair = (tokens, links.swap(tokens, 1))
    d_pair = (cotangent, links.swap(cotangent, 1))
    turns = tables(length)

    n_one, q, key, value, wqkv = project(pos, token_pair, g_one, got_qkv, shard_qkv, turns)
    mixed, lse = attend(q, key, value)
    to_other, mine, wo = mix(pos, mixed, got_out, shard_out)
    hidden, n_two = residual_norm(tokens, mine, links.swap(to_other, 1), g_two)

    n_pair = (n_two, links.swap(n_two, 1))
    blocks = [None] * QUADS
    for rel in (3, 1, 2, 0):
        blocks[rel] = ffn_block(
            pos, rel, n_pair, d_pair, (w_gate, w_up, w_down), (got_gate, got_up, got_down)
        )
    sums_gate, sums_up = links.collect([(b[2], b[3]) for b in blocks])
    sums_low, sums_high = links.collect([(b[4], b[5]) for b in blocks])

    lefts = [b[1] for b in blocks]
    rights = [w for b in blocks for w in (b[6], b[7])]
    to_other = rows_product(lefts, rights, 1, True, BF)
    mine = rows_product(lefts, rights, 0, True, F32)
    d_hidden, grad_g_two, low = norm_back(
        mine, links.swap(to_other, 1), hidden, cotangent, g_two, 1
    )
    acts, downs = [b[0] for b in blocks], [b[8] for b in blocks]
    out_other = rows_product(acts, downs, 1, False, BF)
    out_mine = rows_product(acts, downs, 0, False, F32)
    result = (hidden + out_mine + links.swap(out_other, 1).astype(F32)).astype(BF)

    d_mixed, grad_out = mix_back(low, links.swap(low, 1), mixed, wo)
    d_qkv = attend_back(q, key, value, lse, d_mixed, turns)
    split = 80
    packs = attention_grads(pos, n_one, d_qkv, grad_out, depth, rows, split)
    sums_one, sums_two = links.collect(packs)
    to_other = rows_product([d_qkv], [wqkv], 1, True, BF)
    mine = rows_product([d_qkv], [wqkv], 0, True, F32)
    input_grad, grad_g_one = norm_back(
        mine, links.swap(to_other, 1), tokens, d_hidden, g_one, 0
    )

    a, b, d, e = links.share(sums_gate, sums_up)
    share_gate, share_up = unpack_columns(pos, a, b, depth), unpack_columns(pos, d, e, depth)
    half = d_rows // 2
    (share_down,) = unpack_rows(
        pos,
        links.share(sums_low, sums_high),
        [[(0, half, 0, 0)], [(0, half, half, 0)]],
        [d_rows],
        D,
    )
    qkv_rows, share_out = unpack_rows(
        pos,
        links.share(sums_one, sums_two),
        [
            [(0, split, 0, 0)],
            [(0, quarter - split, split, 0), (1, small, 0, quarter - split)],
        ],
        [quarter, small],
        D,
    )
    qkv_rows = qkv_rows.reshape(2, rows, -1)

    def both_cores(first, width):
        part = qkv_rows[:, :, first : first + width].reshape(2, rows, depth, width // depth)
        return part.transpose(1, 2, 0, 3).reshape(rows, 2 * width)

    share_q = both_cores(0, inner)
    share_k = both_cores(inner, narrow)
    share_v = both_cores(inner + narrow, narrow)

    sums = jnp.concatenate([grad_g_one, grad_g_two], axis=0)
    for bit in (1, 2, 4):
        sums = sums + links.swap(sums, bit)
    sums = links.cells(sums)
    sums = sums.reshape(2, depth, rows)

    def own_part(at):
        return lax.dynamic_index_in_dim(sums, at % depth, 1, keepdims=False)

    gain_sums = own_part(z)
    for by in range(1, depth):
        gain_sums = gain_sums + links.shift(own_part(z + by), by)
    return (
        result,
        input_grad,
        gain_sums[0],
        share_q,
        share_k,
        share_v,
        share_out,
        gain_sums[1],
        share_gate,
        share_up,
        share_down,
    )


def solution(mesh):
    tokens = P(("rep", "fsdp"), None)
    gain, weight = P("fsdp"), P("fsdp", None)
    return jax.shard_map(
        functools.partial(on_device, mesh.shape["rep"], mesh.shape["fsdp"]),
        mesh=mesh,
        in_specs=(tokens, gain, *[weight] * 4, gain, *[weight] * 3, tokens),
        out_specs=(tokens, tokens, gain, *[weight] * 4, gain, *[weight] * 3),
        check_vma=False,
    )
```

```python
import functools
import math

import jax
import jax.numpy as jnp
from jax import lax
from jax.experimental import pallas as pl
from jax.experimental.pallas import tpu as pltpu
from jax.sharding import PartitionSpec as P

D = 1536
HEADS = 16
KV = 8
HD = 96
BF = jnp.bfloat16
F32 = jnp.float32
MiB = 1024 * 1024
ANY = pl.BlockSpec(memory_space=pl.ANY)
WHOLE = pl.BlockSpec(memory_space=pltpu.VMEM)
SCALARS = pl.BlockSpec(memory_space=pltpu.SMEM)
QUADS = 4
TILE = 256
SCALE = 1.0 / math.sqrt(HD)
PACE = 0.5


def after(value, *earlier):
    return lax.optimization_barrier((value, *earlier))[0]


def nt(a, b):
    return lax.dot_general(a, b, (((1,), (1,)), ((), ())), preferred_element_type=F32)


def tn(a, b):
    return lax.dot_general(a, b, (((0,), (0,)), ((), ())), preferred_element_type=F32)


def nn(a, b):
    return jnp.dot(a, b, preferred_element_type=F32)


def rms(values):
    return lax.rsqrt(jnp.mean(values * values, axis=-1, keepdims=True) + 1e-05)


def tile_at(i, size):
    return pl.ds(pl.multiple_of(i * size, size), size)


def call(
    kernel,
    out_shape,
    *args,
    scratch=(),
    vmem=48,
    grid=(),
    in_specs=None,
    out_specs=None,
    us=5,
):
    return pl.pallas_call(
        kernel,
        grid=grid,
        out_shape=out_shape,
        in_specs=in_specs,
        out_specs=out_specs,
        scratch_shapes=list(scratch),
        compiler_params=pltpu.CompilerParams(vmem_limit_bytes=vmem * MiB),
        cost_estimate=pl.CostEstimate(
            flops=int(us * PACE * 1.15e9), bytes_accessed=1024, transcendentals=0
        ),
    )(*args)


def shaped(shape, dtype=BF):
    return jax.ShapeDtypeStruct(shape, dtype)


class Links:
    def __init__(self, reps, depth):
        self.reps, self.depth = reps, depth
        self.rounds = [[], [], []]

    def swap(self, value, bit):
        return lax.ppermute(value, "rep", [(i, i ^ bit) for i in range(self.reps)])

    def round(self, along_x, along_y):
        earlier = self.rounds[-2] + self.rounds[-3]
        moved = [self.swap(after(along_x, *earlier), 2), self.swap(after(along_y, *earlier), 4)]
        self.rounds.append(moved)
        return moved

    def shift(self, value, by):
        return lax.ppermute(value, "fsdp", [(i, (i + by) % self.depth) for i in range(self.depth)])

    def cells(self, value):
        if self.reps == 2 * QUADS:
            return value
        groups = [
            [cell * 2 * QUADS + i for cell in range(self.reps // (2 * QUADS))]
            for i in range(2 * QUADS)
        ]
        return lax.psum(value, "rep", axis_index_groups=groups)

    def spread(self, pos, piece, cut):
        return Gathered(self, pos, piece, cut)


class Summed:
    def __init__(self, links, along_x, along_y):
        self.links = links
        self.low_y, self.high_x = along_y[0], along_x[1]
        self.x_low, self.y_high = links.round(along_x[0], along_y[1])

    def corner(self, low, high):
        self.from_x, self.from_y = self.links.round(low, high)

    def add(self):
        x_high = (self.high_x.astype(F32) + self.from_y.astype(F32)).astype(BF)
        y_low = (self.low_y.astype(F32) + self.from_x.astype(F32)).astype(BF)
        self.added = [x_high, y_low]

    def rest(self):
        self.x_high, self.y_low = self.links.round(*self.added)

    def total(self, low, high):
        depth, n, m = low.shape
        rows = n + high.shape[1]

        def kernel(a, b, c, d, e, f, out):
            out[:, :n] = (
                a[...].astype(F32) + b[...].astype(F32) + c[...].astype(F32)
            ).astype(BF)
            out[:, n:] = (
                d[...].astype(F32) + e[...].astype(F32) + f[...].astype(F32)
            ).astype(BF)

        def block(height):
            return pl.BlockSpec((1, height, m), lambda i: (i, 0, 0))

        return call(
            kernel,
            shaped((depth, rows, m)),
            low,
            self.x_low,
            self.y_low,
            high,
            self.x_high,
            self.y_high,
            grid=(depth,),
            in_specs=[block(n)] * 3 + [block(rows - n)] * 3,
            out_specs=block(rows),
            us=5,
        )

    def own(self, low, high, earlier):
        total = self.total(after(low, earlier), high)
        return self.links.cells(
            lax.psum_scatter(total, "fsdp", scatter_dimension=0, tiled=True)[0]
        )


class Gathered:
    def __init__(self, links, pos, piece, cut):
        self.rows, self.cut, self.depth = piece.shape[0], cut, links.depth
        n, m, depth = piece.shape[0], piece.shape[1], links.depth
        self.own = lax.all_gather(piece, "fsdp", axis=0, tiled=True)

        def kernel(pos_ref, in_ref, out_ref):
            out_ref[...] = in_ref[...]

        remote = pl.pallas_call(
            kernel,
            grid_spec=pltpu.PrefetchScalarGridSpec(
                num_scalar_prefetch=1,
                grid=(depth - 1,),
                in_specs=[pl.BlockSpec((n, m), lambda i, at: (lax.rem(at[0] + 1 + i, depth), 0))],
                out_specs=pl.BlockSpec((n, m), lambda i, at: (i, 0)),
            ),
            out_shape=shaped(((depth - 1) * n, m)),
            cost_estimate=pl.CostEstimate(
                flops=int(4 * PACE * 1.15e9), bytes_accessed=1024, transcendentals=0
            ),
        )(pos, self.own)
        self.links, self.remote = links, remote

    def to_plane(self):
        self.x, self.y = self.links.round(self.remote, self.remote)
        self.parts = after(self.y[: self.cut], self.x), after(self.x[self.cut :], self.y)

    def to_corner(self):
        self.corner = self.links.round(*self.parts)

    def arrays(self, rel):
        return self.corner if rel == 3 else ((self.own, self.x, self.y)[rel],)

    def segments(self, rel, low, high):
        n = self.rows
        found = []
        for i in range(self.depth - 1):
            first, last = i * n + low, i * n + high
            if rel == 0:
                found.append((0, i, low, high - low, 0))
            elif rel < 3:
                found.append((0, i, first, high - low, 0))
            else:
                if first < self.cut:
                    found.append((0, i, first, min(last, self.cut) - first, 0))
                if last > self.cut:
                    begin = max(first, self.cut)
                    found.append((1, i, begin - self.cut, last - begin, begin - first))
        return found

    def copies(self, rel, refs, z, target, stride, base, low, high):
        out = []
        for which, i, row, count, offset in self.segments(rel, low, high):
            shard = lax.rem(z + 1 + i, self.depth)
            source = pl.multiple_of(shard * self.rows + row, 16) if rel == 0 else row
            at = pl.multiple_of(shard * stride + base + offset, 16)
            out.append((refs[which].at[pl.ds(source, count), :], target.at[pl.ds(at, count), :]))
        return out


def start(copies, sems, first=0):
    made = [
        pltpu.make_async_copy(source, target, sems.at[first + i])
        for i, (source, target) in enumerate(copies)
    ]
    for copy in made:
        copy.start()
    return made


def all_parts(got):
    return [array for rel in range(QUADS) for array in got.arrays(rel)]


def whole_copies(got, refs, z, k, target, stride, low, high):
    out, at = [], 0
    for rel in range(QUADS):
        size = len(got.arrays(rel))
        base = (k ^ rel) * (high - low)
        out += got.copies(rel, refs[at : at + size], z, target, stride, base, low, high)
        at += size
    return out


def n_copies(got, low, high, rels=range(QUADS)):
    return sum(len(got.segments(rel, low, high)) for rel in rels)


def tables(length):
    freq = 10000.0 ** (-jnp.arange(0, HD, 2).astype(F32) / HD)
    angle = jnp.arange(length).astype(F32)[:, None] * freq[None, :]
    cosine, sine = jnp.cos(angle), jnp.sin(angle)
    none = jnp.zeros_like(sine)

    def four(a, b):
        return jnp.concatenate([a, b] * 4, axis=1)

    return four(cosine, cosine), four(-sine, none), four(none, sine)


def rotated(u, cosine, right, left, sign):
    width = u.shape[1]
    turned = pltpu.roll(u, width - HD // 2, 1) * right + pltpu.roll(u, HD // 2, 1) * left
    return u * cosine + sign * turned


def project(pos, pair, gain, got, shard, turns):
    length, width = pair[0].shape
    cols = shard.shape[1]
    rows = shard.shape[0]
    parts = all_parts(got)
    narrow = cols // 4
    high = rows // QUADS
    copies_in = 3 + n_copies(got, 0, high)

    def kernel(pos_ref, gain_ref, cos_ref, right_ref, left_ref, ta, tb, shard_ref, *refs):
        part_refs = refs[: len(parts)]
        normed, q, key, value, weight, toks, sems = refs[len(parts) :]
        z, k = pos_ref[0], pos_ref[1]
        first = start(
            [(ta, toks.at[pl.ds(0, length), :]), (tb, toks.at[pl.ds(length, length), :])], sems
        )
        second = start(
            [(shard_ref, weight.at[pl.ds(pl.multiple_of(z * rows, 16), rows), :])]
            + whole_copies(got, part_refs, z, k, weight, rows, 0, high),
            sems,
            2,
        )
        for copy in first:
            copy.wait()

        def norm(i, _):
            at = tile_at(i, TILE)
            x = toks[at, :].astype(F32)
            normed[at, :] = (x * rms(x) * gain_ref[...]).astype(BF)
            return 0

        lax.fori_loop(0, 2 * length // TILE, norm, 0)
        for copy in second:
            copy.wait()

        def body(i, _):
            at = tile_at(i, TILE)
            place = tile_at(lax.rem(i, length // TILE), TILE)
            out = nn(normed[at, :], weight[...])
            cosine, right, left = cos_ref[place, :], right_ref[place, :], left_ref[place, :]
            for t in range(2):
                u = out[:, t * narrow : (t + 1) * narrow]
                q[at, t * narrow : (t + 1) * narrow] = rotated(
                    u, cosine, right, left, 1.0
                ).astype(BF)
            key[at, :] = rotated(
                out[:, 2 * narrow : 3 * narrow], cosine, right, left, 1.0
            ).astype(BF)
            value[at, :] = out[:, 3 * narrow :].astype(BF)
            return 0

        lax.fori_loop(0, 2 * length // TILE, body, 0)

    return call(
        kernel,
        [
            shaped((2 * length, width)),
            shaped((2 * length, 2 * narrow)),
            shaped((2 * length, narrow)),
            shaped((2 * length, narrow)),
            shaped((width, cols)),
        ],
        pos,
        gain,
        *turns,
        *pair,
        shard,
        *parts,
        in_specs=[SCALARS] + [WHOLE] * 4 + [ANY] * (3 + len(parts)),
        out_specs=[WHOLE] * 5,
        scratch=[pltpu.VMEM((2 * length, width), BF), pltpu.SemaphoreType.DMA((copies_in,))],
        us=13,
    )


def masked(scores, first):
    keys = lax.broadcasted_iota(jnp.int32, scores.shape, 0)
    queries = lax.broadcasted_iota(jnp.int32, scores.shape, 1) + first
    return jnp.where(keys <= queries, scores, -1e30)


def attend(q, key, value):
    length = q.shape[0] // 2
    heads, groups = q.shape[1] // HD, key.shape[1] // HD

    def kernel(q_ref, k_ref, v_ref, o_ref, lse_ref):
        for g in range(groups):
            keys = k_ref[:, g * HD : (g + 1) * HD]
            turned = v_ref[:, g * HD : (g + 1) * HD].T
            for j in range(g * heads // groups, (g + 1) * heads // groups):
                for t in range(length // TILE):
                    at = slice(t * TILE, (t + 1) * TILE)
                    reach = (t + 1) * TILE
                    s = nt(keys[:reach], q_ref[at, j * HD : (j + 1) * HD]) * SCALE
                    s = masked(s, t * TILE)
                    peak = jnp.max(s, axis=0, keepdims=True)
                    e = jnp.exp(s - peak)
                    total = jnp.sum(e, axis=0, keepdims=True)
                    lse = peak + jnp.log(total)
                    p = (e * (1.0 / total)).astype(BF)
                    lse_ref[0, j : j + 1, at] = lse
                    o_ref[at, j * HD : (j + 1) * HD] = nn(turned[:, :reach], p).T.astype(BF)

    return call(
        kernel,
        [shaped(q.shape), shaped((2, heads, length), F32)],
        q,
        key,
        value,
        grid=(2,),
        in_specs=[
            pl.BlockSpec((length, q.shape[1]), lambda i: (i, 0)),
            pl.BlockSpec((length, key.shape[1]), lambda i: (i, 0)),
            pl.BlockSpec((length, key.shape[1]), lambda i: (i, 0)),
        ],
        out_specs=[
            pl.BlockSpec((length, q.shape[1]), lambda i: (i, 0)),
            pl.BlockSpec((1, heads, length), lambda i: (i, 0, 0)),
        ],
        us=10,
    )


def attend_back(q, key, value, lse, d_mixed, turns):
    length = q.shape[0] // 2
    heads, groups = q.shape[1] // HD, key.shape[1] // HD
    inner, narrow = q.shape[1], key.shape[1]

    def kernel(q_ref, k_ref, v_ref, lse_ref, do_ref, cos_ref, right_ref, left_ref, out, dq, dk):
        for g in range(groups):
            keys = k_ref[:, g * HD : (g + 1) * HD]
            values = v_ref[:, g * HD : (g + 1) * HD]
            turned = keys.T
            d_key = [jnp.zeros((TILE, HD), F32) for _ in range(length // TILE)]
            d_value = [jnp.zeros((TILE, HD), F32) for _ in range(length // TILE)]
            for j in range(g * heads // groups, (g + 1) * heads // groups):
                for t in range(length // TILE):
                    at = slice(t * TILE, (t + 1) * TILE)
                    reach = (t + 1) * TILE
                    queries = q_ref[at, j * HD : (j + 1) * HD]
                    upstream = do_ref[at, j * HD : (j + 1) * HD]
                    s = masked(nt(keys[:reach], queries) * SCALE, t * TILE)
                    p = jnp.exp(s - lse_ref[0, j : j + 1, at])
                    dp = nt(values[:reach], upstream)
                    centre = jnp.sum(p * dp, axis=0, keepdims=True)
                    ds = (p * (dp - centre)).astype(BF)
                    from_values = nn(p.astype(BF), upstream)
                    from_keys = nn(ds, queries)
                    for i in range(t + 1):
                        rows = slice(i * TILE, (i + 1) * TILE)
                        d_value[i] = d_value[i] + from_values[rows]
                        d_key[i] = d_key[i] + from_keys[rows]
                    dq[at, j * HD : (j + 1) * HD] = nn(turned[:, :reach], ds).T * SCALE
            for i in range(length // TILE):
                rows = slice(i * TILE, (i + 1) * TILE)
                dk[rows, g * HD : (g + 1) * HD] = d_key[i] * SCALE
                first = inner + narrow + g * HD
                out[rows, first : first + HD] = d_value[i].astype(BF)
        cosine, right, left = cos_ref[...], right_ref[...], left_ref[...]
        for t in range(inner // narrow):
            cols = slice(t * narrow, (t + 1) * narrow)
            out[:, cols] = rotated(dq[:, cols], cosine, right, left, -1.0).astype(BF)
        out[:, inner : inner + narrow] = rotated(dk[...], cosine, right, left, -1.0).astype(BF)

    def block(cols):
        return pl.BlockSpec((length, cols), lambda i: (i, 0))

    table = pl.BlockSpec(turns[0].shape, lambda i: (0, 0))
    return call(
        kernel,
        shaped((2 * length, inner + 2 * narrow)),
        q,
        key,
        value,
        lse,
        d_mixed,
        *turns,
        grid=(2,),
        in_specs=[
            block(inner),
            block(narrow),
            block(narrow),
            pl.BlockSpec((1, heads, length), lambda i: (i, 0, 0)),
            block(inner),
            table,
            table,
            table,
        ],
        out_specs=block(inner + 2 * narrow),
        scratch=[pltpu.VMEM((length, inner), F32), pltpu.VMEM((length, narrow), F32)],
        us=17,
    )


def mix(pos, mixed, got, shard):
    tokens, inner = mixed.shape
    width = shard.shape[1]
    rows = shard.shape[0]
    high = got.rows
    low = high - rows // QUADS
    parts = all_parts(got)

    def kernel(pos_ref, mixed_ref, shard_ref, *refs):
        part_refs = refs[: len(parts)]
        other, mine, weight, sems = refs[len(parts) :]
        z, k = pos_ref[0], pos_ref[1]
        copies = start(
            [(shard_ref, weight.at[pl.ds(pl.multiple_of(z * rows, 16), rows), :])]
            + whole_copies(got, part_refs, z, k, weight, rows, low, high),
            sems,
        )
        for copy in copies:
            copy.wait()
        for i in range(tokens // 2 // TILE):
            at = slice(i * TILE, (i + 1) * TILE)
            there = slice(tokens // 2 + i * TILE, tokens // 2 + (i + 1) * TILE)
            other[at, :] = nn(mixed_ref[there, :], weight[...]).astype(BF)
            mine[at, :] = nn(mixed_ref[at, :], weight[...])

    return call(
        kernel,
        [
            shaped((tokens // 2, width)),
            shaped((tokens // 2, width), F32),
            shaped((inner, width)),
        ],
        pos,
        mixed,
        shard,
        *parts,
        in_specs=[SCALARS, WHOLE] + [ANY] * (1 + len(parts)),
        out_specs=[WHOLE] * 3,
        scratch=[pltpu.SemaphoreType.DMA((1 + n_copies(got, low, high),))],
        us=8,
    )


def residual_norm(tokens, mine, received, gain):
    length, width = tokens.shape

    def kernel(x, a, b, gain_ref, hidden, normed):
        h = x[...].astype(F32) + a[...] + b[...].astype(F32)
        hidden[...] = h
        normed[...] = (h * rms(h) * gain_ref[...]).astype(BF)

    block = pl.BlockSpec((TILE, width), lambda i: (i, 0))
    return call(
        kernel,
        [shaped((length, width), F32), shaped((length, width))],
        tokens,
        mine,
        received,
        gain,
        grid=(length // TILE,),
        in_specs=[block, block, block, pl.BlockSpec((1, width), lambda i: (0, 0))],
        out_specs=[block, block],
        us=4,
    )


def norm_back(mine, received, values, residual, gain, rounded):
    length, width = values.shape

    def kernel(a, b, values_ref, residual_ref, gain_ref, grad, gain_grad, *low):
        x = values_ref[...].astype(F32)
        factor = rms(x)
        normed = x * factor
        upstream = a[...] + b[...].astype(F32)
        part = jnp.sum(upstream * normed, axis=0, keepdims=True)

        @pl.when(pl.program_id(0) == 0)
        def _():
            gain_grad[...] = part

        @pl.when(pl.program_id(0) > 0)
        def _():
            gain_grad[...] += part

        scaled = upstream * gain_ref[...]
        inside = scaled - normed * jnp.mean(scaled * normed, axis=-1, keepdims=True)
        total = residual_ref[...].astype(F32) + factor * inside
        grad[...] = total
        if low:
            low[0][...] = total.astype(BF)

    block = pl.BlockSpec((TILE, width), lambda i: (i, 0))
    line = pl.BlockSpec((1, width), lambda i: (0, 0))
    return call(
        kernel,
        [shaped((length, width), F32), shaped((1, width), F32)]
        + [shaped((length, width))] * rounded,
        mine,
        received,
        values,
        residual,
        gain,
        grid=(length // TILE,),
        in_specs=[block] * 4 + [line],
        out_specs=[block, line] + [block] * rounded,
        us=5,
    )


def ffn_block(pos, rel, n_two, d_out, shards, gots):
    depth = gots[0].depth
    rows, d_rows = shards[0].shape[0], gots[2].rows
    cols = gots[0].own.shape[1]
    length, width = n_two[0].shape
    tokens = 2 * length
    seg = cols // depth
    parts = [array for got in gots for array in got.arrays(rel)]
    counts = [len(got.arrays(rel)) for got in gots]
    total = 4 + 3 + 2 * depth + sum(n_copies(got, 0, got.rows, [rel]) for got in gots)
    half = d_rows // 2

    def kernel(pos_ref, na, nb, ya, yb, sg_ref, su_ref, sd_ref, *refs):
        part_refs, refs = refs[: len(parts)], refs[len(parts) :]
        act, dgu, g_gate, g_up, g_low, g_high, w_gate, w_up, w_down, n_all, y_all, sems = refs
        targets = (w_gate, w_up, w_down)
        z, k, c = pos_ref[0], pos_ref[1], pos_ref[2]
        copies = [
            (na, n_all.at[pl.ds(0, length), :]),
            (nb, n_all.at[pl.ds(length, length), :]),
            (ya, y_all.at[pl.ds(0, length), :]),
            (yb, y_all.at[pl.ds(length, length), :]),
        ]
        if rel == 0:
            copies += list(zip(part_refs, targets))
        else:
            j = k ^ rel
            for source, target in ((sg_ref, w_gate), (su_ref, w_up)):
                for s in range(depth):
                    col = pl.multiple_of(((s * 2 + c) * QUADS + j) * seg, 128)
                    at = pl.ds(pl.multiple_of(z * rows, 16), rows)
                    copies.append(
                        (source.at[:, pl.ds(col, seg)], target.at[at, pl.ds(s * seg, seg)])
                    )
            row = pl.multiple_of((c * QUADS + j) * d_rows, 16)
            at = pl.ds(pl.multiple_of(z * d_rows, 16), d_rows)
            copies.append((sd_ref.at[pl.ds(row, d_rows), :], w_down.at[at, :]))
            first = 0
            for got, target, count in zip(gots, targets, counts):
                copies += got.copies(
                    rel, part_refs[first : first + count], z, target, got.rows, 0, 0, got.rows
                )
                first += count
        for copy in start(copies, sems):
            copy.wait()

        def forward(i, _):
            at = tile_at(i, TILE)
            normed, grad = n_all[at, :], y_all[at, :]
            gated = nn(normed, w_gate[...])
            upper = nn(normed, w_up[...])
            d_act = nt(grad, w_down[...])
            sig = 1.0 / (1.0 + jnp.exp(-gated))
            silu = gated * sig
            act[at, :] = (silu * upper).astype(BF)
            dgu[at, :cols] = (d_act * upper * sig * (1.0 + gated * (1.0 - sig))).astype(BF)
            dgu[at, cols:] = (d_act * silu).astype(BF)
            return 0

        lax.fori_loop(0, tokens // TILE, forward, 0)

        def back_in(s, _):
            grads = tn(n_all[:, tile_at(s, rows)], dgu[...])
            g_gate[s] = grads[:, :cols].astype(BF)
            g_up[s] = grads[:, cols:].astype(BF)
            return 0

        lax.fori_loop(0, depth, back_in, 0)

        def back_out(s, _):
            grads = tn(act[:, tile_at(s, d_rows)], y_all[...]).astype(BF)
            g_low[s] = grads[:half]
            g_high[s] = grads[half:]
            return 0

        lax.fori_loop(0, depth, back_out, 0)

    outs = [
        shaped((tokens, cols)),
        shaped((tokens, 2 * cols)),
        shaped((depth, rows, cols)),
        shaped((depth, rows, cols)),
        shaped((depth, half, width)),
        shaped((depth, half, width)),
    ]
    weights = [(width, cols), (width, cols), (cols, width)]
    scratch = [
        pltpu.VMEM((tokens, width), BF),
        pltpu.VMEM((tokens, width), BF),
        pltpu.SemaphoreType.DMA((total,)),
    ]
    if rel == 0:
        scratch = [pltpu.VMEM(shape, BF) for shape in weights] + scratch
    else:
        outs += [shaped(shape) for shape in weights]
    made = call(
        kernel,
        outs,
        pos,
        *n_two,
        *d_out,
        *shards,
        *parts,
        in_specs=[SCALARS] + [ANY] * (7 + len(parts)),
        out_specs=[WHOLE] * len(outs),
        scratch=scratch,
        us=20,
    )
    return made if rel else [*made, *(got.own for got in gots)]


def rows_product(lefts, rights, half, transposed, dtype, us):
    rows = lefts[0].shape[0] // 2
    per = len(rights) // len(lefts)
    width = rights[0].shape[0] if transposed else rights[0].shape[1]
    depth = rights[0].shape[1] if transposed else rights[0].shape[0]
    steps = rows // TILE

    def kernel(*refs):
        left, right, out = refs[: len(lefts)], refs[len(lefts) : -1], refs[-1]
        total = None
        for i, ref in enumerate(right):
            part = left[i // per][:, (i % per) * depth : (i % per + 1) * depth]
            term = (nt if transposed else nn)(part, ref[...])
            total = term if total is None else total + term
        out[...] = total.astype(dtype)

    return call(
        kernel,
        shaped((rows, width), dtype),
        *lefts,
        *rights,
        grid=(steps,),
        in_specs=[
            pl.BlockSpec((TILE, left.shape[1]), lambda i: (i + half * steps, 0)) for left in lefts
        ]
        + [pl.BlockSpec(right.shape, lambda i: (0, 0)) for right in rights],
        out_specs=pl.BlockSpec((TILE, width), lambda i: (i, 0)),
        vmem=56,
        us=us,
    )


def mix_back(low, other, mixed, weight):
    length, width = low.shape
    inner = mixed.shape[1]

    def kernel(a, b, mixed_ref, weight_ref, d_mixed, grad):
        for i in range(2 * length // TILE):
            at = slice(i * TILE, (i + 1) * TILE)
            part = a if i < length // TILE else b
            first = i * TILE % length
            d_mixed[at, :] = nt(part[first : first + TILE, :], weight_ref[...]).astype(BF)

        def body(i, _):
            at = tile_at(i, TILE)
            grad[at, :] = (
                tn(mixed_ref[:length, at], a[...]) + tn(mixed_ref[length:, at], b[...])
            ).astype(BF)
            return 0

        lax.fori_loop(0, inner // TILE, body, 0)

    return call(
        kernel,
        [shaped((2 * length, inner)), shaped((inner, width))],
        low,
        other,
        mixed,
        weight,
        in_specs=[WHOLE] * 4,
        out_specs=[WHOLE] * 2,
        us=10,
    )


def attention_grads(pos, normed, d_qkv, grad_out, depth, rows, low):
    width, cols = normed.shape[1], d_qkv.shape[1]
    quarter = rows // QUADS
    small = quarter // 2
    high = quarter - low + small

    def kernel(pos_ref, normed_ref, d_ref, out_ref, *refs):
        k = pos_ref[1]
        tile = refs[-1]

        def body(s, _):
            tile[...] = tn(normed_ref[:, tile_at(s, rows)], d_ref[...]).astype(BF)
            for rel in range(QUADS):
                j = k ^ rel
                first = pl.multiple_of(j * quarter, 16)
                refs[2 * rel][s] = tile[pl.ds(first, low), :]
                refs[2 * rel + 1][s, : quarter - low] = tile[pl.ds(first + low, quarter - low), :]
                at = pl.multiple_of(s * (rows // 2) + j * small, 16)
                refs[2 * rel + 1][s, quarter - low :] = out_ref[pl.ds(at, small), :]
            return 0

        lax.fori_loop(0, depth, body, 0)

    made = call(
        kernel,
        [shaped((depth, n, cols)) for _ in range(QUADS) for n in (low, high)],
        pos,
        normed,
        d_qkv,
        grad_out,
        in_specs=[SCALARS] + [WHOLE] * 3,
        out_specs=[WHOLE] * (2 * QUADS),
        scratch=[pltpu.VMEM((rows, cols), BF)],
        us=10,
    )
    return [(made[2 * rel], made[2 * rel + 1]) for rel in range(QUADS)]


def unpack_columns(pos, mine, other, depth, half):
    rows, cols = mine.shape[1] // 2, mine.shape[2]
    seg = cols // depth
    width = cols * 2 * QUADS
    tile = 128
    steps = rows // tile

    def kernel(pos_ref, a, b, out):
        k, c = pos_ref[1], pos_ref[2]
        for ref, core in ((a, c), (b, 1 - c)):
            for rel in range(QUADS):
                block = core * QUADS + (k ^ rel)
                for s in range(depth):
                    at = pl.multiple_of((s * 2 * QUADS + block) * seg, 128)
                    out[:, pl.ds(at, seg)] = ref[rel, :, s * seg : (s + 1) * seg].astype(F32)

    spec = pl.BlockSpec((QUADS, tile, cols), lambda i: (0, i + half * steps, 0))
    return call(
        kernel,
        shaped((rows, width), F32),
        pos,
        mine,
        other,
        grid=(steps,),
        in_specs=[SCALARS, spec, spec],
        out_specs=pl.BlockSpec((tile, width), lambda i: (i, 0)),
        us=4,
    )


def unpack_rows(pos, mine, other):
    _, rows, width = mine.shape
    tile = 512

    def kernel(pos_ref, a, b, out):
        k, c = pos_ref[1], pos_ref[2]
        for ref, core in ((a, c), (b, 1 - c)):
            for rel in range(QUADS):
                at = pl.multiple_of((core * QUADS + (k ^ rel)) * rows, 8)
                out[pl.ds(at, rows), :] = ref[rel].astype(F32)

    spec = pl.BlockSpec((QUADS, rows, tile), lambda i: (0, 0, i))
    return call(
        kernel,
        shaped((2 * QUADS * rows, width), F32),
        pos,
        mine,
        other,
        grid=(width // tile,),
        in_specs=[SCALARS, spec, spec],
        out_specs=pl.BlockSpec((2 * QUADS * rows, tile), lambda i: (0, i)),
        us=5,
    )


def unpack_attention(pos, mine, other, depth, rows, inner, narrow):
    quarter = rows // QUADS
    small = quarter // 2

    def kernel(pos_ref, a, b, *outs):
        k, c = pos_ref[1], pos_ref[2]

        def place(first, second):
            for core, ref in ((0, first), (1, second)):
                for rel in range(QUADS):
                    j = k ^ rel
                    at = pl.ds(pl.multiple_of(j * quarter, 8), quarter)
                    cols = 0
                    for out, width in zip(outs[:3], (inner, narrow, narrow)):
                        seg = width // depth
                        for s in range(depth):
                            to = (2 * s + core) * seg
                            out[at, to : to + seg] = ref[
                                rel, :quarter, cols : cols + seg
                            ].astype(F32)
                            cols += seg
                    at = pl.ds(pl.multiple_of(core * (rows // 2) + j * small, 8), small)
                    outs[3][at, :] = ref[rel, quarter:, :].astype(F32)

        @pl.when(c == 0)
        def _():
            place(a, b)

        @pl.when(c == 1)
        def _():
            place(b, a)

    return call(
        kernel,
        [
            shaped((rows, 2 * inner), F32),
            shaped((rows, 2 * narrow), F32),
            shaped((rows, 2 * narrow), F32),
            shaped((rows, 2 * inner), F32),
        ],
        pos,
        mine,
        other,
        in_specs=[SCALARS] + [WHOLE] * 2,
        out_specs=[WHOLE] * 4,
        us=6,
    )


def on_device(
    reps,
    depth,
    tokens,
    gain_attn,
    w_query,
    w_key,
    w_value,
    w_out,
    gain_ffn,
    w_gate,
    w_up,
    w_down,
    cotangent,
):
    links = Links(reps, depth)
    z = lax.axis_index("fsdp")
    r = lax.axis_index("rep")
    c = r % 2
    k = (r // 2) % QUADS
    pos = jnp.stack([z, k, c]).astype(jnp.int32)
    length = tokens.shape[0]
    rows = w_query.shape[0]
    quarter = rows // QUADS
    small = quarter // 2
    inner = D // 2
    narrow = inner // (HEADS // KV)

    def core_columns(weight):
        split = weight.reshape(rows, depth, 2, weight.shape[1] // (2 * depth))
        return lax.dynamic_index_in_dim(split, c, 2, keepdims=False).reshape(rows, -1)

    shard_qkv = jnp.concatenate([core_columns(i) for i in (w_query, w_key, w_value)], axis=1)
    shard_out = lax.dynamic_slice_in_dim(w_out, c * (rows // 2), rows // 2, 0)
    piece_qkv = lax.dynamic_slice_in_dim(shard_qkv, k * quarter, quarter, 0)
    piece_out = lax.dynamic_slice_in_dim(shard_out, k * small, small, 0)
    seg = w_gate.shape[1] // (depth * 2 * QUADS)
    d_rows = w_down.shape[0] // (2 * QUADS)

    def block_columns(weight):
        return jnp.concatenate(
            [
                lax.dynamic_slice_in_dim(weight, ((s * 2 + c) * QUADS + k) * seg, seg, 1)
                for s in range(depth)
            ],
            axis=1,
        )

    piece_gate, piece_up = block_columns(w_gate), block_columns(w_up)
    piece_down = lax.dynamic_slice_in_dim(w_down, (c * QUADS + k) * d_rows, d_rows, 0)

    gains = jnp.stack([gain_attn, gain_ffn])
    gains = jnp.stack([gains] + [links.shift(gains, by) for by in range(1, depth)])
    gains = jnp.take(gains, (z - jnp.arange(depth)) % depth, axis=0)
    g_one = gains[:, 0].reshape(1, -1).astype(F32)
    g_two = gains[:, 1].reshape(1, -1).astype(F32)
    token_pair = (tokens, links.swap(tokens, 1))
    d_pair = (cotangent, links.swap(cotangent, 1))
    turns = tables(length)

    piece = jnp.concatenate([piece_qkv, piece_out], axis=0)
    early = after(pos, g_one, g_two, token_pair[1], d_pair[1], *turns)
    got_attn = links.spread(early, piece, 224)
    got_gate = links.spread(pos, piece_gate, 3 * rows // 2)
    got_up = links.spread(pos, after(piece_up, got_attn.own), 3 * rows // 2)
    got_down = links.spread(pos, after(piece_down, got_gate.own), 3 * d_rows // 2)
    got_attn.to_plane()
    got_attn.to_corner()
    got_gate.to_plane()
    got_gate.to_corner()
    got_up.to_plane()
    got_up.to_corner()
    got_down.to_plane()

    n_one, q, key, value, wqkv = project(pos, token_pair, g_one, got_attn, shard_qkv, turns)
    mixed, lse = attend(q, key, value)
    ready = after(mixed, *got_gate.parts, got_up.remote)
    to_other, mine, wo = mix(pos, ready, got_attn, shard_out)
    hidden, n_two = residual_norm(tokens, mine, links.swap(to_other, 1), g_two)

    n_pair = (n_two, links.swap(n_two, 1))
    shards, gots = (w_gate, w_up, w_down), (got_gate, got_up, got_down)
    blocks = [None] * QUADS

    def block(rel, *earlier):
        return ffn_block(after(pos, *earlier), rel, n_pair, d_pair, shards, gots)

    blocks[1] = block(1)
    got_down.parts = [after(i, blocks[1][0]) for i in got_down.parts]
    got_down.to_corner()
    blocks[2] = block(2, blocks[1][0])
    wide = Summed(links, blocks[1][2:4], blocks[2][2:4])
    deep = Summed(links, blocks[1][4:6], blocks[2][4:6])
    blocks[3] = block(3, blocks[2][0])
    blocks[0] = block(0, blocks[3][0])
    wide.corner(*[after(i, blocks[0][0]) for i in blocks[3][2:4]])
    lefts = [b[1] for b in blocks]
    rights = [w for b in blocks for w in (b[6], b[7])]
    to_other = rows_product(lefts, rights, 1, True, BF, 13)
    mine = rows_product(lefts, rights, 0, True, F32, 13)
    deep.corner(*[after(i, mine) for i in blocks[3][4:6]])
    wide.add()
    wide.rest()
    received = links.swap(after(to_other, *wide.added), 1)
    d_hidden, grad_g_two, low = norm_back(mine, received, hidden, cotangent, g_two, 1)

    low_pair = low, links.swap(after(low, deep.from_x, deep.from_y), 1)
    deep.add()
    deep.rest()
    d_mixed, grad_out = mix_back(*low_pair, after(mixed, *deep.added), wo)
    d_qkv = attend_back(q, key, value, lse, d_mixed, turns)
    sums_wide = wide.own(*blocks[0][2:4], d_qkv)
    packs = attention_grads(pos, n_one, d_qkv, grad_out, depth, rows, 80)
    sums_deep = deep.own(*blocks[0][4:6], packs[0][0])
    small_sums = Summed(links, *packs[1:3])
    small_sums.corner(*packs[3])
    wide_x, wide_y = links.round(sums_wide, sums_wide)
    small_sums.add()
    small_sums.rest()
    sums_attn = small_sums.own(*packs[0], d_qkv)

    late = after(d_qkv, packs[0][0])
    to_other = rows_product([late], [wqkv], 1, True, BF, 7)
    mine = rows_product([late], [wqkv], 0, True, F32, 7)
    input_grad, grad_g_one = norm_back(
        mine, links.swap(to_other, 1), tokens, d_hidden, g_one, 0
    )
    acts, downs = [after(b[0], input_grad) for b in blocks], [b[8] for b in blocks]
    out_other = rows_product(acts, downs, 1, False, BF, 8)
    out_mine = rows_product(acts, downs, 0, False, F32, 8)
    result = (hidden + out_mine + links.swap(out_other, 1).astype(F32)).astype(BF)

    def stacked(own, along_x, along_y, corner):
        mine = jnp.stack([own, along_x, along_y, jnp.concatenate(corner, axis=0)])
        return mine, links.swap(mine, 1)

    wide_corner = links.round(wide_y[:rows], wide_x[rows:])
    deep_x, deep_y = links.round(sums_deep, sums_deep)
    deep_corner = links.round(deep_y[: d_rows // 2], deep_x[d_rows // 2 :])
    wide_pair = stacked(sums_wide, wide_x, wide_y, wide_corner)
    share_gate = unpack_columns(pos, *wide_pair, depth, 0)
    share_up = unpack_columns(pos, *wide_pair, depth, 1)
    share_down = unpack_rows(pos, *stacked(sums_deep, deep_x, deep_y, deep_corner))
    sums = jnp.concatenate([grad_g_one, grad_g_two], axis=0)
    for bit in (1, 2, 4):
        sums = sums + links.swap(sums, bit)
    sums = links.cells(sums)
    sums = sums.reshape(2, depth, rows)

    def own_part(at):
        return lax.dynamic_index_in_dim(sums, at % depth, 1, keepdims=False)

    gain_sums = own_part(z)
    for by in range(1, depth):
        gain_sums = gain_sums + links.shift(own_part(z + by), by)
    sums_attn = after(sums_attn, share_gate, share_up, share_down, result, gain_sums)
    attn_x, attn_y = links.round(sums_attn, sums_attn)
    attn_corner = links.round(attn_y[:80], attn_x[80:])
    share_q, share_k, share_v, share_out = unpack_attention(
        pos, *stacked(sums_attn, attn_x, attn_y, attn_corner), depth, rows, inner, narrow
    )

    return (
        result,
        input_grad,
        gain_sums[0],
        share_q,
        share_k,
        share_v,
        share_out,
        gain_sums[1],
        share_gate,
        share_up,
        share_down,
    )


def solution(mesh):
    tokens = P(("rep", "fsdp"), None)
    gain, weight = P("fsdp"), P("fsdp", None)
    return jax.shard_map(
        functools.partial(on_device, mesh.shape["rep"], mesh.shape["fsdp"]),
        mesh=mesh,
        in_specs=(tokens, gain, *[weight] * 4, gain, *[weight] * 3, tokens),
        out_specs=(tokens, tokens, gain, *[weight] * 4, gain, *[weight] * 3),
        check_vma=False,
    )
```

```python
import functools
import math

import jax
import jax.numpy as jnp
import numpy as np
from jax import lax
from jax.experimental import pallas as pl
from jax.experimental.pallas import tpu as pltpu
from jax.sharding import PartitionSpec as P

D = 1536
HEADS = 16
KV = 8
HD = 96
BF = jnp.bfloat16
F32 = jnp.float32
MiB = 1024 * 1024
ANY = pl.BlockSpec(memory_space=pl.ANY)
WHOLE = pl.BlockSpec(memory_space=pltpu.VMEM)
SCALARS = pl.BlockSpec(memory_space=pltpu.SMEM)
QUADS = 4
TILE = 256
SCALE = 1.0 / math.sqrt(HD)
PACE = 0.02


def after(value, *earlier):
    return lax.optimization_barrier((value, *earlier))[0]


def nt(a, b):
    return lax.dot_general(a, b, (((1,), (1,)), ((), ())), preferred_element_type=F32)


def tn(a, b):
    return lax.dot_general(a, b, (((0,), (0,)), ((), ())), preferred_element_type=F32)


def nn(a, b):
    return jnp.dot(a, b, preferred_element_type=F32)


def rms(values):
    return lax.rsqrt(jnp.mean(values * values, axis=-1, keepdims=True) + 1e-05)


def tile_at(i, size):
    return pl.ds(pl.multiple_of(i * size, size), size)


def call(
    kernel,
    out_shape,
    *args,
    scratch=(),
    vmem=48,
    grid=(),
    in_specs=None,
    out_specs=None,
    us=5,
    aliases=None,
):
    return pl.pallas_call(
        kernel,
        grid=grid,
        out_shape=out_shape,
        in_specs=in_specs,
        out_specs=out_specs,
        scratch_shapes=list(scratch),
        input_output_aliases=aliases or {},
        compiler_params=pltpu.CompilerParams(vmem_limit_bytes=vmem * MiB),
        cost_estimate=pl.CostEstimate(
            flops=int(us * PACE * 1.15e9), bytes_accessed=1024, transcendentals=0
        ),
    )(*args)


def shaped(shape, dtype=BF):
    return jax.ShapeDtypeStruct(shape, dtype)


class Links:
    def __init__(self, reps, depth):
        self.reps, self.depth = reps, depth
        self.rounds = [[], [], []]

    def swap(self, value, bit):
        return lax.ppermute(value, "rep", [(i, i ^ bit) for i in range(self.reps)])

    def round(self, *moves):
        earlier = self.rounds[-2] + self.rounds[-3]
        moved = [self.swap(after(value, *earlier), bit) for value, bit in moves]
        self.rounds.append(moved)
        return moved

    def both(self, along_x, along_y):
        return self.round((along_x, 2), (along_y, 4))

    def shift(self, value, by):
        return lax.ppermute(value, "fsdp", [(i, (i + by) % self.depth) for i in range(self.depth)])

    def over_depth(self, value):
        return self.cells(lax.psum_scatter(value, "fsdp", scatter_dimension=0, tiled=True)[0])

    def cells(self, value):
        if self.reps == 2 * QUADS:
            return value
        groups = [
            [cell * 2 * QUADS + i for cell in range(self.reps // (2 * QUADS))]
            for i in range(2 * QUADS)
        ]
        return lax.psum(value, "rep", axis_index_groups=groups)

    def spread(self, piece, cut):
        return Gathered(self, piece, cut)


class Summed:
    def __init__(self, own, send_x, send_y, high_x, low_y):
        self.own, self.kept = own, (high_x, low_y)
        self.first = (send_x, 2), (send_y, 4)

    def add(self, received, *earlier):
        self.received = received
        high_x, low_y = (after(i, *earlier) for i in self.kept)
        x_high = (high_x.astype(F32) + received[1][0].astype(F32)).astype(BF)
        y_low = (low_y.astype(F32) + received[0][0].astype(F32)).astype(BF)
        self.added = x_high, y_low
        self.second = (x_high, 2), (y_low, 4)

    def total(self, rest, *earlier):
        low, high = self.own
        depth, n, m = low.shape
        rows = n + high.shape[1]

        def kernel(a, b, c, d, e, f, out):
            out[:, :n] = (
                a[...].astype(F32) + b[0].astype(F32) + c[...].astype(F32)
            ).astype(BF)
            out[:, n:] = (
                d[...].astype(F32) + e[0].astype(F32) + f[...].astype(F32)
            ).astype(BF)

        def block(height):
            return pl.BlockSpec((1, height, m), lambda i: (i, 0, 0))

        def second(height):
            return pl.BlockSpec((1, 1, height, m), lambda i: (1, i, 0, 0))

        return call(
            kernel,
            shaped((depth, rows, m)),
            after(low, *earlier),
            self.received[0],
            rest[1],
            high,
            self.received[1],
            rest[0],
            grid=(depth,),
            in_specs=[
                block(n),
                second(n),
                block(n),
                block(rows - n),
                second(rows - n),
                block(rows - n),
            ],
            out_specs=block(rows),
            us=5,
        )


class Gathered:
    def __init__(self, links, piece, cut):
        self.rows, self.cut, self.depth = piece.shape[0], cut, links.depth
        n, m, depth = piece.shape[0], piece.shape[1], links.depth
        self.own = lax.all_gather(piece, "fsdp", axis=0, tiled=True)
        self.links, self.shape = links, (n, m)

    def compact(self, pos):
        (n, m), depth = self.shape, self.depth

        def kernel(pos_ref, in_ref, out_ref):
            out_ref[...] = in_ref[...]

        self.remote = pl.pallas_call(
            kernel,
            grid_spec=pltpu.PrefetchScalarGridSpec(
                num_scalar_prefetch=1,
                grid=(depth - 1,),
                in_specs=[pl.BlockSpec((n, m), lambda i, at: (lax.rem(at[0] + 1 + i, depth), 0))],
                out_specs=pl.BlockSpec((n, m), lambda i, at: (i, 0)),
            ),
            out_shape=shaped(((depth - 1) * n, m)),
            cost_estimate=pl.CostEstimate(
                flops=int(4 * PACE * 1.15e9), bytes_accessed=1024, transcendentals=0
            ),
        )(pos, self.own)

    def to_plane(self):
        self.x, self.y = self.links.both(self.remote, self.remote)
        self.parts = after(self.y[: self.cut], self.x), after(self.x[self.cut :], self.y)

    def to_corner(self):
        self.corner = self.links.both(*self.parts)

    def arrays(self, rel):
        return self.corner if rel == 3 else ((self.own, self.x, self.y)[rel],)

    def segments(self, rel, low, high):
        n = self.rows
        found = []
        for i in range(self.depth - 1):
            first, last = i * n + low, i * n + high
            if rel == 0:
                found.append((0, i, low, high - low, 0))
            elif rel < 3:
                found.append((0, i, first, high - low, 0))
            else:
                if first < self.cut:
                    found.append((0, i, first, min(last, self.cut) - first, 0))
                if last > self.cut:
                    begin = max(first, self.cut)
                    found.append((1, i, begin - self.cut, last - begin, begin - first))
        return found

    def copies(self, rel, refs, z, target, stride, base, low, high):
        out = []
        for which, i, row, count, offset in self.segments(rel, low, high):
            shard = lax.rem(z + 1 + i, self.depth)
            source = pl.multiple_of(shard * self.rows + row, 16) if rel == 0 else row
            at = pl.multiple_of(shard * stride + base + offset, 16)
            out.append((refs[which].at[pl.ds(source, count), :], target.at[pl.ds(at, count), :]))
        return out


def start(copies, sems, first=0):
    made = [
        pltpu.make_async_copy(source, target, sems.at[first + i])
        for i, (source, target) in enumerate(copies)
    ]
    for copy in made:
        copy.start()
    return made


def all_parts(got):
    return [array for rel in range(QUADS) for array in got.arrays(rel)]


def whole_copies(got, refs, z, k, target, stride, low, high):
    out, at = [], 0
    for rel in range(QUADS):
        size = len(got.arrays(rel))
        base = (k ^ rel) * (high - low)
        out += got.copies(rel, refs[at : at + size], z, target, stride, base, low, high)
        at += size
    return out


def n_copies(got, low, high, rels=range(QUADS)):
    return sum(len(got.segments(rel, low, high)) for rel in rels)


def tables(length):
    freq = 10000.0 ** (-np.arange(0, HD, 2) / HD)
    angle = np.arange(length)[:, None] * freq[None, :]
    cosine, sine = np.cos(angle), np.sin(angle)
    none = np.zeros_like(sine)

    def four(a, b):
        return jnp.asarray(np.concatenate([a, b] * 4, axis=1), F32)

    return four(cosine, cosine), four(-sine, none), four(none, sine)


def rotated(u, cosine, right, left, sign):
    width = u.shape[1]
    turned = pltpu.roll(u, width - HD // 2, 1) * right + pltpu.roll(u, HD // 2, 1) * left
    return u * cosine + sign * turned


def project(pos, pair, gain, got, shard, turns):
    length, width = pair[0].shape
    cols = shard.shape[1]
    rows = shard.shape[0]
    parts = all_parts(got)
    narrow = cols // 4
    high = rows // QUADS
    copies_in = 3 + n_copies(got, 0, high)

    def kernel(pos_ref, gain_ref, cos_ref, right_ref, left_ref, ta, tb, shard_ref, *refs):
        part_refs = refs[: len(parts)]
        normed, q, key, value, weight, toks, sems = refs[len(parts) :]
        z, k = pos_ref[0], pos_ref[1]
        first = start(
            [(ta, toks.at[pl.ds(0, length), :]), (tb, toks.at[pl.ds(length, length), :])], sems
        )
        second = start(
            [(shard_ref, weight.at[pl.ds(pl.multiple_of(z * rows, 16), rows), :])]
            + whole_copies(got, part_refs, z, k, weight, rows, 0, high),
            sems,
            2,
        )
        for copy in first:
            copy.wait()

        def norm(i, _):
            at = tile_at(i, TILE)
            x = toks[at, :].astype(F32)
            normed[at, :] = (x * rms(x) * gain_ref[...]).astype(BF)
            return 0

        lax.fori_loop(0, 2 * length // TILE, norm, 0)
        for copy in second:
            copy.wait()

        def body(i, _):
            at = tile_at(i, TILE)
            place = tile_at(lax.rem(i, length // TILE), TILE)
            out = nn(normed[at, :], weight[...])
            cosine, right, left = cos_ref[place, :], right_ref[place, :], left_ref[place, :]
            for t in range(2):
                u = out[:, t * narrow : (t + 1) * narrow]
                q[at, t * narrow : (t + 1) * narrow] = rotated(
                    u, cosine, right, left, 1.0
                ).astype(BF)
            key[at, :] = rotated(
                out[:, 2 * narrow : 3 * narrow], cosine, right, left, 1.0
            ).astype(BF)
            value[at, :] = out[:, 3 * narrow :].astype(BF)
            return 0

        lax.fori_loop(0, 2 * length // TILE, body, 0)

    return call(
        kernel,
        [
            shaped((2 * length, width)),
            shaped((2 * length, 2 * narrow)),
            shaped((2 * length, narrow)),
            shaped((2 * length, narrow)),
            shaped((width, cols)),
        ],
        pos,
        gain,
        *turns,
        *pair,
        shard,
        *parts,
        in_specs=[SCALARS] + [WHOLE] * 4 + [ANY] * (3 + len(parts)),
        out_specs=[WHOLE] * 5,
        scratch=[pltpu.VMEM((2 * length, width), BF), pltpu.SemaphoreType.DMA((copies_in,))],
        us=13,
    )


def masked(scores, first):
    keys = lax.broadcasted_iota(jnp.int32, scores.shape, 0)
    queries = lax.broadcasted_iota(jnp.int32, scores.shape, 1) + first
    return jnp.where(keys <= queries, scores, -1e30)


def attend(q, key, value):
    length = q.shape[0] // 2
    heads, groups = q.shape[1] // HD, key.shape[1] // HD

    def kernel(q_ref, k_ref, v_ref, o_ref, lse_ref):
        for g in range(groups):
            keys = k_ref[:, g * HD : (g + 1) * HD]
            turned = v_ref[:, g * HD : (g + 1) * HD].T
            for j in range(g * heads // groups, (g + 1) * heads // groups):
                for t in range(length // TILE):
                    at = slice(t * TILE, (t + 1) * TILE)
                    reach = (t + 1) * TILE
                    s = nt(keys[:reach], q_ref[at, j * HD : (j + 1) * HD]) * SCALE
                    s = masked(s, t * TILE)
                    peak = jnp.max(s, axis=0, keepdims=True)
                    e = jnp.exp(s - peak)
                    total = jnp.sum(e, axis=0, keepdims=True)
                    lse = peak + jnp.log(total)
                    p = (e * (1.0 / total)).astype(BF)
                    lse_ref[0, j : j + 1, at] = lse
                    o_ref[at, j * HD : (j + 1) * HD] = nn(turned[:, :reach], p).T.astype(BF)

    return call(
        kernel,
        [shaped(q.shape), shaped((2, heads, length), F32)],
        q,
        key,
        value,
        grid=(2,),
        in_specs=[
            pl.BlockSpec((length, q.shape[1]), lambda i: (i, 0)),
            pl.BlockSpec((length, key.shape[1]), lambda i: (i, 0)),
            pl.BlockSpec((length, key.shape[1]), lambda i: (i, 0)),
        ],
        out_specs=[
            pl.BlockSpec((length, q.shape[1]), lambda i: (i, 0)),
            pl.BlockSpec((1, heads, length), lambda i: (i, 0, 0)),
        ],
        us=10,
    )


def attend_back(q, key, value, lse, d_mixed, turns):
    length = q.shape[0] // 2
    heads, groups = q.shape[1] // HD, key.shape[1] // HD
    inner, narrow = q.shape[1], key.shape[1]

    def kernel(q_ref, k_ref, v_ref, lse_ref, do_ref, cos_ref, right_ref, left_ref, out, dq, dk):
        for g in range(groups):
            keys = k_ref[:, g * HD : (g + 1) * HD]
            values = v_ref[:, g * HD : (g + 1) * HD]
            turned = keys.T
            d_key = [jnp.zeros((TILE, HD), F32) for _ in range(length // TILE)]
            d_value = [jnp.zeros((TILE, HD), F32) for _ in range(length // TILE)]
            for j in range(g * heads // groups, (g + 1) * heads // groups):
                for t in range(length // TILE):
                    at = slice(t * TILE, (t + 1) * TILE)
                    reach = (t + 1) * TILE
                    queries = q_ref[at, j * HD : (j + 1) * HD]
                    upstream = do_ref[at, j * HD : (j + 1) * HD]
                    s = masked(nt(keys[:reach], queries) * SCALE, t * TILE)
                    p = jnp.exp(s - lse_ref[0, j : j + 1, at])
                    dp = nt(values[:reach], upstream)
                    centre = jnp.sum(p * dp, axis=0, keepdims=True)
                    ds = (p * (dp - centre)).astype(BF)
                    from_values = nn(p.astype(BF), upstream)
                    from_keys = nn(ds, queries)
                    for i in range(t + 1):
                        rows = slice(i * TILE, (i + 1) * TILE)
                        d_value[i] = d_value[i] + from_values[rows]
                        d_key[i] = d_key[i] + from_keys[rows]
                    dq[at, j * HD : (j + 1) * HD] = nn(turned[:, :reach], ds).T * SCALE
            for i in range(length // TILE):
                rows = slice(i * TILE, (i + 1) * TILE)
                dk[rows, g * HD : (g + 1) * HD] = d_key[i] * SCALE
                first = inner + narrow + g * HD
                out[rows, first : first + HD] = d_value[i].astype(BF)
        cosine, right, left = cos_ref[...], right_ref[...], left_ref[...]
        for t in range(inner // narrow):
            cols = slice(t * narrow, (t + 1) * narrow)
            out[:, cols] = rotated(dq[:, cols], cosine, right, left, -1.0).astype(BF)
        out[:, inner : inner + narrow] = rotated(dk[...], cosine, right, left, -1.0).astype(BF)

    def block(cols):
        return pl.BlockSpec((length, cols), lambda i: (i, 0))

    table = pl.BlockSpec(turns[0].shape, lambda i: (0, 0))
    return call(
        kernel,
        shaped((2 * length, inner + 2 * narrow)),
        q,
        key,
        value,
        lse,
        d_mixed,
        *turns,
        grid=(2,),
        in_specs=[
            block(inner),
            block(narrow),
            block(narrow),
            pl.BlockSpec((1, heads, length), lambda i: (i, 0, 0)),
            block(inner),
            table,
            table,
            table,
        ],
        out_specs=block(inner + 2 * narrow),
        scratch=[pltpu.VMEM((length, inner), F32), pltpu.VMEM((length, narrow), F32)],
        us=17,
    )


def mix(pos, mixed, got, shard):
    tokens, inner = mixed.shape
    width = shard.shape[1]
    rows = shard.shape[0]
    high = got.rows
    low = high - rows // QUADS
    parts = all_parts(got)

    def kernel(pos_ref, mixed_ref, shard_ref, *refs):
        part_refs = refs[: len(parts)]
        other, mine, weight, sems = refs[len(parts) :]
        z, k = pos_ref[0], pos_ref[1]
        copies = start(
            [(shard_ref, weight.at[pl.ds(pl.multiple_of(z * rows, 16), rows), :])]
            + whole_copies(got, part_refs, z, k, weight, rows, low, high),
            sems,
        )
        for copy in copies:
            copy.wait()
        for i in range(tokens // 2 // TILE):
            at = slice(i * TILE, (i + 1) * TILE)
            there = slice(tokens // 2 + i * TILE, tokens // 2 + (i + 1) * TILE)
            other[at, :] = nn(mixed_ref[there, :], weight[...]).astype(BF)
            mine[at, :] = nn(mixed_ref[at, :], weight[...])

    return call(
        kernel,
        [
            shaped((tokens // 2, width)),
            shaped((tokens // 2, width), F32),
            shaped((inner, width)),
        ],
        pos,
        mixed,
        shard,
        *parts,
        in_specs=[SCALARS, WHOLE] + [ANY] * (1 + len(parts)),
        out_specs=[WHOLE] * 3,
        scratch=[pltpu.SemaphoreType.DMA((1 + n_copies(got, low, high),))],
        us=8,
    )


def residual_norm(tokens, mine, received, gain):
    length, width = tokens.shape

    def kernel(x, a, b, gain_ref, hidden, normed):
        h = x[...].astype(F32) + a[...] + b[...].astype(F32)
        hidden[...] = h
        normed[...] = (h * rms(h) * gain_ref[...]).astype(BF)

    block = pl.BlockSpec((TILE, width), lambda i: (i, 0))
    return call(
        kernel,
        [shaped((length, width), F32), shaped((length, width))],
        tokens,
        mine,
        received,
        gain,
        grid=(length // TILE,),
        in_specs=[block, block, block, pl.BlockSpec((1, width), lambda i: (0, 0))],
        out_specs=[block, block],
        us=4,
    )


def norm_back(mine, received, values, residual, gain, rounded):
    length, width = values.shape

    def kernel(a, b, values_ref, residual_ref, gain_ref, grad, gain_grad, *low):
        x = values_ref[...].astype(F32)
        factor = rms(x)
        normed = x * factor
        upstream = a[...] + b[...].astype(F32)
        part = jnp.sum(upstream * normed, axis=0, keepdims=True)

        @pl.when(pl.program_id(0) == 0)
        def _():
            gain_grad[...] = part

        @pl.when(pl.program_id(0) > 0)
        def _():
            gain_grad[...] += part

        scaled = upstream * gain_ref[...]
        inside = scaled - normed * jnp.mean(scaled * normed, axis=-1, keepdims=True)
        total = residual_ref[...].astype(F32) + factor * inside
        grad[...] = total
        if low:
            low[0][...] = total.astype(BF)

    block = pl.BlockSpec((TILE, width), lambda i: (i, 0))
    line = pl.BlockSpec((1, width), lambda i: (0, 0))
    return call(
        kernel,
        [shaped((length, width), F32), shaped((1, width), F32)]
        + [shaped((length, width))] * rounded,
        mine,
        received,
        values,
        residual,
        gain,
        grid=(length // TILE,),
        in_specs=[block] * 4 + [line],
        out_specs=[block, line] + [block] * rounded,
        us=5,
    )


def weight_copies(pos_ref, rel, got, refs, shard_ref, target):
    z, k, c = pos_ref[0], pos_ref[1], pos_ref[2]
    if rel == 0:
        return [(refs[0], target)]
    depth, rows = got.depth, got.rows
    j = k ^ rel
    at = pl.ds(pl.multiple_of(z * rows, 16), rows)
    if shard_ref.shape[0] == rows:
        seg = target.shape[1] // depth
        copies = []
        for s in range(depth):
            col = pl.multiple_of(((s * 2 + c) * QUADS + j) * seg, 128)
            copies.append(
                (shard_ref.at[:, pl.ds(col, seg)], target.at[at, pl.ds(s * seg, seg)])
            )
    else:
        row = pl.multiple_of((c * QUADS + j) * rows, 16)
        copies = [(shard_ref.at[pl.ds(row, rows), :], target.at[at, :])]
    return copies + got.copies(rel, refs, z, target, rows, 0, 0, rows)


def count_copies(rel, got, columns):
    return 1 if rel == 0 else (got.depth if columns else 1) + n_copies(got, 0, got.rows, [rel])


class Weights:
    def __init__(self, shards, gots, columns, rels=range(QUADS)):
        self.shards, self.gots, self.columns, self.rels = shards, gots, columns, rels
        self.operands = list(shards)
        self.places = {}
        for i, got in enumerate(gots):
            for rel in rels:
                arrays = got.arrays(rel)
                self.places[i, rel] = (len(self.operands), len(arrays))
                self.operands += arrays
        self.total = sum(
            count_copies(rel, got, col) for got, col in zip(gots, columns) for rel in rels
        )
        self.scratch = [pltpu.VMEM((len(rels), *got.own.shape), BF) for got in gots]

    def start(self, pos_ref, refs, targets, sems, first):
        begun = []
        for slot, rel in enumerate(self.rels):
            copies = []
            for i, got in enumerate(self.gots):
                at, count = self.places[i, rel]
                copies += weight_copies(
                    pos_ref, rel, got, refs[at : at + count], refs[i], targets[i].at[slot]
                )
            begun.append(start(copies, sems, first))
            first += len(copies)
        return begun


def wait(copies):
    for copy in copies:
        copy.wait()


def ffn_forward(pos, rels, n_two, d_out, shards, gots, deep):
    weights = Weights(shards, gots, (True, True, False), rels)
    length, width = n_two[0].shape
    tokens = 2 * length
    cols = gots[0].own.shape[1]
    depth, rows = gots[2].depth, gots[2].rows
    given = [] if deep is None else [deep]
    count = len(weights.operands)
    n = len(rels)
    tile = 2 * TILE

    def kernel(pos_ref, na, nb, ya, yb, *refs):
        operands, refs = refs[:count], refs[count + len(given) :]
        acts, dgus, grads = refs[:n], refs[n : 2 * n], refs[2 * n]
        n_all, y_all, w_gate, w_up, w_down, act, dgu, made, sems = refs[2 * n + 1 :]
        first = start(
            [
                (na, n_all.at[pl.ds(0, length), :]),
                (nb, n_all.at[pl.ds(length, length), :]),
                (ya, y_all.at[pl.ds(0, length), :]),
                (yb, y_all.at[pl.ds(length, length), :]),
            ],
            sems,
        )
        begun = weights.start(pos_ref, operands, (w_gate, w_up, w_down), sems, 4)
        wait(first)
        written = []
        for slot, rel in enumerate(rels):
            wait(begun[slot])

            def body(i, _, slot=slot):
                at = tile_at(i, tile)
                normed, grad = n_all[at, :], y_all[at, :]
                gated = nn(normed, w_gate[slot])
                upper = nn(normed, w_up[slot])
                d_act = nt(grad, w_down[slot])
                sig = 1.0 / (1.0 + jnp.exp(-gated))
                silu = gated * sig
                act[slot, at, :] = (silu * upper).astype(BF)
                dgu[slot, at, :cols] = (
                    d_act * upper * sig * (1.0 + gated * (1.0 - sig))
                ).astype(BF)
                dgu[slot, at, cols:] = (d_act * silu).astype(BF)
                return 0

            lax.fori_loop(0, tokens // tile, body, 0)
            at = 4 + weights.total + 3 * slot
            written += start([(act.at[slot], acts[slot]), (dgu.at[slot], dgus[slot])], sems, at)

            def grad(s, _, slot=slot):
                made[slot, s] = tn(act[slot, :, tile_at(s, rows)], y_all[...]).astype(BF)
                return 0

            lax.fori_loop(0, depth, grad, 0)
            written += start([(made.at[slot], grads.at[:, rel])], sems, at + 2)
        wait(written)

    made = call(
        kernel,
        [shaped((tokens, cols))] * n
        + [shaped((tokens, 2 * cols))] * n
        + [shaped((depth, QUADS, rows, width))],
        pos,
        *n_two,
        *d_out,
        *weights.operands,
        *given,
        in_specs=[SCALARS] + [ANY] * (4 + count + len(given)),
        out_specs=[ANY] * (2 * n + 1),
        scratch=[
            pltpu.VMEM((tokens, width), BF),
            pltpu.VMEM((tokens, width), BF),
            *weights.scratch,
            pltpu.VMEM((n, tokens, cols), BF),
            pltpu.VMEM((n, tokens, 2 * cols), BF),
            pltpu.VMEM((n, depth, rows, width), BF),
            pltpu.SemaphoreType.DMA((4 + weights.total + 3 * n,)),
        ],
        vmem=56,
        us=3 + 9 * n,
        aliases={5 + count: 2 * n} if given else None,
    )
    return made[:n], made[n : 2 * n], made[2 * n]


def ffn_grads(n_two, dgus, depth):
    length, width = n_two[0].shape
    tokens = 2 * length
    rows = width // depth
    cols = dgus[0].shape[1] // 2

    def kernel(na, nb, *refs):
        ins, outs, refs = refs[:QUADS], refs[QUADS : QUADS + 6], refs[QUADS + 6 :]
        own_gate, own_up, send_x, send_y, x_up, y_gate = outs
        places = [
            (own_gate, own_up),
            (send_x.at[1], x_up),
            (y_gate, send_y.at[1]),
            (send_x.at[0], send_y.at[0]),
        ]
        n_all, dgu, turned, made, sems = refs
        first = start(
            [
                (na, n_all.at[pl.ds(0, length), :]),
                (nb, n_all.at[pl.ds(length, length), :]),
                *[(ins[rel], dgu.at[rel]) for rel in range(QUADS)],
            ],
            sems,
        )
        wait(first[:2])
        for s in range(depth):
            at = slice(s * rows, (s + 1) * rows)
            turned[at, :] = n_all[:, at].T
        written = [[], []]
        for rel in (3, 1, 2, 0):
            first[2 + rel].wait()
            for part in range(2):
                wait(written[part])
                grads = nn(turned[...], dgu[rel, :, part * cols : (part + 1) * cols])
                for s in range(depth):
                    made[part, s] = grads[s * rows : (s + 1) * rows].astype(BF)
                written[part] = start(
                    [(made.at[part], places[rel][part])], sems, 2 + QUADS + part
                )
        wait(written[0] + written[1])

    made = call(
        kernel,
        [shaped((depth, rows, cols))] * 2
        + [shaped((2, depth, rows, cols))] * 2
        + [shaped((depth, rows, cols))] * 2,
        *n_two,
        *dgus,
        in_specs=[ANY] * (2 + QUADS),
        out_specs=[ANY] * 6,
        scratch=[
            pltpu.VMEM((tokens, width), BF),
            pltpu.VMEM((QUADS, tokens, 2 * cols), BF),
            pltpu.VMEM((width, tokens), BF),
            pltpu.VMEM((2, depth, rows, cols), BF),
            pltpu.SemaphoreType.DMA((4 + QUADS,)),
        ],
        us=16,
    )
    return Summed(made[:2], *made[2:])


def ffn_product(pos, lefts, shards, gots, transposed):
    weights = Weights(shards, gots, (transposed,) * len(gots))
    tokens = lefts[0].shape[0]
    half = tokens // 2
    cols = lefts[0].shape[1] // len(gots)
    width = gots[0].own.shape[0] if transposed else gots[0].own.shape[1]
    count = len(weights.operands)

    def kernel(pos_ref, *refs):
        ins, operands, refs = refs[:QUADS], refs[QUADS : QUADS + count], refs[QUADS + count :]
        other, mine, refs = refs[0], refs[1], refs[2:]
        targets, (left, total, sems) = refs[: len(gots)], refs[len(gots) :]
        first = start([(ins[rel], left.at[rel]) for rel in range(QUADS)], sems)
        begun = weights.start(pos_ref, operands, targets, sems, QUADS)
        for rel in range(QUADS):
            first[rel].wait()
            wait(begun[rel])

            def body(i, _, rel=rel):
                at = tile_at(i, 2 * TILE)
                part = None if rel == 0 else total[at, :]
                for n, target in enumerate(targets):
                    term = (nt if transposed else nn)(
                        left[rel, at, n * cols : (n + 1) * cols], target[rel]
                    )
                    part = term if part is None else part + term
                total[at, :] = part
                return 0

            lax.fori_loop(0, tokens // (2 * TILE), body, 0)
        other[...] = total[half:, :].astype(BF)
        mine[...] = total[:half, :]

    return call(
        kernel,
        [shaped((half, width)), shaped((half, width), F32)],
        pos,
        *lefts,
        *weights.operands,
        in_specs=[SCALARS] + [ANY] * (QUADS + count),
        out_specs=[WHOLE] * 2,
        scratch=[
            *weights.scratch,
            pltpu.VMEM((QUADS, tokens, len(gots) * cols), BF),
            pltpu.VMEM((tokens, width), F32),
            pltpu.SemaphoreType.DMA((QUADS + weights.total,)),
        ],
        vmem=56,
        us=20,
    )


def rows_product(lefts, rights, half, transposed, dtype, us):
    rows = lefts[0].shape[0] // 2
    per = len(rights) // len(lefts)
    width = rights[0].shape[0] if transposed else rights[0].shape[1]
    depth = rights[0].shape[1] if transposed else rights[0].shape[0]
    steps = rows // TILE

    def kernel(*refs):
        left, right, out = refs[: len(lefts)], refs[len(lefts) : -1], refs[-1]
        total = None
        for i, ref in enumerate(right):
            part = left[i // per][:, (i % per) * depth : (i % per + 1) * depth]
            term = (nt if transposed else nn)(part, ref[...])
            total = term if total is None else total + term
        out[...] = total.astype(dtype)

    return call(
        kernel,
        shaped((rows, width), dtype),
        *lefts,
        *rights,
        grid=(steps,),
        in_specs=[
            pl.BlockSpec((TILE, left.shape[1]), lambda i: (i + half * steps, 0)) for left in lefts
        ]
        + [pl.BlockSpec(right.shape, lambda i: (0, 0)) for right in rights],
        out_specs=pl.BlockSpec((TILE, width), lambda i: (i, 0)),
        vmem=56,
        us=us,
    )


def mix_back(low, other, mixed, weight):
    length, width = low.shape
    inner = mixed.shape[1]

    def kernel(a, b, mixed_ref, weight_ref, d_mixed, grad):
        for i in range(2 * length // TILE):
            at = slice(i * TILE, (i + 1) * TILE)
            part = a if i < length // TILE else b
            first = i * TILE % length
            d_mixed[at, :] = nt(part[first : first + TILE, :], weight_ref[...]).astype(BF)

        def body(i, _):
            at = tile_at(i, TILE)
            grad[at, :] = (
                tn(mixed_ref[:length, at], a[...]) + tn(mixed_ref[length:, at], b[...])
            ).astype(BF)
            return 0

        lax.fori_loop(0, inner // TILE, body, 0)

    return call(
        kernel,
        [shaped((2 * length, inner)), shaped((inner, width))],
        low,
        other,
        mixed,
        weight,
        in_specs=[WHOLE] * 4,
        out_specs=[WHOLE] * 2,
        us=10,
    )


def attention_grads(pos, normed, d_qkv, grad_out, depth, rows, low):
    width, cols = normed.shape[1], d_qkv.shape[1]
    quarter = rows // QUADS
    small = quarter // 2
    high = quarter - low + small

    def kernel(pos_ref, normed_ref, d_ref, out_ref, *refs):
        own_low, own_high, send_x, send_y, x_high, y_low, tile = refs
        places = [
            (own_low, own_high),
            (send_x.at[1], x_high),
            (y_low, send_y.at[1]),
            (send_x.at[0], send_y.at[0]),
        ]
        k = pos_ref[1]

        def body(s, _):
            tile[...] = tn(normed_ref[:, tile_at(s, rows)], d_ref[...]).astype(BF)
            for rel in range(QUADS):
                j = k ^ rel
                first = pl.multiple_of(j * quarter, 16)
                to_low, to_high = places[rel]
                to_low[s] = tile[pl.ds(first, low), :]
                to_high[s, : quarter - low] = tile[pl.ds(first + low, quarter - low), :]
                at = pl.multiple_of(s * (rows // 2) + j * small, 16)
                to_high[s, quarter - low :] = out_ref[pl.ds(at, small), :]
            return 0

        lax.fori_loop(0, depth, body, 0)

    def part(n):
        return shaped((depth, n, cols))

    made = call(
        kernel,
        [
            part(low),
            part(high),
            shaped((2, depth, low, cols)),
            shaped((2, depth, high, cols)),
            part(high),
            part(low),
        ],
        pos,
        normed,
        d_qkv,
        grad_out,
        in_specs=[SCALARS] + [WHOLE] * 3,
        out_specs=[WHOLE] * 6,
        scratch=[pltpu.VMEM((rows, cols), BF)],
        us=10,
    )
    return Summed(made[:2], *made[2:])


def unpack_columns(pos, mine, other, depth, half):
    cols = mine.shape[2]
    rows = D // depth
    seg = cols // depth
    width = cols * 2 * QUADS
    tile = 128
    steps = rows // tile

    def kernel(pos_ref, a, b, out):
        k, c = pos_ref[1], pos_ref[2]
        for ref, core in ((a, c), (b, 1 - c)):
            for rel in range(QUADS):
                block = core * QUADS + (k ^ rel)
                for s in range(depth):
                    at = pl.multiple_of((s * 2 * QUADS + block) * seg, 128)
                    out[:, pl.ds(at, seg)] = ref[rel, :, s * seg : (s + 1) * seg].astype(F32)

    spec = pl.BlockSpec((QUADS, tile, cols), lambda i: (0, i + half * steps, 0))
    return call(
        kernel,
        shaped((rows, width), F32),
        pos,
        mine,
        other,
        grid=(steps,),
        in_specs=[SCALARS, spec, spec],
        out_specs=pl.BlockSpec((tile, width), lambda i: (i, 0)),
        us=4,
    )


def unpack_rows(pos, mine, other, rows, width, first):
    tile = mine.shape[2]

    def kernel(pos_ref, a, b, out):
        k, c = pos_ref[1], pos_ref[2]
        for ref, core in ((a, c), (b, 1 - c)):
            for rel in range(QUADS):
                at = pl.multiple_of((core * QUADS + (k ^ rel)) * rows, 8)
                out[pl.ds(at, rows), :] = ref[rel].astype(F32)

    spec = pl.BlockSpec((QUADS, rows, tile), lambda i: (0, first // rows + i, 0))
    return call(
        kernel,
        shaped((2 * QUADS * rows, width), F32),
        pos,
        mine,
        other,
        grid=(width // tile,),
        in_specs=[SCALARS, spec, spec],
        out_specs=pl.BlockSpec((2 * QUADS * rows, tile), lambda i: (0, i)),
        us=5,
    )


def unpack_attention(pos, mine, other, depth, rows, inner, narrow):
    quarter = rows // QUADS
    small = quarter // 2

    def kernel(pos_ref, a, b, *outs):
        k, c = pos_ref[1], pos_ref[2]

        def place(first, second):
            for core, ref in ((0, first), (1, second)):
                for rel in range(QUADS):
                    j = k ^ rel
                    at = pl.ds(pl.multiple_of(j * quarter, 8), quarter)
                    cols = 0
                    for out, width in zip(outs[:3], (inner, narrow, narrow)):
                        seg = width // depth
                        for s in range(depth):
                            to = (2 * s + core) * seg
                            out[at, to : to + seg] = ref[
                                rel, :quarter, cols : cols + seg
                            ].astype(F32)
                            cols += seg
                    at = pl.ds(pl.multiple_of(core * (rows // 2) + j * small, 8), small)
                    outs[3][at, :] = ref[rel, quarter:, :].astype(F32)

        @pl.when(c == 0)
        def _():
            place(a, b)

        @pl.when(c == 1)
        def _():
            place(b, a)

    return call(
        kernel,
        [
            shaped((rows, 2 * inner), F32),
            shaped((rows, 2 * narrow), F32),
            shaped((rows, 2 * narrow), F32),
            shaped((rows, 2 * inner), F32),
        ],
        pos,
        mine,
        other,
        in_specs=[SCALARS] + [WHOLE] * 2,
        out_specs=[WHOLE] * 4,
        us=6,
    )


def on_device(
    reps,
    depth,
    tokens,
    gain_attn,
    w_query,
    w_key,
    w_value,
    w_out,
    gain_ffn,
    w_gate,
    w_up,
    w_down,
    cotangent,
):
    links = Links(reps, depth)
    z = lax.axis_index("fsdp")
    r = lax.axis_index("rep")
    c = r % 2
    k = (r // 2) % QUADS
    pos = jnp.stack([z, k, c]).astype(jnp.int32)
    length = tokens.shape[0]
    rows = w_query.shape[0]
    quarter = rows // QUADS
    small = quarter // 2
    inner = D // 2
    narrow = inner // (HEADS // KV)

    def core_columns(weight):
        split = weight.reshape(rows, depth, 2, weight.shape[1] // (2 * depth))
        return lax.dynamic_index_in_dim(split, c, 2, keepdims=False).reshape(rows, -1)

    shard_qkv = jnp.concatenate([core_columns(i) for i in (w_query, w_key, w_value)], axis=1)
    shard_out = lax.dynamic_slice_in_dim(w_out, c * (rows // 2), rows // 2, 0)
    piece_qkv = lax.dynamic_slice_in_dim(shard_qkv, k * quarter, quarter, 0)
    piece_out = lax.dynamic_slice_in_dim(shard_out, k * small, small, 0)
    seg = w_gate.shape[1] // (depth * 2 * QUADS)
    d_rows = w_down.shape[0] // (2 * QUADS)

    def block_columns(weight):
        return jnp.concatenate(
            [
                lax.dynamic_slice_in_dim(weight, ((s * 2 + c) * QUADS + k) * seg, seg, 1)
                for s in range(depth)
            ],
            axis=1,
        )

    piece_gate, piece_up = block_columns(w_gate), block_columns(w_up)
    piece_down = lax.dynamic_slice_in_dim(w_down, (c * QUADS + k) * d_rows, d_rows, 0)

    gains = jnp.stack([gain_attn, gain_ffn])
    gains = jnp.stack([gains] + [links.shift(gains, by) for by in range(1, depth)])
    gains = jnp.take(gains, (z - jnp.arange(depth)) % depth, axis=0)
    g_one = gains[:, 0].reshape(1, -1).astype(F32)
    g_two = gains[:, 1].reshape(1, -1).astype(F32)
    token_pair = (tokens, links.swap(tokens, 1))
    d_pair = (cotangent, links.swap(cotangent, 1))
    turns = tables(length)

    piece = jnp.concatenate([piece_qkv, piece_out], axis=0)
    early = after(pos, g_one, g_two, token_pair[1], d_pair[1])
    got_attn = links.spread(piece, 224)
    got_gate = links.spread(piece_gate, 3 * rows // 2)
    got_up = links.spread(after(piece_up, got_attn.own), 3 * rows // 2)
    got_down = links.spread(after(piece_down, got_gate.own), 3 * d_rows // 2)
    got_attn.compact(early)
    got_attn.to_plane()
    got_gate.compact(pos)
    got_gate.to_plane()
    got_attn.to_corner()
    got_up.compact(pos)
    got_up.to_plane()
    got_gate.parts = [after(i, got_up.remote) for i in got_gate.parts]
    got_gate.to_corner()

    ready = after(pos, got_up.remote)
    n_one, q, key, value, wqkv = project(ready, token_pair, g_one, got_attn, shard_qkv, turns)
    mixed, lse = attend(q, key, value)
    got_down.compact(after(pos, lse))
    got_down.to_plane()
    got_up.to_corner()
    got_down.to_corner()
    to_other, mine, wo = mix(pos, mixed, got_attn, shard_out)
    ready = after(to_other, *got_gate.corner, got_up.x, got_up.y, got_down.remote)
    hidden, n_two = residual_norm(tokens, mine, links.swap(ready, 1), g_two)

    n_pair = (n_two, links.swap(n_two, 1))
    shards, gots = (w_gate, w_up, w_down), (got_gate, got_up, got_down)
    acts, dgus, deep = [], [], None
    for rels in ((0, 1, 2), (3,)):
        at = after(pos, dgus[-1]) if dgus else pos
        act, dgu, deep = ffn_forward(at, rels, n_pair, d_pair, shards, gots, deep)
        acts += act
        dgus += dgu
    deep_sum = links.over_depth(deep)
    half = d_rows // 2
    wide = ffn_grads(n_pair, dgus, depth)
    wide_first = links.round(*wide.first)
    lefts = [after(i, wide.own[0]) for i in dgus]
    to_other, mine = ffn_product(pos, lefts, (w_gate, w_up), (got_gate, got_up), True)
    acts = [after(i, to_other) for i in acts]
    out_other, out_mine = ffn_product(pos, acts, (w_down,), (got_down,), False)
    received = links.swap(to_other, 1)
    mine = after(mine, out_mine, *wide_first)
    d_hidden, grad_g_two, low = norm_back(mine, received, hidden, cotangent, g_two, 1)

    wide.add(wide_first)
    low_pair = low, links.swap(after(low, *wide.added), 1)
    wide_second = links.round(*wide.second)
    d_mixed, grad_out = mix_back(*low_pair, mixed, wo)
    d_qkv = attend_back(q, key, value, lse, d_mixed, turns)
    deep = Summed(
        [deep_sum[0, :half][None], deep_sum[0, half:][None]],
        jnp.stack([deep_sum[3, :half][None], deep_sum[1, :half][None]]),
        jnp.stack([deep_sum[3, half:][None], deep_sum[2, half:][None]]),
        deep_sum[1, half:][None],
        deep_sum[2, :half][None],
    )
    ready = after(pos, deep.first[0][0], deep.first[1][0])
    deep_first = links.both(deep.first[0][0], deep.first[1][0])
    small = attention_grads(ready, n_one, d_qkv, grad_out, depth, rows, 80)
    deep.add(deep_first)
    deep_second = links.round(*deep.second)
    small_first = links.round(*small.first)
    sums_wide = wide.total(wide_second, small.own[0], *deep.added)
    late = after(d_qkv, sums_wide)
    sums_wide = links.over_depth(sums_wide)
    to_other = rows_product([late], [wqkv], 1, True, BF, 7)
    mine = rows_product([late], [wqkv], 0, True, F32, 7)
    out_received = links.swap(after(out_other, d_hidden), 1)
    result = (hidden + out_mine + out_received.astype(F32)).astype(BF)
    small.add(small_first)
    small_second = links.round(*small.second)
    sums_attn = small.total(small_second)
    sums_deep = deep.total(deep_second)[0]
    split = sums_deep.shape[1] // sums_wide.shape[1]
    sums_ffn = jnp.concatenate([sums_wide, *jnp.split(sums_deep, split, axis=1)], axis=0)
    ffn_x, ffn_y = links.both(*[after(sums_ffn, sums_attn)] * 2)
    received = links.swap(after(to_other, mine, result, ffn_x, ffn_y), 1)
    input_grad, grad_g_one = norm_back(mine, received, tokens, d_hidden, g_one, 0)
    gain_sums = jnp.concatenate([grad_g_one, grad_g_two], axis=0)
    sums_attn = links.over_depth(sums_attn)
    cut = sums_ffn.shape[0] // 2
    ffn_corner = links.both(ffn_y[:cut], ffn_x[cut:])
    gain_sums = gain_sums + links.swap(after(gain_sums, *ffn_corner), 1)

    def stacked(own, along_x, along_y, corner, *earlier):
        mine = jnp.stack([own, along_x, along_y, jnp.concatenate(corner, axis=0)])
        return mine, links.swap(after(mine, *earlier), 1)

    ffn_pair = stacked(sums_ffn, ffn_x, ffn_y, ffn_corner, sums_attn, gain_sums)
    share_gate = unpack_columns(pos, *ffn_pair, depth, 0)
    share_up = unpack_columns(pos, *ffn_pair, depth, 1)
    share_down = unpack_rows(pos, *ffn_pair, d_rows, D, 2 * rows)
    attn_x, attn_y, gains_x = links.round((sums_attn, 2), (sums_attn, 4), (gain_sums, 2))
    gain_sums = gain_sums + gains_x
    *attn_corner, gains_y = links.round((attn_y[:80], 2), (attn_x[80:], 4), (gain_sums, 4))
    gain_sums = links.cells(gain_sums + gains_y).reshape(2, depth, rows)

    def own_part(at):
        return lax.dynamic_index_in_dim(gain_sums, at % depth, 1, keepdims=False)

    own_gains = own_part(z)
    for by in range(1, depth):
        own_gains = own_gains + links.shift(own_part(z + by), by)

    share_q, share_k, share_v, share_out = unpack_attention(
        pos,
        *stacked(
            sums_attn, attn_x, attn_y, attn_corner, share_gate, share_up, share_down, gains_y
        ),
        depth, rows, inner, narrow
    )
    return (
        result,
        input_grad,
        own_gains[0],
        share_q,
        share_k,
        share_v,
        share_out,
        own_gains[1],
        share_gate,
        share_up,
        share_down,
    )


def solution(mesh):
    tokens = P(("rep", "fsdp"), None)
    gain, weight = P("fsdp"), P("fsdp", None)
    return jax.shard_map(
        functools.partial(on_device, mesh.shape["rep"], mesh.shape["fsdp"]),
        mesh=mesh,
        in_specs=(tokens, gain, *[weight] * 4, gain, *[weight] * 3, tokens),
        out_specs=(tokens, tokens, gain, *[weight] * 4, gain, *[weight] * 3),
        check_vma=False,
    )
```

```python
import functools
import math

import jax
import jax.numpy as jnp
import numpy as np
from jax import lax
from jax.experimental import pallas as pl
from jax.experimental.pallas import tpu as pltpu
from jax.sharding import PartitionSpec as P

D = 1536
HEADS = 16
KV = 8
HD = 96
BF = jnp.bfloat16
F32 = jnp.float32
MiB = 1024 * 1024
ANY = pl.BlockSpec(memory_space=pl.ANY)
WHOLE = pl.BlockSpec(memory_space=pltpu.VMEM)
SCALARS = pl.BlockSpec(memory_space=pltpu.SMEM)
QUADS = 4
TILE = 256
SCALE = 1.0 / math.sqrt(HD)
PACE = 0.02


def after(value, *earlier):
    return lax.optimization_barrier((value, *earlier))[0]


def nt(a, b):
    return lax.dot_general(a, b, (((1,), (1,)), ((), ())), preferred_element_type=F32)


def tn(a, b):
    return lax.dot_general(a, b, (((0,), (0,)), ((), ())), preferred_element_type=F32)


def nn(a, b):
    return jnp.dot(a, b, preferred_element_type=F32)


def rms(values):
    return lax.rsqrt(jnp.mean(values * values, axis=-1, keepdims=True) + 1e-05)


def tile_at(i, size):
    return pl.ds(pl.multiple_of(i * size, size), size)


def call(
    kernel,
    out_shape,
    *args,
    scratch=(),
    vmem=48,
    grid=(),
    in_specs=None,
    out_specs=None,
    us=5,
    aliases=None,
):
    return pl.pallas_call(
        kernel,
        grid=grid,
        out_shape=out_shape,
        in_specs=in_specs,
        out_specs=out_specs,
        scratch_shapes=list(scratch),
        input_output_aliases=aliases or {},
        compiler_params=pltpu.CompilerParams(vmem_limit_bytes=vmem * MiB),
        cost_estimate=pl.CostEstimate(
            flops=int(us * PACE * 1.15e9), bytes_accessed=1024, transcendentals=0
        ),
    )(*args)


def shaped(shape, dtype=BF):
    return jax.ShapeDtypeStruct(shape, dtype)


class Links:
    def __init__(self, reps, depth):
        self.reps, self.depth = reps, depth
        self.rounds = [[], [], []]

    def swap(self, value, bit):
        return lax.ppermute(value, "rep", [(i, i ^ bit) for i in range(self.reps)])

    def round(self, *moves):
        earlier = self.rounds[-2] + self.rounds[-3]
        moved = [self.swap(after(value, *earlier), bit) for value, bit in moves]
        self.rounds.append(moved)
        return moved

    def both(self, along_x, along_y):
        return self.round((along_x, 2), (along_y, 4))

    def shift(self, value, by):
        return lax.ppermute(value, "fsdp", [(i, (i + by) % self.depth) for i in range(self.depth)])

    def over_depth(self, value):
        return self.cells(lax.psum_scatter(value, "fsdp", scatter_dimension=0, tiled=True)[0])

    def cells(self, value):
        if self.reps == 2 * QUADS:
            return value
        groups = [
            [cell * 2 * QUADS + i for cell in range(self.reps // (2 * QUADS))]
            for i in range(2 * QUADS)
        ]
        return lax.psum(value, "rep", axis_index_groups=groups)

    def spread(self, piece, cut):
        return Gathered(self, piece, cut)


class Summed:
    def __init__(self, links, own, along_x, along_y, corner):
        self.links, self.own, self.along_x, self.along_y = links, own, along_x, along_y
        self.first = links.both(*corner)
        self.second = links.both(along_x[0], along_y[1])

    def add(self):
        x_high = (self.along_x[1].astype(F32) + self.first[1].astype(F32)).astype(BF)
        y_low = (self.along_y[0].astype(F32) + self.first[0].astype(F32)).astype(BF)
        self.added = x_high, y_low
        self.third = self.links.both(*self.added)

    def total(self, earlier=(), more=0):
        low, high = self.own
        depth, n, m = low.shape
        n, rows = n - more, n + high.shape[1] - 2 * more

        def kernel(a, b, c, d, e, f, out, *rest):
            lows = a[0].astype(F32) + b[0].astype(F32) + c[0].astype(F32)
            highs = d[0].astype(F32) + e[0].astype(F32) + f[0].astype(F32)
            out[0, :n] = lows[:n].astype(BF)
            out[0, n:] = highs[: rows - n].astype(BF)
            if more:
                rest[0][0] = lows[n:].astype(BF)
                rest[0][1] = highs[rows - n :].astype(BF)

        def block(height):
            return pl.BlockSpec((1, height, m), lambda i: (i, 0, 0))

        outs = [shaped((depth, rows, m)), shaped((2, depth * more, m))]
        specs = [block(rows), pl.BlockSpec((2, more, m), lambda i: (0, i, 0))]
        count = 2 if more else 1
        return call(
            kernel,
            outs[:count],
            after(low, *earlier),
            self.second[0],
            self.third[1],
            high,
            self.third[0],
            self.second[1],
            grid=(depth,),
            in_specs=[block(n + more)] * 3 + [block(rows - n + more)] * 3,
            out_specs=specs[:count],
            us=5,
        )


class Gathered:
    def __init__(self, links, piece, cut):
        self.rows, self.cut, self.depth = piece.shape[0], cut, links.depth
        n, m, depth = piece.shape[0], piece.shape[1], links.depth
        self.own = lax.all_gather(piece, "fsdp", axis=0, tiled=True)
        self.links, self.shape = links, (n, m)

    def compact(self, pos):
        (n, m), depth = self.shape, self.depth

        def kernel(pos_ref, in_ref, out_ref):
            out_ref[...] = in_ref[...]

        self.remote = pl.pallas_call(
            kernel,
            grid_spec=pltpu.PrefetchScalarGridSpec(
                num_scalar_prefetch=1,
                grid=(depth - 1,),
                in_specs=[pl.BlockSpec((n, m), lambda i, at: (lax.rem(at[0] + 1 + i, depth), 0))],
                out_specs=pl.BlockSpec((n, m), lambda i, at: (i, 0)),
            ),
            out_shape=shaped(((depth - 1) * n, m)),
            cost_estimate=pl.CostEstimate(
                flops=int(4 * PACE * 1.15e9), bytes_accessed=1024, transcendentals=0
            ),
        )(pos, self.own)

    def to_plane(self):
        self.x, self.y = self.links.both(self.remote, self.remote)
        self.parts = after(self.y[: self.cut], self.x), after(self.x[self.cut :], self.y)

    def to_corner(self):
        self.corner = self.links.both(*self.parts)

    def arrays(self, rel):
        return self.corner if rel == 3 else ((self.own, self.x, self.y)[rel],)

    def segments(self, rel, low, high):
        n = self.rows
        found = []
        for i in range(self.depth - 1):
            first, last = i * n + low, i * n + high
            if rel == 0:
                found.append((0, i, low, high - low, 0))
            elif rel < 3:
                found.append((0, i, first, high - low, 0))
            else:
                if first < self.cut:
                    found.append((0, i, first, min(last, self.cut) - first, 0))
                if last > self.cut:
                    begin = max(first, self.cut)
                    found.append((1, i, begin - self.cut, last - begin, begin - first))
        return found

    def copies(self, rel, refs, z, target, stride, base, low, high):
        out = []
        for which, i, row, count, offset in self.segments(rel, low, high):
            shard = lax.rem(z + 1 + i, self.depth)
            source = pl.multiple_of(shard * self.rows + row, 16) if rel == 0 else row
            at = pl.multiple_of(shard * stride + base + offset, 16)
            out.append((refs[which].at[pl.ds(source, count), :], target.at[pl.ds(at, count), :]))
        return out


def start(copies, sems, first=0):
    made = [
        pltpu.make_async_copy(source, target, sems.at[first + i])
        for i, (source, target) in enumerate(copies)
    ]
    for copy in made:
        copy.start()
    return made


def all_parts(got):
    return [array for rel in range(QUADS) for array in got.arrays(rel)]


def whole_copies(got, refs, z, k, target, stride, low, high):
    out, at = [], 0
    for rel in range(QUADS):
        size = len(got.arrays(rel))
        base = (k ^ rel) * (high - low)
        out += got.copies(rel, refs[at : at + size], z, target, stride, base, low, high)
        at += size
    return out


def n_copies(got, low, high, rels=range(QUADS)):
    return sum(len(got.segments(rel, low, high)) for rel in rels)


def tables(length):
    freq = 10000.0 ** (-np.arange(0, HD, 2) / HD)
    angle = np.arange(length)[:, None] * freq[None, :]
    cosine, sine = np.cos(angle), np.sin(angle)
    none = np.zeros_like(sine)

    def four(a, b):
        return jnp.asarray(np.concatenate([a, b] * 4, axis=1), F32)

    return four(cosine, cosine), four(-sine, none), four(none, sine)


def rotated(u, cosine, right, left, sign):
    width = u.shape[1]
    turned = pltpu.roll(u, width - HD // 2, 1) * right + pltpu.roll(u, HD // 2, 1) * left
    return u * cosine + sign * turned


def project(pos, pair, gain, got, shard, turns):
    length, width = pair[0].shape
    cols = shard.shape[1]
    rows = shard.shape[0]
    parts = all_parts(got)
    narrow = cols // 4
    high = rows // QUADS
    copies_in = 3 + n_copies(got, 0, high)

    def kernel(pos_ref, gain_ref, cos_ref, right_ref, left_ref, ta, tb, shard_ref, *refs):
        part_refs = refs[: len(parts)]
        normed, q, key, value, weight, toks, sems = refs[len(parts) :]
        z, k = pos_ref[0], pos_ref[1]
        first = start(
            [(ta, toks.at[pl.ds(0, length), :]), (tb, toks.at[pl.ds(length, length), :])], sems
        )
        second = start(
            [(shard_ref, weight.at[pl.ds(pl.multiple_of(z * rows, 16), rows), :])]
            + whole_copies(got, part_refs, z, k, weight, rows, 0, high),
            sems,
            2,
        )
        for copy in first:
            copy.wait()

        def norm(i, _):
            at = tile_at(i, TILE)
            x = toks[at, :].astype(F32)
            normed[at, :] = (x * rms(x) * gain_ref[...]).astype(BF)
            return 0

        lax.fori_loop(0, 2 * length // TILE, norm, 0)
        for copy in second:
            copy.wait()

        def body(i, _):
            at = tile_at(i, TILE)
            place = tile_at(lax.rem(i, length // TILE), TILE)
            out = nn(normed[at, :], weight[...])
            cosine, right, left = cos_ref[place, :], right_ref[place, :], left_ref[place, :]
            for t in range(2):
                u = out[:, t * narrow : (t + 1) * narrow]
                q[at, t * narrow : (t + 1) * narrow] = rotated(
                    u, cosine, right, left, 1.0
                ).astype(BF)
            key[at, :] = rotated(
                out[:, 2 * narrow : 3 * narrow], cosine, right, left, 1.0
            ).astype(BF)
            value[at, :] = out[:, 3 * narrow :].astype(BF)
            return 0

        lax.fori_loop(0, 2 * length // TILE, body, 0)

    return call(
        kernel,
        [
            shaped((2 * length, width)),
            shaped((2 * length, 2 * narrow)),
            shaped((2 * length, narrow)),
            shaped((2 * length, narrow)),
            shaped((width, cols)),
        ],
        pos,
        gain,
        *turns,
        *pair,
        shard,
        *parts,
        in_specs=[SCALARS] + [WHOLE] * 4 + [ANY] * (3 + len(parts)),
        out_specs=[WHOLE] * 5,
        scratch=[pltpu.VMEM((2 * length, width), BF), pltpu.SemaphoreType.DMA((copies_in,))],
        us=13,
    )


def masked(scores, first):
    keys = lax.broadcasted_iota(jnp.int32, scores.shape, 0)
    queries = lax.broadcasted_iota(jnp.int32, scores.shape, 1) + first
    return jnp.where(keys <= queries, scores, -1e30)


def attend(q, key, value):
    length = q.shape[0] // 2
    heads, groups = q.shape[1] // HD, key.shape[1] // HD

    def kernel(q_ref, k_ref, v_ref, o_ref, lse_ref):
        for g in range(groups):
            keys = k_ref[:, g * HD : (g + 1) * HD]
            turned = v_ref[:, g * HD : (g + 1) * HD].T
            for j in range(g * heads // groups, (g + 1) * heads // groups):
                for t in range(length // TILE):
                    at = slice(t * TILE, (t + 1) * TILE)
                    reach = (t + 1) * TILE
                    s = nt(keys[:reach], q_ref[at, j * HD : (j + 1) * HD]) * SCALE
                    s = masked(s, t * TILE)
                    peak = jnp.max(s, axis=0, keepdims=True)
                    e = jnp.exp(s - peak)
                    total = jnp.sum(e, axis=0, keepdims=True)
                    lse = peak + jnp.log(total)
                    p = (e * (1.0 / total)).astype(BF)
                    lse_ref[0, j : j + 1, at] = lse
                    o_ref[at, j * HD : (j + 1) * HD] = nn(turned[:, :reach], p).T.astype(BF)

    return call(
        kernel,
        [shaped(q.shape), shaped((2, heads, length), F32)],
        q,
        key,
        value,
        grid=(2,),
        in_specs=[
            pl.BlockSpec((length, q.shape[1]), lambda i: (i, 0)),
            pl.BlockSpec((length, key.shape[1]), lambda i: (i, 0)),
            pl.BlockSpec((length, key.shape[1]), lambda i: (i, 0)),
        ],
        out_specs=[
            pl.BlockSpec((length, q.shape[1]), lambda i: (i, 0)),
            pl.BlockSpec((1, heads, length), lambda i: (i, 0, 0)),
        ],
        us=10,
    )


def attend_back(q, key, value, lse, d_mixed, turns):
    length = q.shape[0] // 2
    heads, groups = q.shape[1] // HD, key.shape[1] // HD
    inner, narrow = q.shape[1], key.shape[1]

    def kernel(q_ref, k_ref, v_ref, lse_ref, do_ref, cos_ref, right_ref, left_ref, out, dq, dk):
        for g in range(groups):
            keys = k_ref[:, g * HD : (g + 1) * HD]
            values = v_ref[:, g * HD : (g + 1) * HD]
            turned = keys.T
            d_key = [jnp.zeros((TILE, HD), F32) for _ in range(length // TILE)]
            d_value = [jnp.zeros((TILE, HD), F32) for _ in range(length // TILE)]
            for j in range(g * heads // groups, (g + 1) * heads // groups):
                for t in range(length // TILE):
                    at = slice(t * TILE, (t + 1) * TILE)
                    reach = (t + 1) * TILE
                    queries = q_ref[at, j * HD : (j + 1) * HD]
                    upstream = do_ref[at, j * HD : (j + 1) * HD]
                    s = masked(nt(keys[:reach], queries) * SCALE, t * TILE)
                    p = jnp.exp(s - lse_ref[0, j : j + 1, at])
                    dp = nt(values[:reach], upstream)
                    centre = jnp.sum(p * dp, axis=0, keepdims=True)
                    ds = (p * (dp - centre)).astype(BF)
                    from_values = nn(p.astype(BF), upstream)
                    from_keys = nn(ds, queries)
                    for i in range(t + 1):
                        rows = slice(i * TILE, (i + 1) * TILE)
                        d_value[i] = d_value[i] + from_values[rows]
                        d_key[i] = d_key[i] + from_keys[rows]
                    dq[at, j * HD : (j + 1) * HD] = nn(turned[:, :reach], ds).T * SCALE
            for i in range(length // TILE):
                rows = slice(i * TILE, (i + 1) * TILE)
                dk[rows, g * HD : (g + 1) * HD] = d_key[i] * SCALE
                first = inner + narrow + g * HD
                out[rows, first : first + HD] = d_value[i].astype(BF)
        cosine, right, left = cos_ref[...], right_ref[...], left_ref[...]
        for t in range(inner // narrow):
            cols = slice(t * narrow, (t + 1) * narrow)
            out[:, cols] = rotated(dq[:, cols], cosine, right, left, -1.0).astype(BF)
        out[:, inner : inner + narrow] = rotated(dk[...], cosine, right, left, -1.0).astype(BF)

    def block(cols):
        return pl.BlockSpec((length, cols), lambda i: (i, 0))

    table = pl.BlockSpec(turns[0].shape, lambda i: (0, 0))
    return call(
        kernel,
        shaped((2 * length, inner + 2 * narrow)),
        q,
        key,
        value,
        lse,
        d_mixed,
        *turns,
        grid=(2,),
        in_specs=[
            block(inner),
            block(narrow),
            block(narrow),
            pl.BlockSpec((1, heads, length), lambda i: (i, 0, 0)),
            block(inner),
            table,
            table,
            table,
        ],
        out_specs=block(inner + 2 * narrow),
        scratch=[pltpu.VMEM((length, inner), F32), pltpu.VMEM((length, narrow), F32)],
        us=17,
    )


def mix(pos, mixed, got, shard):
    tokens, inner = mixed.shape
    width = shard.shape[1]
    rows = shard.shape[0]
    high = got.rows
    low = high - rows // QUADS
    parts = all_parts(got)

    def kernel(pos_ref, mixed_ref, shard_ref, *refs):
        part_refs = refs[: len(parts)]
        other, mine, weight, sems = refs[len(parts) :]
        z, k = pos_ref[0], pos_ref[1]
        copies = start(
            [(shard_ref, weight.at[pl.ds(pl.multiple_of(z * rows, 16), rows), :])]
            + whole_copies(got, part_refs, z, k, weight, rows, low, high),
            sems,
        )
        for copy in copies:
            copy.wait()
        for i in range(tokens // 2 // TILE):
            at = slice(i * TILE, (i + 1) * TILE)
            there = slice(tokens // 2 + i * TILE, tokens // 2 + (i + 1) * TILE)
            other[at, :] = nn(mixed_ref[there, :], weight[...]).astype(BF)
            mine[at, :] = nn(mixed_ref[at, :], weight[...])

    return call(
        kernel,
        [
            shaped((tokens // 2, width)),
            shaped((tokens // 2, width), F32),
            shaped((inner, width)),
        ],
        pos,
        mixed,
        shard,
        *parts,
        in_specs=[SCALARS, WHOLE] + [ANY] * (1 + len(parts)),
        out_specs=[WHOLE] * 3,
        scratch=[pltpu.SemaphoreType.DMA((1 + n_copies(got, low, high),))],
        us=8,
    )


def residual_norm(tokens, mine, received, gain):
    length, width = tokens.shape

    def kernel(x, a, b, gain_ref, hidden, normed):
        h = x[...].astype(F32) + a[...] + b[...].astype(F32)
        hidden[...] = h
        normed[...] = (h * rms(h) * gain_ref[...]).astype(BF)

    block = pl.BlockSpec((TILE, width), lambda i: (i, 0))
    return call(
        kernel,
        [shaped((length, width), F32), shaped((length, width))],
        tokens,
        mine,
        received,
        gain,
        grid=(length // TILE,),
        in_specs=[block, block, block, pl.BlockSpec((1, width), lambda i: (0, 0))],
        out_specs=[block, block],
        us=4,
    )


def norm_back(mine, received, values, residual, gain, rounded):
    length, width = values.shape

    def kernel(a, b, values_ref, residual_ref, gain_ref, grad, gain_grad, *low):
        x = values_ref[...].astype(F32)
        factor = rms(x)
        normed = x * factor
        upstream = a[...] + b[...].astype(F32)
        part = jnp.sum(upstream * normed, axis=0, keepdims=True)

        @pl.when(pl.program_id(0) == 0)
        def _():
            gain_grad[...] = part

        @pl.when(pl.program_id(0) > 0)
        def _():
            gain_grad[...] += part

        scaled = upstream * gain_ref[...]
        inside = scaled - normed * jnp.mean(scaled * normed, axis=-1, keepdims=True)
        total = residual_ref[...].astype(F32) + factor * inside
        grad[...] = total
        if low:
            low[0][...] = total.astype(BF)

    block = pl.BlockSpec((TILE, width), lambda i: (i, 0))
    line = pl.BlockSpec((1, width), lambda i: (0, 0))
    return call(
        kernel,
        [shaped((length, width), F32), shaped((1, width), F32)]
        + [shaped((length, width))] * rounded,
        mine,
        received,
        values,
        residual,
        gain,
        grid=(length // TILE,),
        in_specs=[block] * 4 + [line],
        out_specs=[block, line] + [block] * rounded,
        us=5,
    )


def weight_copies(pos_ref, rel, got, refs, shard_ref, target):
    z, k, c = pos_ref[0], pos_ref[1], pos_ref[2]
    if rel == 0:
        return [(refs[0], target)]
    depth, rows = got.depth, got.rows
    j = k ^ rel
    at = pl.ds(pl.multiple_of(z * rows, 16), rows)
    if shard_ref.shape[0] == rows:
        seg = target.shape[1] // depth
        copies = []
        for s in range(depth):
            col = pl.multiple_of(((s * 2 + c) * QUADS + j) * seg, 128)
            copies.append(
                (shard_ref.at[:, pl.ds(col, seg)], target.at[at, pl.ds(s * seg, seg)])
            )
    else:
        row = pl.multiple_of((c * QUADS + j) * rows, 16)
        copies = [(shard_ref.at[pl.ds(row, rows), :], target.at[at, :])]
    return copies + got.copies(rel, refs, z, target, rows, 0, 0, rows)


def count_copies(rel, got, columns):
    return 1 if rel == 0 else (got.depth if columns else 1) + n_copies(got, 0, got.rows, [rel])


class Weights:
    def __init__(self, shards, gots, columns, rels=range(QUADS)):
        self.shards, self.gots, self.columns, self.rels = shards, gots, columns, rels
        self.operands = list(shards)
        self.places = {}
        for i, got in enumerate(gots):
            for rel in rels:
                arrays = got.arrays(rel)
                self.places[i, rel] = (len(self.operands), len(arrays))
                self.operands += arrays
        self.total = sum(
            count_copies(rel, got, col) for got, col in zip(gots, columns) for rel in rels
        )
        self.scratch = [pltpu.VMEM((len(rels), *got.own.shape), BF) for got in gots]

    def start(self, pos_ref, refs, targets, sems, first):
        begun = []
        for slot, rel in enumerate(self.rels):
            copies = []
            for i, got in enumerate(self.gots):
                at, count = self.places[i, rel]
                copies += weight_copies(
                    pos_ref, rel, got, refs[at : at + count], refs[i], targets[i].at[slot]
                )
            begun.append(start(copies, sems, first))
            first += len(copies)
        return begun


def wait(copies):
    for copy in copies:
        copy.wait()


def ffn_forward(pos, rels, n_two, d_out, shards, gots, deep):
    weights = Weights(shards, gots, (True, True, False), rels)
    length, width = n_two[0].shape
    tokens = 2 * length
    cols = gots[0].own.shape[1]
    depth, rows = gots[2].depth, gots[2].rows
    given = [] if deep is None else [deep]
    count = len(weights.operands)
    n = len(rels)
    tile = 2 * TILE

    def kernel(pos_ref, na, nb, ya, yb, *refs):
        operands, refs = refs[:count], refs[count + len(given) :]
        acts, dgus, grads = refs[:n], refs[n : 2 * n], refs[2 * n]
        n_all, y_all, w_gate, w_up, w_down, act, dgu, made, sems = refs[2 * n + 1 :]
        first = start(
            [
                (na, n_all.at[pl.ds(0, length), :]),
                (nb, n_all.at[pl.ds(length, length), :]),
                (ya, y_all.at[pl.ds(0, length), :]),
                (yb, y_all.at[pl.ds(length, length), :]),
            ],
            sems,
        )
        begun = weights.start(pos_ref, operands, (w_gate, w_up, w_down), sems, 4)
        wait(first)
        written = []
        for slot, rel in enumerate(rels):
            wait(begun[slot])

            def body(i, _, slot=slot):
                at = tile_at(i, tile)
                normed, grad = n_all[at, :], y_all[at, :]
                gated = nn(normed, w_gate[slot])
                upper = nn(normed, w_up[slot])
                d_act = nt(grad, w_down[slot])
                sig = 1.0 / (1.0 + jnp.exp(-gated))
                silu = gated * sig
                act[slot, at, :] = (silu * upper).astype(BF)
                dgu[slot, at, :cols] = (
                    d_act * upper * sig * (1.0 + gated * (1.0 - sig))
                ).astype(BF)
                dgu[slot, at, cols:] = (d_act * silu).astype(BF)
                return 0

            lax.fori_loop(0, tokens // tile, body, 0)
            at = 4 + weights.total + 3 * slot
            written += start([(act.at[slot], acts[slot]), (dgu.at[slot], dgus[slot])], sems, at)

            def grad(s, _, slot=slot):
                made[slot, s] = tn(act[slot, :, tile_at(s, rows)], y_all[...]).astype(BF)
                return 0

            lax.fori_loop(0, depth, grad, 0)
            written += start([(made.at[slot], grads.at[:, rel])], sems, at + 2)
        wait(written)

    made = call(
        kernel,
        [shaped((tokens, cols))] * n
        + [shaped((tokens, 2 * cols))] * n
        + [shaped((depth, QUADS, rows, width))],
        pos,
        *n_two,
        *d_out,
        *weights.operands,
        *given,
        in_specs=[SCALARS] + [ANY] * (4 + count + len(given)),
        out_specs=[ANY] * (2 * n + 1),
        scratch=[
            pltpu.VMEM((tokens, width), BF),
            pltpu.VMEM((tokens, width), BF),
            *weights.scratch,
            pltpu.VMEM((n, tokens, cols), BF),
            pltpu.VMEM((n, tokens, 2 * cols), BF),
            pltpu.VMEM((n, depth, rows, width), BF),
            pltpu.SemaphoreType.DMA((4 + weights.total + 3 * n,)),
        ],
        vmem=56,
        us=3 + 9 * n,
        aliases={5 + count: 2 * n} if given else None,
    )
    return made[:n], made[n : 2 * n], made[2 * n]


def ffn_grads(n_two, dgus, depth):
    length, width = n_two[0].shape
    tokens = 2 * length
    rows = width // depth
    cols = dgus[0].shape[1] // 2
    n = len(dgus)

    def kernel(na, nb, *refs):
        ins, outs, refs = refs[:n], refs[n : 3 * n], refs[3 * n :]
        n_all, dgu, turned, made, sems = refs
        first = start(
            [
                (na, n_all.at[pl.ds(0, length), :]),
                (nb, n_all.at[pl.ds(length, length), :]),
                *[(ins[rel], dgu.at[rel]) for rel in range(n)],
            ],
            sems,
        )
        wait(first[:2])
        for s in range(depth):
            at = slice(s * rows, (s + 1) * rows)
            turned[at, :] = n_all[:, at].T
        written = [[], []]
        for rel in range(n):
            first[2 + rel].wait()
            for part in range(2):
                wait(written[part])
                grads = nn(turned[...], dgu[rel, :, part * cols : (part + 1) * cols])
                for s in range(depth):
                    made[part, s] = grads[s * rows : (s + 1) * rows].astype(BF)
                written[part] = start(
                    [(made.at[part], outs[2 * rel + part])], sems, 2 + n + part
                )
        wait(written[0] + written[1])

    made = call(
        kernel,
        [shaped((depth, rows, cols))] * (2 * n),
        *n_two,
        *dgus,
        in_specs=[ANY] * (2 + n),
        out_specs=[ANY] * (2 * n),
        scratch=[
            pltpu.VMEM((tokens, width), BF),
            pltpu.VMEM((n, tokens, 2 * cols), BF),
            pltpu.VMEM((width, tokens), BF),
            pltpu.VMEM((2, depth, rows, cols), BF),
            pltpu.SemaphoreType.DMA((4 + n,)),
        ],
        us=16,
    )
    return [made[2 * rel : 2 * rel + 2] for rel in range(n)]


def ffn_product(pos, lefts, shards, gots, transposed):
    weights = Weights(shards, gots, (transposed,) * len(gots))
    tokens = lefts[0].shape[0]
    half = tokens // 2
    cols = lefts[0].shape[1] // len(gots)
    width = gots[0].own.shape[0] if transposed else gots[0].own.shape[1]
    count = len(weights.operands)

    def kernel(pos_ref, *refs):
        ins, operands, refs = refs[:QUADS], refs[QUADS : QUADS + count], refs[QUADS + count :]
        other, mine, refs = refs[0], refs[1], refs[2:]
        targets, (left, total, sems) = refs[: len(gots)], refs[len(gots) :]
        first = start([(ins[rel], left.at[rel]) for rel in range(QUADS)], sems)
        begun = weights.start(pos_ref, operands, targets, sems, QUADS)
        for rel in range(QUADS):
            first[rel].wait()
            wait(begun[rel])

            def body(i, _, rel=rel):
                at = tile_at(i, 2 * TILE)
                part = None if rel == 0 else total[at, :]
                for n, target in enumerate(targets):
                    term = (nt if transposed else nn)(
                        left[rel, at, n * cols : (n + 1) * cols], target[rel]
                    )
                    part = term if part is None else part + term
                total[at, :] = part
                return 0

            lax.fori_loop(0, tokens // (2 * TILE), body, 0)
        other[...] = total[half:, :].astype(BF)
        mine[...] = total[:half, :]

    return call(
        kernel,
        [shaped((half, width)), shaped((half, width), F32)],
        pos,
        *lefts,
        *weights.operands,
        in_specs=[SCALARS] + [ANY] * (QUADS + count),
        out_specs=[WHOLE] * 2,
        scratch=[
            *weights.scratch,
            pltpu.VMEM((QUADS, tokens, len(gots) * cols), BF),
            pltpu.VMEM((tokens, width), F32),
            pltpu.SemaphoreType.DMA((QUADS + weights.total,)),
        ],
        vmem=56,
        us=20,
    )


def rows_product(lefts, rights, half, transposed, dtype, us):
    rows = lefts[0].shape[0] // 2
    per = len(rights) // len(lefts)
    width = rights[0].shape[0] if transposed else rights[0].shape[1]
    depth = rights[0].shape[1] if transposed else rights[0].shape[0]
    steps = rows // TILE

    def kernel(*refs):
        left, right, out = refs[: len(lefts)], refs[len(lefts) : -1], refs[-1]
        total = None
        for i, ref in enumerate(right):
            part = left[i // per][:, (i % per) * depth : (i % per + 1) * depth]
            term = (nt if transposed else nn)(part, ref[...])
            total = term if total is None else total + term
        out[...] = total.astype(dtype)

    return call(
        kernel,
        shaped((rows, width), dtype),
        *lefts,
        *rights,
        grid=(steps,),
        in_specs=[
            pl.BlockSpec((TILE, left.shape[1]), lambda i: (i + half * steps, 0)) for left in lefts
        ]
        + [pl.BlockSpec(right.shape, lambda i: (0, 0)) for right in rights],
        out_specs=pl.BlockSpec((TILE, width), lambda i: (i, 0)),
        vmem=56,
        us=us,
    )


def mix_back(low, other, mixed, weight):
    length, width = low.shape
    inner = mixed.shape[1]

    def kernel(a, b, mixed_ref, weight_ref, d_mixed, grad):
        for i in range(2 * length // TILE):
            at = slice(i * TILE, (i + 1) * TILE)
            part = a if i < length // TILE else b
            first = i * TILE % length
            d_mixed[at, :] = nt(part[first : first + TILE, :], weight_ref[...]).astype(BF)

        def body(i, _):
            at = tile_at(i, TILE)
            grad[at, :] = (
                tn(mixed_ref[:length, at], a[...]) + tn(mixed_ref[length:, at], b[...])
            ).astype(BF)
            return 0

        lax.fori_loop(0, inner // TILE, body, 0)

    return call(
        kernel,
        [shaped((2 * length, inner)), shaped((inner, width))],
        low,
        other,
        mixed,
        weight,
        in_specs=[WHOLE] * 4,
        out_specs=[WHOLE] * 2,
        us=10,
    )


def attention_grads(links, pos, normed, d_qkv, grad_out, deep, depth, rows, low):
    width, cols = normed.shape[1], d_qkv.shape[1]
    quarter = rows // QUADS
    small = quarter // 2
    high = quarter - low + small
    more = deep.shape[1] // (2 * depth)

    def kernel(pos_ref, normed_ref, d_ref, out_ref, deep_ref, *refs):
        outs, tile = refs[:-1], refs[-1]
        k = pos_ref[1]

        def body(s, _):
            tile[...] = tn(normed_ref[:, tile_at(s, rows)], d_ref[...]).astype(BF)
            for rel in range(QUADS):
                j = k ^ rel
                first = pl.multiple_of(j * quarter, 16)
                to_low, to_high = outs[2 * rel : 2 * rel + 2]
                to_low[s, :low] = tile[pl.ds(first, low), :]
                to_high[s, : quarter - low] = tile[pl.ds(first + low, quarter - low), :]
                at = pl.multiple_of(s * (rows // 2) + j * small, 16)
                to_high[s, quarter - low : high] = out_ref[pl.ds(at, small), :]
                at = pl.multiple_of(s * more, 16)
                to_low[s, low:] = deep_ref[rel, pl.ds(at, more), :]
                to_high[s, high:] = deep_ref[rel, pl.ds(at + depth * more, more), :]
            return 0

        lax.fori_loop(0, depth, body, 0)

    made = call(
        kernel,
        [shaped((depth, n + more, cols)) for _ in range(QUADS) for n in (low, high)],
        pos,
        normed,
        d_qkv,
        grad_out,
        deep,
        in_specs=[SCALARS] + [WHOLE] * 4,
        out_specs=[WHOLE] * (2 * QUADS),
        scratch=[pltpu.VMEM((rows, cols), BF)],
        us=10,
    )
    return Summed(links, *[made[2 * rel : 2 * rel + 2] for rel in range(QUADS)])


def unpack_columns(pos, mine, other, depth, half):
    cols = mine.shape[2]
    rows = D // depth
    seg = cols // depth
    width = cols * 2 * QUADS
    tile = 128
    steps = rows // tile

    def kernel(pos_ref, a, b, out):
        k, c = pos_ref[1], pos_ref[2]
        for ref, core in ((a, c), (b, 1 - c)):
            for rel in range(QUADS):
                block = core * QUADS + (k ^ rel)
                for s in range(depth):
                    at = pl.multiple_of((s * 2 * QUADS + block) * seg, 128)
                    out[:, pl.ds(at, seg)] = ref[rel, :, s * seg : (s + 1) * seg].astype(F32)

    spec = pl.BlockSpec((QUADS, tile, cols), lambda i: (0, i + half * steps, 0))
    return call(
        kernel,
        shaped((rows, width), F32),
        pos,
        mine,
        other,
        grid=(steps,),
        in_specs=[SCALARS, spec, spec],
        out_specs=pl.BlockSpec((tile, width), lambda i: (i, 0)),
        us=4,
    )


def unpack_rows(pos, mine, other, rows, width, first):
    tile = mine.shape[2]

    def kernel(pos_ref, a, b, out):
        k, c = pos_ref[1], pos_ref[2]
        for ref, core in ((a, c), (b, 1 - c)):
            for rel in range(QUADS):
                at = pl.multiple_of((core * QUADS + (k ^ rel)) * rows, 8)
                out[pl.ds(at, rows), :] = ref[rel].astype(F32)

    spec = pl.BlockSpec((QUADS, rows, tile), lambda i: (0, first // rows + i, 0))
    return call(
        kernel,
        shaped((2 * QUADS * rows, width), F32),
        pos,
        mine,
        other,
        grid=(width // tile,),
        in_specs=[SCALARS, spec, spec],
        out_specs=pl.BlockSpec((2 * QUADS * rows, tile), lambda i: (0, i)),
        us=5,
    )


def unpack_attention(pos, mine, other, depth, rows, inner, narrow):
    quarter = rows // QUADS
    small = quarter // 2

    def kernel(pos_ref, a, b, *outs):
        k, c = pos_ref[1], pos_ref[2]

        def place(first, second):
            for core, ref in ((0, first), (1, second)):
                for rel in range(QUADS):
                    j = k ^ rel
                    at = pl.ds(pl.multiple_of(j * quarter, 8), quarter)
                    cols = 0
                    for out, width in zip(outs[:3], (inner, narrow, narrow)):
                        seg = width // depth
                        for s in range(depth):
                            to = (2 * s + core) * seg
                            out[at, to : to + seg] = ref[
                                rel, :quarter, cols : cols + seg
                            ].astype(F32)
                            cols += seg
                    at = pl.ds(pl.multiple_of(core * (rows // 2) + j * small, 8), small)
                    outs[3][at, :] = ref[rel, quarter:, :].astype(F32)

        @pl.when(c == 0)
        def _():
            place(a, b)

        @pl.when(c == 1)
        def _():
            place(b, a)

    return call(
        kernel,
        [
            shaped((rows, 2 * inner), F32),
            shaped((rows, 2 * narrow), F32),
            shaped((rows, 2 * narrow), F32),
            shaped((rows, 2 * inner), F32),
        ],
        pos,
        mine,
        other,
        in_specs=[SCALARS] + [WHOLE] * 2,
        out_specs=[WHOLE] * 4,
        us=6,
    )


def on_device(
    reps,
    depth,
    tokens,
    gain_attn,
    w_query,
    w_key,
    w_value,
    w_out,
    gain_ffn,
    w_gate,
    w_up,
    w_down,
    cotangent,
):
    links = Links(reps, depth)
    z = lax.axis_index("fsdp")
    r = lax.axis_index("rep")
    c = r % 2
    k = (r // 2) % QUADS
    pos = jnp.stack([z, k, c]).astype(jnp.int32)
    length = tokens.shape[0]
    rows = w_query.shape[0]
    quarter = rows // QUADS
    small = quarter // 2
    inner = D // 2
    narrow = inner // (HEADS // KV)

    def core_columns(weight):
        split = weight.reshape(rows, depth, 2, weight.shape[1] // (2 * depth))
        return lax.dynamic_index_in_dim(split, c, 2, keepdims=False).reshape(rows, -1)

    shard_qkv = jnp.concatenate([core_columns(i) for i in (w_query, w_key, w_value)], axis=1)
    shard_out = lax.dynamic_slice_in_dim(w_out, c * (rows // 2), rows // 2, 0)
    piece_qkv = lax.dynamic_slice_in_dim(shard_qkv, k * quarter, quarter, 0)
    piece_out = lax.dynamic_slice_in_dim(shard_out, k * small, small, 0)
    seg = w_gate.shape[1] // (depth * 2 * QUADS)
    d_rows = w_down.shape[0] // (2 * QUADS)

    def block_columns(weight):
        return jnp.concatenate(
            [
                lax.dynamic_slice_in_dim(weight, ((s * 2 + c) * QUADS + k) * seg, seg, 1)
                for s in range(depth)
            ],
            axis=1,
        )

    piece_gate, piece_up = block_columns(w_gate), block_columns(w_up)
    piece_down = lax.dynamic_slice_in_dim(w_down, (c * QUADS + k) * d_rows, d_rows, 0)

    gains = jnp.stack([gain_attn, gain_ffn])
    gains = jnp.stack([gains] + [links.shift(gains, by) for by in range(1, depth)])
    gains = jnp.take(gains, (z - jnp.arange(depth)) % depth, axis=0)
    g_one = gains[:, 0].reshape(1, -1).astype(F32)
    g_two = gains[:, 1].reshape(1, -1).astype(F32)
    token_pair = (tokens, links.swap(tokens, 1))
    d_pair = (cotangent, links.swap(cotangent, 1))
    turns = tables(length)

    piece = jnp.concatenate([piece_qkv, piece_out], axis=0)
    early = after(pos, g_one, g_two, token_pair[1], d_pair[1])
    got_attn = links.spread(piece, 224)
    got_gate = links.spread(piece_gate, 3 * rows // 2)
    got_up = links.spread(after(piece_up, got_attn.own), 3 * rows // 2)
    got_down = links.spread(after(piece_down, got_gate.own), 3 * d_rows // 2)
    got_attn.compact(early)
    got_attn.to_plane()
    got_gate.compact(pos)
    got_gate.to_plane()
    got_attn.to_corner()
    got_up.compact(pos)
    got_up.to_plane()
    got_gate.parts = [after(i, got_up.remote) for i in got_gate.parts]
    got_gate.to_corner()

    ready = after(pos, got_up.remote)
    n_one, q, key, value, wqkv = project(ready, token_pair, g_one, got_attn, shard_qkv, turns)
    mixed, lse = attend(q, key, value)
    got_down.compact(after(pos, lse))
    got_down.to_plane()
    got_up.to_corner()
    got_down.to_corner()
    to_other, mine, wo = mix(pos, mixed, got_attn, shard_out)
    ready = after(to_other, *got_gate.corner, got_up.x, got_up.y, got_down.remote)
    hidden, n_two = residual_norm(tokens, mine, links.swap(ready, 1), g_two)

    n_pair = (n_two, links.swap(n_two, 1))
    shards, gots = (w_gate, w_up, w_down), (got_gate, got_up, got_down)
    acts, dgus, deep = [], [], None
    for rels in ((0, 1, 2), (3,)):
        at = after(pos, dgus[-1]) if dgus else pos
        act, dgu, deep = ffn_forward(at, rels, n_pair, d_pair, shards, gots, deep)
        acts += act
        dgus += dgu
    deep_sum = links.over_depth(deep)
    half = d_rows // 2
    (corner,) = ffn_grads(n_pair, dgus[3:], depth)
    others = ffn_grads(n_pair, [after(i, corner[0]) for i in dgus[:3]], depth)
    wide = Summed(links, *others, corner)
    lefts = [after(i, wide.own[0]) for i in dgus]
    to_other, mine = ffn_product(pos, lefts, (w_gate, w_up), (got_gate, got_up), True)
    wide.add()
    acts = [after(i, to_other, *wide.added) for i in acts]
    out_other, out_mine = ffn_product(pos, acts, (w_down,), (got_down,), False)
    received = links.swap(to_other, 1)
    mine = after(mine, out_mine, *wide.second)
    d_hidden, grad_g_two, low = norm_back(mine, received, hidden, cotangent, g_two, 1)

    low_pair = low, links.swap(after(low, *wide.added), 1)
    d_mixed, grad_out = mix_back(*low_pair, mixed, wo)
    d_qkv = attend_back(q, key, value, lse, d_mixed, turns)
    deep_sum = after(deep_sum, d_qkv)
    small = attention_grads(links, pos, n_one, d_qkv, grad_out, deep_sum, depth, rows, 80)
    (sums_wide,) = wide.total([small.own[0]])
    late = after(d_qkv, sums_wide)
    sums_wide = links.over_depth(sums_wide)
    to_other = rows_product([late], [wqkv], 1, True, BF, 7)
    mine = rows_product([late], [wqkv], 0, True, F32, 7)
    out_received = links.swap(after(out_other, d_hidden), 1)
    result = (hidden + out_mine + out_received.astype(F32)).astype(BF)
    small.add()
    sums_attn, sums_deep = small.total(more=half // depth)
    sums_deep = sums_deep.reshape(d_rows, -1)
    split = sums_deep.shape[1] // sums_wide.shape[1]
    sums_ffn = jnp.concatenate([sums_wide, *jnp.split(sums_deep, split, axis=1)], axis=0)
    ffn_x, ffn_y = links.both(*[after(sums_ffn, sums_attn)] * 2)
    received = links.swap(after(to_other, mine, result, ffn_x, ffn_y), 1)
    input_grad, grad_g_one = norm_back(mine, received, tokens, d_hidden, g_one, 0)
    gain_sums = jnp.concatenate([grad_g_one, grad_g_two], axis=0)
    sums_attn = links.over_depth(sums_attn)
    cut = sums_ffn.shape[0] // 2
    ffn_corner = links.both(ffn_y[:cut], ffn_x[cut:])

    def stacked(own, along_x, along_y, corner, *earlier):
        mine = jnp.stack([own, along_x, along_y, jnp.concatenate(corner, axis=0)])
        return mine, links.swap(after(mine, *earlier), 1)

    sums_attn = after(sums_attn, received)
    attn_x, attn_y = links.both(sums_attn, sums_attn)
    ffn_pair = stacked(sums_ffn, ffn_x, ffn_y, ffn_corner, attn_x, attn_y)
    gain_sums = gain_sums + links.swap(after(gain_sums, attn_x, attn_y), 1)
    *attn_corner, gains_x = links.round((attn_y[:80], 2), (attn_x[80:], 4), (gain_sums, 2))
    gain_sums = gain_sums + gains_x
    attn_pair = stacked(sums_attn, attn_x, attn_y, attn_corner)
    share_gate = unpack_columns(pos, *ffn_pair, depth, 0)
    gain_sums = gain_sums + links.swap(after(gain_sums, share_gate), 4)
    gain_sums = links.cells(gain_sums).reshape(2, depth, rows)
    share_up = unpack_columns(after(pos, share_gate), *ffn_pair, depth, 1)

    def own_part(at):
        part = lax.dynamic_index_in_dim(gain_sums, at % depth, 1, keepdims=False)
        return after(part, share_up)

    own_gains = own_part(z)
    for by in range(1, depth):
        own_gains = own_gains + links.shift(own_part(z + by), by)
    share_down = unpack_rows(after(pos, share_up), *ffn_pair, d_rows, D, 2 * rows)
    share_q, share_k, share_v, share_out = unpack_attention(
        after(pos, share_down), *attn_pair, depth, rows, inner, narrow
    )
    return (
        result,
        input_grad,
        own_gains[0],
        share_q,
        share_k,
        share_v,
        share_out,
        own_gains[1],
        share_gate,
        share_up,
        share_down,
    )


def solution(mesh):
    tokens = P(("rep", "fsdp"), None)
    gain, weight = P("fsdp"), P("fsdp", None)
    return jax.shard_map(
        functools.partial(on_device, mesh.shape["rep"], mesh.shape["fsdp"]),
        mesh=mesh,
        in_specs=(tokens, gain, *[weight] * 4, gain, *[weight] * 3, tokens),
        out_specs=(tokens, tokens, gain, *[weight] * 4, gain, *[weight] * 3),
        check_vma=False,
    )
```

```python
import functools
import math

import jax
import jax.numpy as jnp
import numpy as np
from jax import lax
from jax.experimental import pallas as pl
from jax.experimental.pallas import tpu as pltpu
from jax.sharding import PartitionSpec as P

D = 1536
HEADS = 16
KV = 8
HD = 96
BF = jnp.bfloat16
F32 = jnp.float32
MiB = 1024 * 1024
ANY = pl.BlockSpec(memory_space=pl.ANY)
WHOLE = pl.BlockSpec(memory_space=pltpu.VMEM)
SCALARS = pl.BlockSpec(memory_space=pltpu.SMEM)
QUADS = 4
TILE = 256
SCALE = 1.0 / math.sqrt(HD)
PACE = 0.02


def after(value, *earlier):
    return lax.optimization_barrier((value, *earlier))[0]


def nt(a, b):
    return lax.dot_general(a, b, (((1,), (1,)), ((), ())), preferred_element_type=F32)


def tn(a, b):
    return lax.dot_general(a, b, (((0,), (0,)), ((), ())), preferred_element_type=F32)


def nn(a, b):
    return jnp.dot(a, b, preferred_element_type=F32)


def rms(values):
    return lax.rsqrt(jnp.mean(values * values, axis=-1, keepdims=True) + 1e-05)


def tile_at(i, size):
    return pl.ds(pl.multiple_of(i * size, size), size)


def call(
    kernel,
    out_shape,
    *args,
    scratch=(),
    vmem=48,
    grid=(),
    in_specs=None,
    out_specs=None,
    us=5,
    aliases=None,
):
    return pl.pallas_call(
        kernel,
        grid=grid,
        out_shape=out_shape,
        in_specs=in_specs,
        out_specs=out_specs,
        scratch_shapes=list(scratch),
        input_output_aliases=aliases or {},
        compiler_params=pltpu.CompilerParams(vmem_limit_bytes=vmem * MiB),
        cost_estimate=pl.CostEstimate(
            flops=int(us * PACE * 1.15e9), bytes_accessed=1024, transcendentals=0
        ),
    )(*args)


def shaped(shape, dtype=BF):
    return jax.ShapeDtypeStruct(shape, dtype)


class Links:
    def __init__(self, reps, depth):
        self.reps, self.depth = reps, depth
        self.rounds = [[], [], []]

    def swap(self, value, bit):
        return lax.ppermute(value, "rep", [(i, i ^ bit) for i in range(self.reps)])

    def round(self, *moves):
        earlier = self.rounds[-2] + self.rounds[-3]
        moved = [self.swap(after(value, *earlier), bit) for value, bit in moves]
        self.rounds.append(moved)
        return moved

    def both(self, along_x, along_y):
        return self.round((along_x, 2), (along_y, 4))

    def shift(self, value, by):
        return lax.ppermute(value, "fsdp", [(i, (i + by) % self.depth) for i in range(self.depth)])

    def over_depth(self, value):
        return self.cells(lax.psum_scatter(value, "fsdp", scatter_dimension=0, tiled=True)[0])

    def cells(self, value):
        if self.reps == 2 * QUADS:
            return value
        groups = [
            [cell * 2 * QUADS + i for cell in range(self.reps // (2 * QUADS))]
            for i in range(2 * QUADS)
        ]
        return lax.psum(value, "rep", axis_index_groups=groups)

    def spread(self, piece, cut):
        return Gathered(self, piece, cut)


class Summed:
    def __init__(self, links, own, along_x, along_y, corner):
        self.links, self.own, self.along_x, self.along_y = links, own, along_x, along_y
        self.first = links.both(*corner)
        self.second = links.both(along_x[0], along_y[1])

    def add(self):
        x_high = (self.along_x[1].astype(F32) + self.first[1].astype(F32)).astype(BF)
        y_low = (self.along_y[0].astype(F32) + self.first[0].astype(F32)).astype(BF)
        self.added = x_high, y_low
        self.third = self.links.both(*self.added)

    def total(self, earlier=(), more=0):
        low, high = self.own
        depth, n, m = low.shape
        n, rows = n - more, n + high.shape[1] - 2 * more

        def kernel(a, b, c, d, e, f, out, *rest):
            lows = a[0].astype(F32) + b[0].astype(F32) + c[0].astype(F32)
            highs = d[0].astype(F32) + e[0].astype(F32) + f[0].astype(F32)
            out[0, :n] = lows[:n].astype(BF)
            out[0, n:] = highs[: rows - n].astype(BF)
            if more:
                rest[0][0] = lows[n:].astype(BF)
                rest[0][1] = highs[rows - n :].astype(BF)

        def block(height):
            return pl.BlockSpec((1, height, m), lambda i: (i, 0, 0))

        outs = [shaped((depth, rows, m)), shaped((2, depth * more, m))]
        specs = [block(rows), pl.BlockSpec((2, more, m), lambda i: (0, i, 0))]
        count = 2 if more else 1
        return call(
            kernel,
            outs[:count],
            after(low, *earlier),
            self.second[0],
            self.third[1],
            high,
            self.third[0],
            self.second[1],
            grid=(depth,),
            in_specs=[block(n + more)] * 3 + [block(rows - n + more)] * 3,
            out_specs=specs[:count],
            us=5,
        )


class Gathered:
    def __init__(self, links, piece, cut):
        self.rows, self.cut, self.depth = piece.shape[0], cut, links.depth
        n, m, depth = piece.shape[0], piece.shape[1], links.depth
        self.own = lax.all_gather(piece, "fsdp", axis=0, tiled=True)
        self.links, self.shape = links, (n, m)

    def compact(self, pos):
        (n, m), depth = self.shape, self.depth

        def kernel(pos_ref, in_ref, out_ref):
            out_ref[...] = in_ref[...]

        self.remote = pl.pallas_call(
            kernel,
            grid_spec=pltpu.PrefetchScalarGridSpec(
                num_scalar_prefetch=1,
                grid=(depth - 1,),
                in_specs=[pl.BlockSpec((n, m), lambda i, at: (lax.rem(at[0] + 1 + i, depth), 0))],
                out_specs=pl.BlockSpec((n, m), lambda i, at: (i, 0)),
            ),
            out_shape=shaped(((depth - 1) * n, m)),
            cost_estimate=pl.CostEstimate(
                flops=int(4 * PACE * 1.15e9), bytes_accessed=1024, transcendentals=0
            ),
        )(pos, self.own)

    def to_plane(self):
        self.x, self.y = self.links.both(self.remote, self.remote)
        self.parts = after(self.y[: self.cut], self.x), after(self.x[self.cut :], self.y)

    def to_corner(self):
        self.corner = self.links.both(*self.parts)

    def arrays(self, rel):
        return self.corner if rel == 3 else ((self.own, self.x, self.y)[rel],)

    def segments(self, rel, low, high):
        n = self.rows
        found = []
        for i in range(self.depth - 1):
            first, last = i * n + low, i * n + high
            if rel == 0:
                found.append((0, i, low, high - low, 0))
            elif rel < 3:
                found.append((0, i, first, high - low, 0))
            else:
                if first < self.cut:
                    found.append((0, i, first, min(last, self.cut) - first, 0))
                if last > self.cut:
                    begin = max(first, self.cut)
                    found.append((1, i, begin - self.cut, last - begin, begin - first))
        return found

    def copies(self, rel, refs, z, target, stride, base, low, high):
        out = []
        for which, i, row, count, offset in self.segments(rel, low, high):
            shard = lax.rem(z + 1 + i, self.depth)
            source = pl.multiple_of(shard * self.rows + row, 16) if rel == 0 else row
            at = pl.multiple_of(shard * stride + base + offset, 16)
            out.append((refs[which].at[pl.ds(source, count), :], target.at[pl.ds(at, count), :]))
        return out


def start(copies, sems, first=0):
    made = [
        pltpu.make_async_copy(source, target, sems.at[first + i])
        for i, (source, target) in enumerate(copies)
    ]
    for copy in made:
        copy.start()
    return made


def all_parts(got):
    return [array for rel in range(QUADS) for array in got.arrays(rel)]


def whole_copies(got, refs, z, k, target, stride, low, high):
    out, at = [], 0
    for rel in range(QUADS):
        size = len(got.arrays(rel))
        base = (k ^ rel) * (high - low)
        out += got.copies(rel, refs[at : at + size], z, target, stride, base, low, high)
        at += size
    return out


def n_copies(got, low, high, rels=range(QUADS)):
    return sum(len(got.segments(rel, low, high)) for rel in rels)


def tables(length):
    freq = 10000.0 ** (-np.arange(0, HD, 2) / HD)
    angle = np.arange(length)[:, None] * freq[None, :]
    cosine, sine = np.cos(angle), np.sin(angle)
    none = np.zeros_like(sine)

    def four(a, b):
        return jnp.asarray(np.concatenate([a, b] * 4, axis=1), F32)

    return four(cosine, cosine), four(-sine, none), four(none, sine)


def rotated(u, cosine, right, left, sign):
    width = u.shape[1]
    turned = pltpu.roll(u, width - HD // 2, 1) * right + pltpu.roll(u, HD // 2, 1) * left
    return u * cosine + sign * turned


def project(pos, pair, gain, got, shard, turns):
    length, width = pair[0].shape
    cols = shard.shape[1]
    rows = shard.shape[0]
    parts = all_parts(got)
    narrow = cols // 4
    high = rows // QUADS
    copies_in = 3 + n_copies(got, 0, high)

    def kernel(pos_ref, gain_ref, cos_ref, right_ref, left_ref, ta, tb, shard_ref, *refs):
        part_refs = refs[: len(parts)]
        normed, q, key, value, weight, toks, sems = refs[len(parts) :]
        z, k = pos_ref[0], pos_ref[1]
        first = start(
            [(ta, toks.at[pl.ds(0, length), :]), (tb, toks.at[pl.ds(length, length), :])], sems
        )
        second = start(
            [(shard_ref, weight.at[pl.ds(pl.multiple_of(z * rows, 16), rows), :])]
            + whole_copies(got, part_refs, z, k, weight, rows, 0, high),
            sems,
            2,
        )
        for copy in first:
            copy.wait()

        def norm(i, _):
            at = tile_at(i, TILE)
            x = toks[at, :].astype(F32)
            normed[at, :] = (x * rms(x) * gain_ref[...]).astype(BF)
            return 0

        lax.fori_loop(0, 2 * length // TILE, norm, 0)
        for copy in second:
            copy.wait()

        def body(i, _):
            at = tile_at(i, TILE)
            place = tile_at(lax.rem(i, length // TILE), TILE)
            out = nn(normed[at, :], weight[...])
            cosine, right, left = cos_ref[place, :], right_ref[place, :], left_ref[place, :]
            for t in range(2):
                u = out[:, t * narrow : (t + 1) * narrow]
                q[at, t * narrow : (t + 1) * narrow] = rotated(
                    u, cosine, right, left, 1.0
                ).astype(BF)
            key[at, :] = rotated(
                out[:, 2 * narrow : 3 * narrow], cosine, right, left, 1.0
            ).astype(BF)
            value[at, :] = out[:, 3 * narrow :].astype(BF)
            return 0

        lax.fori_loop(0, 2 * length // TILE, body, 0)

    return call(
        kernel,
        [
            shaped((2 * length, width)),
            shaped((2 * length, 2 * narrow)),
            shaped((2 * length, narrow)),
            shaped((2 * length, narrow)),
            shaped((width, cols)),
        ],
        pos,
        gain,
        *turns,
        *pair,
        shard,
        *parts,
        in_specs=[SCALARS] + [WHOLE] * 4 + [ANY] * (3 + len(parts)),
        out_specs=[WHOLE] * 5,
        scratch=[pltpu.VMEM((2 * length, width), BF), pltpu.SemaphoreType.DMA((copies_in,))],
        us=13,
    )


def masked(scores, first):
    keys = lax.broadcasted_iota(jnp.int32, scores.shape, 0)
    queries = lax.broadcasted_iota(jnp.int32, scores.shape, 1) + first
    return jnp.where(keys <= queries, scores, -1e30)


def attend(q, key, value):
    length = q.shape[0] // 2
    heads, groups = q.shape[1] // HD, key.shape[1] // HD

    def kernel(q_ref, k_ref, v_ref, o_ref, lse_ref):
        for g in range(groups):
            keys = k_ref[:, g * HD : (g + 1) * HD]
            turned = v_ref[:, g * HD : (g + 1) * HD].T
            for j in range(g * heads // groups, (g + 1) * heads // groups):
                for t in range(length // TILE):
                    at = slice(t * TILE, (t + 1) * TILE)
                    reach = (t + 1) * TILE
                    s = nt(keys[:reach], q_ref[at, j * HD : (j + 1) * HD]) * SCALE
                    s = masked(s, t * TILE)
                    peak = jnp.max(s, axis=0, keepdims=True)
                    e = jnp.exp(s - peak)
                    total = jnp.sum(e, axis=0, keepdims=True)
                    lse = peak + jnp.log(total)
                    p = (e * (1.0 / total)).astype(BF)
                    lse_ref[0, j : j + 1, at] = lse
                    o_ref[at, j * HD : (j + 1) * HD] = nn(turned[:, :reach], p).T.astype(BF)

    return call(
        kernel,
        [shaped(q.shape), shaped((2, heads, length), F32)],
        q,
        key,
        value,
        grid=(2,),
        in_specs=[
            pl.BlockSpec((length, q.shape[1]), lambda i: (i, 0)),
            pl.BlockSpec((length, key.shape[1]), lambda i: (i, 0)),
            pl.BlockSpec((length, key.shape[1]), lambda i: (i, 0)),
        ],
        out_specs=[
            pl.BlockSpec((length, q.shape[1]), lambda i: (i, 0)),
            pl.BlockSpec((1, heads, length), lambda i: (i, 0, 0)),
        ],
        us=10,
    )


def attend_back(q, key, value, lse, d_mixed, turns):
    length = q.shape[0] // 2
    heads, groups = q.shape[1] // HD, key.shape[1] // HD
    inner, narrow = q.shape[1], key.shape[1]

    def kernel(q_ref, k_ref, v_ref, lse_ref, do_ref, cos_ref, right_ref, left_ref, out, dq, dk):
        for g in range(groups):
            keys = k_ref[:, g * HD : (g + 1) * HD]
            values = v_ref[:, g * HD : (g + 1) * HD]
            turned = keys.T
            d_key = [jnp.zeros((TILE, HD), F32) for _ in range(length // TILE)]
            d_value = [jnp.zeros((TILE, HD), F32) for _ in range(length // TILE)]
            for j in range(g * heads // groups, (g + 1) * heads // groups):
                for t in range(length // TILE):
                    at = slice(t * TILE, (t + 1) * TILE)
                    reach = (t + 1) * TILE
                    queries = q_ref[at, j * HD : (j + 1) * HD]
                    upstream = do_ref[at, j * HD : (j + 1) * HD]
                    s = masked(nt(keys[:reach], queries) * SCALE, t * TILE)
                    p = jnp.exp(s - lse_ref[0, j : j + 1, at])
                    dp = nt(values[:reach], upstream)
                    centre = jnp.sum(p * dp, axis=0, keepdims=True)
                    ds = (p * (dp - centre)).astype(BF)
                    from_values = nn(p.astype(BF), upstream)
                    from_keys = nn(ds, queries)
                    for i in range(t + 1):
                        rows = slice(i * TILE, (i + 1) * TILE)
                        d_value[i] = d_value[i] + from_values[rows]
                        d_key[i] = d_key[i] + from_keys[rows]
                    dq[at, j * HD : (j + 1) * HD] = nn(turned[:, :reach], ds).T * SCALE
            for i in range(length // TILE):
                rows = slice(i * TILE, (i + 1) * TILE)
                dk[rows, g * HD : (g + 1) * HD] = d_key[i] * SCALE
                first = inner + narrow + g * HD
                out[rows, first : first + HD] = d_value[i].astype(BF)
        cosine, right, left = cos_ref[...], right_ref[...], left_ref[...]
        for t in range(inner // narrow):
            cols = slice(t * narrow, (t + 1) * narrow)
            out[:, cols] = rotated(dq[:, cols], cosine, right, left, -1.0).astype(BF)
        out[:, inner : inner + narrow] = rotated(dk[...], cosine, right, left, -1.0).astype(BF)

    def block(cols):
        return pl.BlockSpec((length, cols), lambda i: (i, 0))

    table = pl.BlockSpec(turns[0].shape, lambda i: (0, 0))
    return call(
        kernel,
        shaped((2 * length, inner + 2 * narrow)),
        q,
        key,
        value,
        lse,
        d_mixed,
        *turns,
        grid=(2,),
        in_specs=[
            block(inner),
            block(narrow),
            block(narrow),
            pl.BlockSpec((1, heads, length), lambda i: (i, 0, 0)),
            block(inner),
            table,
            table,
            table,
        ],
        out_specs=block(inner + 2 * narrow),
        scratch=[pltpu.VMEM((length, inner), F32), pltpu.VMEM((length, narrow), F32)],
        us=17,
    )


def mix(pos, mixed, got, shard):
    tokens, inner = mixed.shape
    width = shard.shape[1]
    rows = shard.shape[0]
    high = got.rows
    low = high - rows // QUADS
    parts = all_parts(got)

    def kernel(pos_ref, mixed_ref, shard_ref, *refs):
        part_refs = refs[: len(parts)]
        other, mine, weight, sems = refs[len(parts) :]
        z, k = pos_ref[0], pos_ref[1]
        copies = start(
            [(shard_ref, weight.at[pl.ds(pl.multiple_of(z * rows, 16), rows), :])]
            + whole_copies(got, part_refs, z, k, weight, rows, low, high),
            sems,
        )
        for copy in copies:
            copy.wait()
        for i in range(tokens // 2 // TILE):
            at = slice(i * TILE, (i + 1) * TILE)
            there = slice(tokens // 2 + i * TILE, tokens // 2 + (i + 1) * TILE)
            other[at, :] = nn(mixed_ref[there, :], weight[...]).astype(BF)
            mine[at, :] = nn(mixed_ref[at, :], weight[...])

    return call(
        kernel,
        [
            shaped((tokens // 2, width)),
            shaped((tokens // 2, width), F32),
            shaped((inner, width)),
        ],
        pos,
        mixed,
        shard,
        *parts,
        in_specs=[SCALARS, WHOLE] + [ANY] * (1 + len(parts)),
        out_specs=[WHOLE] * 3,
        scratch=[pltpu.SemaphoreType.DMA((1 + n_copies(got, low, high),))],
        us=8,
    )


def residual_norm(tokens, mine, received, gain):
    length, width = tokens.shape

    def kernel(x, a, b, gain_ref, hidden, normed):
        h = x[...].astype(F32) + a[...] + b[...].astype(F32)
        hidden[...] = h
        normed[...] = (h * rms(h) * gain_ref[...]).astype(BF)

    block = pl.BlockSpec((TILE, width), lambda i: (i, 0))
    return call(
        kernel,
        [shaped((length, width), F32), shaped((length, width))],
        tokens,
        mine,
        received,
        gain,
        grid=(length // TILE,),
        in_specs=[block, block, block, pl.BlockSpec((1, width), lambda i: (0, 0))],
        out_specs=[block, block],
        us=4,
    )


def norm_back(mine, received, values, residual, gain, rounded):
    length, width = values.shape

    def kernel(a, b, values_ref, residual_ref, gain_ref, grad, gain_grad, *low):
        x = values_ref[...].astype(F32)
        factor = rms(x)
        normed = x * factor
        upstream = a[...] + b[...].astype(F32)
        part = jnp.sum(upstream * normed, axis=0, keepdims=True)

        @pl.when(pl.program_id(0) == 0)
        def _():
            gain_grad[...] = part

        @pl.when(pl.program_id(0) > 0)
        def _():
            gain_grad[...] += part

        scaled = upstream * gain_ref[...]
        inside = scaled - normed * jnp.mean(scaled * normed, axis=-1, keepdims=True)
        total = residual_ref[...].astype(F32) + factor * inside
        grad[...] = total
        if low:
            low[0][...] = total.astype(BF)

    block = pl.BlockSpec((TILE, width), lambda i: (i, 0))
    line = pl.BlockSpec((1, width), lambda i: (0, 0))
    return call(
        kernel,
        [shaped((length, width), F32), shaped((1, width), F32)]
        + [shaped((length, width))] * rounded,
        mine,
        received,
        values,
        residual,
        gain,
        grid=(length // TILE,),
        in_specs=[block] * 4 + [line],
        out_specs=[block, line] + [block] * rounded,
        us=5,
    )


def weight_copies(pos_ref, rel, got, refs, shard_ref, target):
    z, k, c = pos_ref[0], pos_ref[1], pos_ref[2]
    if rel == 0:
        return [(refs[0], target)]
    depth, rows = got.depth, got.rows
    j = k ^ rel
    at = pl.ds(pl.multiple_of(z * rows, 16), rows)
    if shard_ref.shape[0] == rows:
        seg = target.shape[1] // depth
        copies = []
        for s in range(depth):
            col = pl.multiple_of(((s * 2 + c) * QUADS + j) * seg, 128)
            copies.append(
                (shard_ref.at[:, pl.ds(col, seg)], target.at[at, pl.ds(s * seg, seg)])
            )
    else:
        row = pl.multiple_of((c * QUADS + j) * rows, 16)
        copies = [(shard_ref.at[pl.ds(row, rows), :], target.at[at, :])]
    return copies + got.copies(rel, refs, z, target, rows, 0, 0, rows)


def count_copies(rel, got, columns):
    return 1 if rel == 0 else (got.depth if columns else 1) + n_copies(got, 0, got.rows, [rel])


class Weights:
    def __init__(self, shards, gots, columns, rels=range(QUADS)):
        self.shards, self.gots, self.columns, self.rels = shards, gots, columns, rels
        self.operands = list(shards)
        self.places = {}
        for i, got in enumerate(gots):
            for rel in rels:
                arrays = got.arrays(rel)
                self.places[i, rel] = (len(self.operands), len(arrays))
                self.operands += arrays
        self.total = sum(
            count_copies(rel, got, col) for got, col in zip(gots, columns) for rel in rels
        )
        self.scratch = [pltpu.VMEM((len(rels), *got.own.shape), BF) for got in gots]

    def start(self, pos_ref, refs, targets, sems, first):
        begun = []
        for slot, rel in enumerate(self.rels):
            copies = []
            for i, got in enumerate(self.gots):
                at, count = self.places[i, rel]
                copies += weight_copies(
                    pos_ref, rel, got, refs[at : at + count], refs[i], targets[i].at[slot]
                )
            begun.append(start(copies, sems, first))
            first += len(copies)
        return begun


def wait(copies):
    for copy in copies:
        copy.wait()


def ffn_forward(pos, rels, n_two, d_out, shards, gots, deep, whole=False):
    weights = Weights(shards, gots, (True, True, False), rels)
    length, width = n_two[0].shape
    tokens = 2 * length
    cols = gots[0].own.shape[1]
    depth, rows = gots[2].depth, gots[2].rows
    given = [] if deep is None else [deep]
    count = len(weights.operands)
    n = len(rels)
    tile = 2 * TILE

    def kernel(pos_ref, na, nb, ya, yb, *refs):
        operands, refs = refs[:count], refs[count + len(given) :]
        acts, dgus, grads = refs[:n], refs[n : 2 * n], refs[2 * n]
        extra, refs = refs[2 * n + 1 : 2 * n + 1 + 2 * whole], refs[2 * n + 1 + 2 * whole :]
        n_all, y_all, w_gate, w_up, w_down, act, dgu, made, sems = refs[:9]
        first = start(
            [
                (na, n_all.at[pl.ds(0, length), :]),
                (nb, n_all.at[pl.ds(length, length), :]),
                (ya, y_all.at[pl.ds(0, length), :]),
                (yb, y_all.at[pl.ds(length, length), :]),
            ],
            sems,
        )
        begun = weights.start(pos_ref, operands, (w_gate, w_up, w_down), sems, 4)
        written = []
        for slot, rel in enumerate(rels):
            wait(begun[slot])
            for i in range(tokens // tile):
                if slot == 0:
                    wait(first[i::2])
                at = slice(i * tile, (i + 1) * tile)
                normed, grad = n_all[at, :], y_all[at, :]
                gated = nn(normed, w_gate[slot])
                upper = nn(normed, w_up[slot])
                d_act = nt(grad, w_down[slot])
                sig = 1.0 / (1.0 + jnp.exp(-gated))
                silu = gated * sig
                act[slot, at, :] = (silu * upper).astype(BF)
                dgu[slot, at, :cols] = (
                    d_act * upper * sig * (1.0 + gated * (1.0 - sig))
                ).astype(BF)
                dgu[slot, at, cols:] = (d_act * silu).astype(BF)
            if whole and slot == 0:
                turned, sides = refs[9:]
                for s in range(depth):
                    at = slice(s * (width // depth), (s + 1) * (width // depth))
                    turned[at, :] = n_all[:, at].T
                for part in range(2):
                    out = nn(turned[...], dgu[slot, :, part * cols : (part + 1) * cols])
                    for s in range(depth):
                        at = slice(s * (width // depth), (s + 1) * (width // depth))
                        sides[part, s] = out[at].astype(BF)
                    written += start(
                        [(sides.at[part], extra[part])], sems, 4 + weights.total + 3 * n + part
                    )
            at = 4 + weights.total + 3 * slot
            written += start([(act.at[slot], acts[slot]), (dgu.at[slot], dgus[slot])], sems, at)

            def grad(s, _, slot=slot):
                made[slot, s] = tn(act[slot, :, tile_at(s, rows)], y_all[...]).astype(BF)
                return 0

            lax.fori_loop(0, depth, grad, 0)
            written += start([(made.at[slot], grads.at[:, rel])], sems, at + 2)
        wait(written)

    made = call(
        kernel,
        [shaped((tokens, cols))] * n
        + [shaped((tokens, 2 * cols))] * n
        + [shaped((depth, QUADS, rows, width))]
        + [shaped((depth, width // depth, cols))] * (2 * whole),
        pos,
        *n_two,
        *d_out,
        *weights.operands,
        *given,
        in_specs=[SCALARS] + [ANY] * (4 + count + len(given)),
        out_specs=[ANY] * (2 * n + 1 + 2 * whole),
        scratch=[
            pltpu.VMEM((tokens, width), BF),
            pltpu.VMEM((tokens, width), BF),
            *weights.scratch,
            pltpu.VMEM((n, tokens, cols), BF),
            pltpu.VMEM((n, tokens, 2 * cols), BF),
            pltpu.VMEM((n, depth, rows, width), BF),
            pltpu.SemaphoreType.DMA((4 + weights.total + 3 * n + 2,)),
        ]
        + [pltpu.VMEM((width, tokens), BF), pltpu.VMEM((2, depth, width // depth, cols), BF)]
        * whole,
        vmem=56,
        us=3 + 9 * n,
        aliases={5 + count: 2 * n} if given else None,
    )
    return made[:n], made[n : 2 * n], made[2 * n], made[2 * n + 1 :]


def ffn_grads(n_two, dgus, depth):
    length, width = n_two[0].shape
    tokens = 2 * length
    rows = width // depth
    cols = dgus[0].shape[1] // 2
    n = len(dgus)

    def kernel(na, nb, *refs):
        ins, outs, refs = refs[:n], refs[n : 3 * n], refs[3 * n :]
        n_all, dgu, turned, made, sems = refs
        first = start(
            [
                (na, n_all.at[pl.ds(0, length), :]),
                (nb, n_all.at[pl.ds(length, length), :]),
                *[(ins[rel], dgu.at[rel]) for rel in range(n)],
            ],
            sems,
        )
        wait(first[:2])
        for s in range(depth):
            at = slice(s * rows, (s + 1) * rows)
            turned[at, :] = n_all[:, at].T
        written = [[], []]
        for rel in range(n):
            first[2 + rel].wait()
            for part in range(2):
                wait(written[part])
                grads = nn(turned[...], dgu[rel, :, part * cols : (part + 1) * cols])
                for s in range(depth):
                    made[part, s] = grads[s * rows : (s + 1) * rows].astype(BF)
                written[part] = start(
                    [(made.at[part], outs[2 * rel + part])], sems, 2 + n + part
                )
        wait(written[0] + written[1])

    made = call(
        kernel,
        [shaped((depth, rows, cols))] * (2 * n),
        *n_two,
        *dgus,
        in_specs=[ANY] * (2 + n),
        out_specs=[ANY] * (2 * n),
        scratch=[
            pltpu.VMEM((tokens, width), BF),
            pltpu.VMEM((n, tokens, 2 * cols), BF),
            pltpu.VMEM((width, tokens), BF),
            pltpu.VMEM((2, depth, rows, cols), BF),
            pltpu.SemaphoreType.DMA((4 + n,)),
        ],
        us=16,
    )
    return [made[2 * rel : 2 * rel + 2] for rel in range(n)]


def ffn_product(pos, lefts, shards, gots, transposed):
    weights = Weights(shards, gots, (transposed,) * len(gots))
    tokens = lefts[0].shape[0]
    half = tokens // 2
    cols = lefts[0].shape[1] // len(gots)
    width = gots[0].own.shape[0] if transposed else gots[0].own.shape[1]
    count = len(weights.operands)

    def kernel(pos_ref, *refs):
        ins, operands, refs = refs[:QUADS], refs[QUADS : QUADS + count], refs[QUADS + count :]
        other, mine, refs = refs[0], refs[1], refs[2:]
        targets, (left, total, sems) = refs[: len(gots)], refs[len(gots) :]
        first = start([(ins[rel], left.at[rel]) for rel in range(QUADS)], sems)
        begun = weights.start(pos_ref, operands, targets, sems, QUADS)
        for rel in range(QUADS):
            first[rel].wait()
            wait(begun[rel])

            def body(i, _, rel=rel):
                at = tile_at(i, 2 * TILE)
                part = None if rel == 0 else total[at, :]
                for n, target in enumerate(targets):
                    term = (nt if transposed else nn)(
                        left[rel, at, n * cols : (n + 1) * cols], target[rel]
                    )
                    part = term if part is None else part + term
                total[at, :] = part
                return 0

            lax.fori_loop(0, tokens // (2 * TILE), body, 0)
        other[...] = total[half:, :].astype(BF)
        mine[...] = total[:half, :]

    return call(
        kernel,
        [shaped((half, width)), shaped((half, width), F32)],
        pos,
        *lefts,
        *weights.operands,
        in_specs=[SCALARS] + [ANY] * (QUADS + count),
        out_specs=[WHOLE] * 2,
        scratch=[
            *weights.scratch,
            pltpu.VMEM((QUADS, tokens, len(gots) * cols), BF),
            pltpu.VMEM((tokens, width), F32),
            pltpu.SemaphoreType.DMA((QUADS + weights.total,)),
        ],
        vmem=56,
        us=20,
    )


def rows_product(lefts, rights, half, transposed, dtype, us):
    rows = lefts[0].shape[0] // 2
    per = len(rights) // len(lefts)
    width = rights[0].shape[0] if transposed else rights[0].shape[1]
    depth = rights[0].shape[1] if transposed else rights[0].shape[0]
    steps = rows // TILE

    def kernel(*refs):
        left, right, out = refs[: len(lefts)], refs[len(lefts) : -1], refs[-1]
        total = None
        for i, ref in enumerate(right):
            part = left[i // per][:, (i % per) * depth : (i % per + 1) * depth]
            term = (nt if transposed else nn)(part, ref[...])
            total = term if total is None else total + term
        out[...] = total.astype(dtype)

    return call(
        kernel,
        shaped((rows, width), dtype),
        *lefts,
        *rights,
        grid=(steps,),
        in_specs=[
            pl.BlockSpec((TILE, left.shape[1]), lambda i: (i + half * steps, 0)) for left in lefts
        ]
        + [pl.BlockSpec(right.shape, lambda i: (0, 0)) for right in rights],
        out_specs=pl.BlockSpec((TILE, width), lambda i: (i, 0)),
        vmem=56,
        us=us,
    )


def mix_back(low, other, mixed, weight):
    length, width = low.shape
    inner = mixed.shape[1]

    def kernel(a, b, mixed_ref, weight_ref, d_mixed, grad):
        for i in range(2 * length // TILE):
            at = slice(i * TILE, (i + 1) * TILE)
            part = a if i < length // TILE else b
            first = i * TILE % length
            d_mixed[at, :] = nt(part[first : first + TILE, :], weight_ref[...]).astype(BF)

        def body(i, _):
            at = tile_at(i, TILE)
            grad[at, :] = (
                tn(mixed_ref[:length, at], a[...]) + tn(mixed_ref[length:, at], b[...])
            ).astype(BF)
            return 0

        lax.fori_loop(0, inner // TILE, body, 0)

    return call(
        kernel,
        [shaped((2 * length, inner)), shaped((inner, width))],
        low,
        other,
        mixed,
        weight,
        in_specs=[WHOLE] * 4,
        out_specs=[WHOLE] * 2,
        us=10,
    )


def attention_grads(links, pos, normed, d_qkv, grad_out, deep, depth, rows, low):
    width, cols = normed.shape[1], d_qkv.shape[1]
    quarter = rows // QUADS
    small = quarter // 2
    high = quarter - low + small
    more = deep.shape[1] // (2 * depth)

    def kernel(pos_ref, normed_ref, d_ref, out_ref, deep_ref, *refs):
        outs, tile = refs[:-1], refs[-1]
        k = pos_ref[1]

        def body(s, _):
            tile[...] = tn(normed_ref[:, tile_at(s, rows)], d_ref[...]).astype(BF)
            for rel in range(QUADS):
                j = k ^ rel
                first = pl.multiple_of(j * quarter, 16)
                to_low, to_high = outs[2 * rel : 2 * rel + 2]
                to_low[s, :low] = tile[pl.ds(first, low), :]
                to_high[s, : quarter - low] = tile[pl.ds(first + low, quarter - low), :]
                at = pl.multiple_of(s * (rows // 2) + j * small, 16)
                to_high[s, quarter - low : high] = out_ref[pl.ds(at, small), :]
                at = pl.multiple_of(s * more, 16)
                to_low[s, low:] = deep_ref[rel, pl.ds(at, more), :]
                to_high[s, high:] = deep_ref[rel, pl.ds(at + depth * more, more), :]
            return 0

        lax.fori_loop(0, depth, body, 0)

    made = call(
        kernel,
        [shaped((depth, n + more, cols)) for _ in range(QUADS) for n in (low, high)],
        pos,
        normed,
        d_qkv,
        grad_out,
        deep,
        in_specs=[SCALARS] + [WHOLE] * 4,
        out_specs=[WHOLE] * (2 * QUADS),
        scratch=[pltpu.VMEM((rows, cols), BF)],
        us=10,
    )
    return Summed(links, *[made[2 * rel : 2 * rel + 2] for rel in range(QUADS)])


def unpack_columns(pos, mine, other, depth, half):
    cols = mine.shape[2]
    rows = D // depth
    seg = cols // depth
    width = cols * 2 * QUADS
    tile = 128
    steps = rows // tile

    def kernel(pos_ref, a, b, out):
        k, c = pos_ref[1], pos_ref[2]
        for ref, core in ((a, c), (b, 1 - c)):
            for rel in range(QUADS):
                block = core * QUADS + (k ^ rel)
                for s in range(depth):
                    at = pl.multiple_of((s * 2 * QUADS + block) * seg, 128)
                    out[:, pl.ds(at, seg)] = ref[rel, :, s * seg : (s + 1) * seg].astype(F32)

    spec = pl.BlockSpec((QUADS, tile, cols), lambda i: (0, i + half * steps, 0))
    return call(
        kernel,
        shaped((rows, width), F32),
        pos,
        mine,
        other,
        grid=(steps,),
        in_specs=[SCALARS, spec, spec],
        out_specs=pl.BlockSpec((tile, width), lambda i: (i, 0)),
        us=4,
    )


def unpack_rows(pos, mine, other, rows, width, first):
    tile = mine.shape[2]

    def kernel(pos_ref, a, b, out):
        k, c = pos_ref[1], pos_ref[2]
        for ref, core in ((a, c), (b, 1 - c)):
            for rel in range(QUADS):
                at = pl.multiple_of((core * QUADS + (k ^ rel)) * rows, 8)
                out[pl.ds(at, rows), :] = ref[rel].astype(F32)

    spec = pl.BlockSpec((QUADS, rows, tile), lambda i: (0, first // rows + i, 0))
    return call(
        kernel,
        shaped((2 * QUADS * rows, width), F32),
        pos,
        mine,
        other,
        grid=(width // tile,),
        in_specs=[SCALARS, spec, spec],
        out_specs=pl.BlockSpec((2 * QUADS * rows, tile), lambda i: (0, i)),
        us=5,
    )


def unpack_attention(pos, mine, other, depth, rows, inner, narrow):
    quarter = rows // QUADS
    small = quarter // 2

    def kernel(pos_ref, a, b, *outs):
        k, c = pos_ref[1], pos_ref[2]

        def place(first, second):
            for core, ref in ((0, first), (1, second)):
                for rel in range(QUADS):
                    j = k ^ rel
                    at = pl.ds(pl.multiple_of(j * quarter, 8), quarter)
                    cols = 0
                    for out, width in zip(outs[:3], (inner, narrow, narrow)):
                        seg = width // depth
                        for s in range(depth):
                            to = (2 * s + core) * seg
                            out[at, to : to + seg] = ref[
                                rel, :quarter, cols : cols + seg
                            ].astype(F32)
                            cols += seg
                    at = pl.ds(pl.multiple_of(core * (rows // 2) + j * small, 8), small)
                    outs[3][at, :] = ref[rel, quarter:, :].astype(F32)

        @pl.when(c == 0)
        def _():
            place(a, b)

        @pl.when(c == 1)
        def _():
            place(b, a)

    return call(
        kernel,
        [
            shaped((rows, 2 * inner), F32),
            shaped((rows, 2 * narrow), F32),
            shaped((rows, 2 * narrow), F32),
            shaped((rows, 2 * inner), F32),
        ],
        pos,
        mine,
        other,
        in_specs=[SCALARS] + [WHOLE] * 2,
        out_specs=[WHOLE] * 4,
        us=6,
    )


def on_device(
    reps,
    depth,
    tokens,
    gain_attn,
    w_query,
    w_key,
    w_value,
    w_out,
    gain_ffn,
    w_gate,
    w_up,
    w_down,
    cotangent,
):
    links = Links(reps, depth)
    z = lax.axis_index("fsdp")
    r = lax.axis_index("rep")
    c = r % 2
    k = (r // 2) % QUADS
    pos = jnp.stack([z, k, c]).astype(jnp.int32)
    length = tokens.shape[0]
    rows = w_query.shape[0]
    quarter = rows // QUADS
    small = quarter // 2
    inner = D // 2
    narrow = inner // (HEADS // KV)

    def core_columns(weight):
        split = weight.reshape(rows, depth, 2, weight.shape[1] // (2 * depth))
        return lax.dynamic_index_in_dim(split, c, 2, keepdims=False).reshape(rows, -1)

    shard_qkv = jnp.concatenate([core_columns(i) for i in (w_query, w_key, w_value)], axis=1)
    shard_out = lax.dynamic_slice_in_dim(w_out, c * (rows // 2), rows // 2, 0)
    piece_qkv = lax.dynamic_slice_in_dim(shard_qkv, k * quarter, quarter, 0)
    piece_out = lax.dynamic_slice_in_dim(shard_out, k * small, small, 0)
    seg = w_gate.shape[1] // (depth * 2 * QUADS)
    d_rows = w_down.shape[0] // (2 * QUADS)

    def block_columns(weight):
        return jnp.concatenate(
            [
                lax.dynamic_slice_in_dim(weight, ((s * 2 + c) * QUADS + k) * seg, seg, 1)
                for s in range(depth)
            ],
            axis=1,
        )

    piece_gate, piece_up = block_columns(w_gate), block_columns(w_up)
    piece_down = lax.dynamic_slice_in_dim(w_down, (c * QUADS + k) * d_rows, d_rows, 0)

    gains = jnp.stack([gain_attn, gain_ffn])
    gains = jnp.stack([gains] + [links.shift(gains, by) for by in range(1, depth)])
    gains = jnp.take(gains, (z - jnp.arange(depth)) % depth, axis=0)
    g_one = gains[:, 0].reshape(1, -1).astype(F32)
    g_two = gains[:, 1].reshape(1, -1).astype(F32)
    token_pair = (tokens, links.swap(tokens, 1))
    d_pair = (cotangent, links.swap(cotangent, 1))
    turns = tables(length)

    piece = jnp.concatenate([piece_qkv, piece_out], axis=0)
    early = after(pos, token_pair[1], d_pair[1])
    got_attn = links.spread(piece, 224)
    got_gate = links.spread(piece_gate, 3 * rows // 2)
    got_up = links.spread(after(piece_up, got_attn.own), 3 * rows // 2)
    got_down = links.spread(after(piece_down, got_gate.own), 3 * d_rows // 2)
    got_attn.compact(early)
    got_attn.to_plane()
    got_attn.to_corner()
    got_gate.compact(after(pos, *got_attn.corner, g_one, g_two))
    got_gate.to_plane()
    n_one, q, key, value, wqkv = project(pos, token_pair, g_one, got_attn, shard_qkv, turns)
    got_up.compact(after(pos, q))
    got_up.to_plane()
    got_gate.parts = [after(i, got_up.remote) for i in got_gate.parts]
    got_gate.to_corner()

    mixed, lse = attend(q, key, value)
    got_down.compact(after(pos, lse))
    got_down.to_plane()
    got_up.to_corner()
    got_down.to_corner()
    to_other, mine, wo = mix(pos, mixed, got_attn, shard_out)
    ready = after(to_other, *got_gate.corner, got_up.x, got_up.y, got_down.remote)
    hidden, n_two = residual_norm(tokens, mine, links.swap(ready, 1), g_two)

    n_pair = (n_two, links.swap(n_two, 1))
    shards, gots = (w_gate, w_up, w_down), (got_gate, got_up, got_down)
    acts, dgus, deep, _ = ffn_forward(pos, (0, 1, 2), n_pair, d_pair, shards, gots, None)
    at = after(pos, dgus[-1])
    act, dgu, deep, corner = ffn_forward(at, (3,), n_pair, d_pair, shards, gots, deep, True)
    acts, dgus = [*acts, *act], [*dgus, *dgu]
    deep_sum = links.over_depth(deep)
    half = d_rows // 2
    others = ffn_grads(n_pair, [after(i, corner[0]) for i in dgus[:3]], depth)
    wide = Summed(links, *others, corner)
    lefts = [after(i, wide.own[0]) for i in dgus]
    to_other, mine = ffn_product(pos, lefts, (w_gate, w_up), (got_gate, got_up), True)
    wide.add()
    acts = [after(i, to_other, *wide.added) for i in acts]
    out_other, out_mine = ffn_product(pos, acts, (w_down,), (got_down,), False)
    received = links.swap(to_other, 1)
    mine = after(mine, out_mine, *wide.second)
    d_hidden, grad_g_two, low = norm_back(mine, received, hidden, cotangent, g_two, 1)

    low_pair = low, links.swap(after(low, *wide.added), 1)
    d_mixed, grad_out = mix_back(*low_pair, mixed, wo)
    d_qkv = attend_back(q, key, value, lse, d_mixed, turns)
    deep_sum = after(deep_sum, d_qkv)
    small = attention_grads(links, pos, n_one, d_qkv, grad_out, deep_sum, depth, rows, 80)
    (sums_wide,) = wide.total([small.own[0]])
    late = after(d_qkv, sums_wide)
    sums_wide = links.over_depth(sums_wide)
    to_other = rows_product([late], [wqkv], 1, True, BF, 7)
    mine = rows_product([late], [wqkv], 0, True, F32, 7)
    out_received = links.swap(after(out_other, d_hidden), 1)
    result = (hidden + out_mine + out_received.astype(F32)).astype(BF)
    small.add()
    sums_attn, sums_deep = small.total(more=half // depth)
    sums_deep = sums_deep.reshape(d_rows, -1)
    split = sums_deep.shape[1] // sums_wide.shape[1]
    sums_ffn = jnp.concatenate([sums_wide, *jnp.split(sums_deep, split, axis=1)], axis=0)
    ffn_x, ffn_y = links.both(*[after(sums_ffn, sums_attn)] * 2)
    received = links.swap(after(to_other, mine, result, ffn_x, ffn_y), 1)
    input_grad, grad_g_one = norm_back(mine, received, tokens, d_hidden, g_one, 0)
    gain_sums = jnp.concatenate([grad_g_one, grad_g_two], axis=0)
    sums_attn = links.over_depth(sums_attn)
    cut = sums_ffn.shape[0] // 2
    ffn_corner = links.both(ffn_y[:cut], ffn_x[cut:])

    def stacked(own, along_x, along_y, corner, *earlier):
        mine = jnp.stack([own, along_x, along_y, jnp.concatenate(corner, axis=0)])
        return mine, links.swap(after(mine, *earlier), 1)

    sums_attn = after(sums_attn, received)
    attn_x, attn_y = links.both(sums_attn, sums_attn)
    ffn_pair = stacked(sums_ffn, ffn_x, ffn_y, ffn_corner, attn_x, attn_y, input_grad)
    attn_corner = links.both(attn_y[:80], attn_x[80:])
    attn_pair = stacked(sums_attn, attn_x, attn_y, attn_corner)
    gain_sums = gain_sums + links.swap(after(gain_sums, attn_x, attn_y), 1)
    share_gate = unpack_columns(pos, *ffn_pair, depth, 0)
    gain_sums = gain_sums + links.swap(after(gain_sums, share_gate), 2)
    share_up = unpack_columns(after(pos, share_gate), *ffn_pair, depth, 1)
    gain_sums = gain_sums + links.swap(after(gain_sums, share_up), 4)
    gain_sums = links.cells(gain_sums).reshape(2, depth, rows)
    share_down = unpack_rows(after(pos, share_up), *ffn_pair, d_rows, D, 2 * rows)

    def own_part(at):
        part = lax.dynamic_index_in_dim(gain_sums, at % depth, 1, keepdims=False)
        return after(part, share_down)

    own_gains = own_part(z)
    for by in range(1, depth):
        own_gains = own_gains + links.shift(own_part(z + by), by)
    share_q, share_k, share_v, share_out = unpack_attention(
        after(pos, share_down), *attn_pair, depth, rows, inner, narrow
    )
    return (
        result,
        input_grad,
        own_gains[0],
        share_q,
        share_k,
        share_v,
        share_out,
        own_gains[1],
        share_gate,
        share_up,
        share_down,
    )


def solution(mesh):
    tokens = P(("rep", "fsdp"), None)
    gain, weight = P("fsdp"), P("fsdp", None)
    return jax.shard_map(
        functools.partial(on_device, mesh.shape["rep"], mesh.shape["fsdp"]),
        mesh=mesh,
        in_specs=(tokens, gain, *[weight] * 4, gain, *[weight] * 3, tokens),
        out_specs=(tokens, tokens, gain, *[weight] * 4, gain, *[weight] * 3),
        check_vma=False,
    )
```

```python
import functools
import math

import jax
import jax.numpy as jnp
import numpy as np
from jax import lax
from jax.experimental import pallas as pl
from jax.experimental.pallas import tpu as pltpu
from jax.sharding import PartitionSpec as P

D = 1536
HEADS = 16
KV = 8
HD = 96
BF = jnp.bfloat16
F32 = jnp.float32
MiB = 1024 * 1024
ANY = pl.BlockSpec(memory_space=pl.ANY)
WHOLE = pl.BlockSpec(memory_space=pltpu.VMEM)
SCALARS = pl.BlockSpec(memory_space=pltpu.SMEM)
QUADS = 4
TILE = 256
SCALE = 1.0 / math.sqrt(HD)
PACE = 0.02


def after(value, *earlier):
    return lax.optimization_barrier((value, *earlier))[0]


def nt(a, b):
    return lax.dot_general(a, b, (((1,), (1,)), ((), ())), preferred_element_type=F32)


def tn(a, b):
    return lax.dot_general(a, b, (((0,), (0,)), ((), ())), preferred_element_type=F32)


def nn(a, b):
    return jnp.dot(a, b, preferred_element_type=F32)


def rms(values):
    return lax.rsqrt(jnp.mean(values * values, axis=-1, keepdims=True) + 1e-05)


def tile_at(i, size):
    return pl.ds(pl.multiple_of(i * size, size), size)


def call(
    kernel,
    out_shape,
    *args,
    scratch=(),
    vmem=48,
    grid=(),
    in_specs=None,
    out_specs=None,
    us=5,
    aliases=None,
):
    return pl.pallas_call(
        kernel,
        grid=grid,
        out_shape=out_shape,
        in_specs=in_specs,
        out_specs=out_specs,
        scratch_shapes=list(scratch),
        input_output_aliases=aliases or {},
        compiler_params=pltpu.CompilerParams(vmem_limit_bytes=vmem * MiB),
        cost_estimate=pl.CostEstimate(
            flops=int(us * PACE * 1.15e9), bytes_accessed=1024, transcendentals=0
        ),
    )(*args)


def shaped(shape, dtype=BF):
    return jax.ShapeDtypeStruct(shape, dtype)


class Links:
    def __init__(self, reps, depth):
        self.reps, self.depth = reps, depth
        self.rounds = [[], [], []]

    def swap(self, value, bit):
        return lax.ppermute(value, "rep", [(i, i ^ bit) for i in range(self.reps)])

    def round(self, *moves):
        earlier = self.rounds[-2] + self.rounds[-3]
        moved = [self.swap(after(value, *earlier), bit) for value, bit in moves]
        self.rounds.append(moved)
        return moved

    def both(self, along_x, along_y):
        return self.round((along_x, 2), (along_y, 4))

    def shift(self, value, by):
        return lax.ppermute(value, "fsdp", [(i, (i + by) % self.depth) for i in range(self.depth)])

    def over_depth(self, value):
        return self.cells(lax.psum_scatter(value, "fsdp", scatter_dimension=0, tiled=True)[0])

    def cells(self, value):
        if self.reps == 2 * QUADS:
            return value
        groups = [
            [cell * 2 * QUADS + i for cell in range(self.reps // (2 * QUADS))]
            for i in range(2 * QUADS)
        ]
        return lax.psum(value, "rep", axis_index_groups=groups)

    def spread(self, piece, cut):
        return Gathered(self, piece, cut)


class Summed:
    def __init__(self, links, own, along_x, along_y, corner):
        self.links, self.own, self.along_x, self.along_y = links, own, along_x, along_y
        self.first = links.both(*corner)
        self.second = links.both(along_x[0], along_y[1])

    def add(self):
        x_high = (self.along_x[1].astype(F32) + self.first[1].astype(F32)).astype(BF)
        y_low = (self.along_y[0].astype(F32) + self.first[0].astype(F32)).astype(BF)
        self.added = x_high, y_low
        self.third = self.links.both(*self.added)

    def total(self, earlier=(), more=0):
        low, high = self.own
        depth, n, m = low.shape
        n, rows = n - more, n + high.shape[1] - 2 * more

        def kernel(a, b, c, d, e, f, out, *rest):
            lows = a[0].astype(F32) + b[0].astype(F32) + c[0].astype(F32)
            highs = d[0].astype(F32) + e[0].astype(F32) + f[0].astype(F32)
            out[0, :n] = lows[:n].astype(BF)
            out[0, n:] = highs[: rows - n].astype(BF)
            if more:
                rest[0][0] = lows[n:].astype(BF)
                rest[0][1] = highs[rows - n :].astype(BF)

        def block(height):
            return pl.BlockSpec((1, height, m), lambda i: (i, 0, 0))

        outs = [shaped((depth, rows, m)), shaped((2, depth * more, m))]
        specs = [block(rows), pl.BlockSpec((2, more, m), lambda i: (0, i, 0))]
        count = 2 if more else 1
        return call(
            kernel,
            outs[:count],
            after(low, *earlier),
            self.second[0],
            self.third[1],
            high,
            self.third[0],
            self.second[1],
            grid=(depth,),
            in_specs=[block(n + more)] * 3 + [block(rows - n + more)] * 3,
            out_specs=specs[:count],
            us=5,
        )


class Gathered:
    def __init__(self, links, piece, cut):
        self.rows, self.cut, self.depth = piece.shape[0], cut, links.depth
        n, m, depth = piece.shape[0], piece.shape[1], links.depth
        self.own = lax.all_gather(piece, "fsdp", axis=0, tiled=True)
        self.links, self.shape = links, (n, m)

    def compact(self, pos):
        (n, m), depth = self.shape, self.depth

        def kernel(pos_ref, in_ref, out_ref):
            out_ref[...] = in_ref[...]

        self.remote = pl.pallas_call(
            kernel,
            grid_spec=pltpu.PrefetchScalarGridSpec(
                num_scalar_prefetch=1,
                grid=(depth - 1,),
                in_specs=[pl.BlockSpec((n, m), lambda i, at: (lax.rem(at[0] + 1 + i, depth), 0))],
                out_specs=pl.BlockSpec((n, m), lambda i, at: (i, 0)),
            ),
            out_shape=shaped(((depth - 1) * n, m)),
            cost_estimate=pl.CostEstimate(
                flops=int(4 * PACE * 1.15e9), bytes_accessed=1024, transcendentals=0
            ),
        )(pos, self.own)

    def to_plane(self):
        self.x, self.y = self.links.both(self.remote, self.remote)
        self.parts = after(self.y[: self.cut], self.x), after(self.x[self.cut :], self.y)

    def to_corner(self):
        self.corner = self.links.both(*self.parts)

    def arrays(self, rel):
        return self.corner if rel == 3 else ((self.own, self.x, self.y)[rel],)

    def segments(self, rel, low, high):
        n = self.rows
        found = []
        for i in range(self.depth - 1):
            first, last = i * n + low, i * n + high
            if rel == 0:
                found.append((0, i, low, high - low, 0))
            elif rel < 3:
                found.append((0, i, first, high - low, 0))
            else:
                if first < self.cut:
                    found.append((0, i, first, min(last, self.cut) - first, 0))
                if last > self.cut:
                    begin = max(first, self.cut)
                    found.append((1, i, begin - self.cut, last - begin, begin - first))
        return found

    def copies(self, rel, refs, z, target, stride, base, low, high):
        out = []
        for which, i, row, count, offset in self.segments(rel, low, high):
            shard = lax.rem(z + 1 + i, self.depth)
            source = pl.multiple_of(shard * self.rows + row, 16) if rel == 0 else row
            at = pl.multiple_of(shard * stride + base + offset, 16)
            out.append((refs[which].at[pl.ds(source, count), :], target.at[pl.ds(at, count), :]))
        return out


def start(copies, sems, first=0):
    made = [
        pltpu.make_async_copy(source, target, sems.at[first + i])
        for i, (source, target) in enumerate(copies)
    ]
    for copy in made:
        copy.start()
    return made


def all_parts(got):
    return [array for rel in range(QUADS) for array in got.arrays(rel)]


def whole_copies(got, refs, z, k, target, stride, low, high):
    out, at = [], 0
    for rel in range(QUADS):
        size = len(got.arrays(rel))
        base = (k ^ rel) * (high - low)
        out += got.copies(rel, refs[at : at + size], z, target, stride, base, low, high)
        at += size
    return out


def n_copies(got, low, high, rels=range(QUADS)):
    return sum(len(got.segments(rel, low, high)) for rel in rels)


def tables(length):
    freq = 10000.0 ** (-np.arange(0, HD, 2) / HD)
    angle = np.arange(length)[:, None] * freq[None, :]
    cosine, sine = np.cos(angle), np.sin(angle)
    none = np.zeros_like(sine)

    def four(a, b):
        return jnp.asarray(np.concatenate([a, b] * 4, axis=1), F32)

    return four(cosine, cosine), four(-sine, none), four(none, sine)


def rotated(u, cosine, right, left, sign):
    width = u.shape[1]
    turned = pltpu.roll(u, width - HD // 2, 1) * right + pltpu.roll(u, HD // 2, 1) * left
    return u * cosine + sign * turned


def project(pos, pair, gain, got, shard, turns):
    length, width = pair[0].shape
    cols = shard.shape[1]
    rows = shard.shape[0]
    parts = all_parts(got)
    narrow = cols // 4
    high = rows // QUADS
    copies_in = 3 + n_copies(got, 0, high)

    def kernel(pos_ref, gain_ref, cos_ref, right_ref, left_ref, ta, tb, shard_ref, *refs):
        part_refs = refs[: len(parts)]
        normed, q, key, value, weight, toks, sems = refs[len(parts) :]
        z, k = pos_ref[0], pos_ref[1]
        first = start(
            [(ta, toks.at[pl.ds(0, length), :]), (tb, toks.at[pl.ds(length, length), :])], sems
        )
        second = start(
            [(shard_ref, weight.at[pl.ds(pl.multiple_of(z * rows, 16), rows), :])]
            + whole_copies(got, part_refs, z, k, weight, rows, 0, high),
            sems,
            2,
        )
        for copy in first:
            copy.wait()

        def norm(i, _):
            at = tile_at(i, TILE)
            x = toks[at, :].astype(F32)
            normed[at, :] = (x * rms(x) * gain_ref[...]).astype(BF)
            return 0

        lax.fori_loop(0, 2 * length // TILE, norm, 0)
        for copy in second:
            copy.wait()

        def body(i, _):
            at = tile_at(i, TILE)
            place = tile_at(lax.rem(i, length // TILE), TILE)
            out = nn(normed[at, :], weight[...])
            cosine, right, left = cos_ref[place, :], right_ref[place, :], left_ref[place, :]
            for t in range(2):
                u = out[:, t * narrow : (t + 1) * narrow]
                q[at, t * narrow : (t + 1) * narrow] = rotated(
                    u, cosine, right, left, 1.0
                ).astype(BF)
            key[at, :] = rotated(
                out[:, 2 * narrow : 3 * narrow], cosine, right, left, 1.0
            ).astype(BF)
            value[at, :] = out[:, 3 * narrow :].astype(BF)
            return 0

        lax.fori_loop(0, 2 * length // TILE, body, 0)

    return call(
        kernel,
        [
            shaped((2 * length, width)),
            shaped((2 * length, 2 * narrow)),
            shaped((2 * length, narrow)),
            shaped((2 * length, narrow)),
            shaped((width, cols)),
        ],
        pos,
        gain,
        *turns,
        *pair,
        shard,
        *parts,
        in_specs=[SCALARS] + [WHOLE] * 4 + [ANY] * (3 + len(parts)),
        out_specs=[WHOLE] * 5,
        scratch=[pltpu.VMEM((2 * length, width), BF), pltpu.SemaphoreType.DMA((copies_in,))],
        us=13,
    )


def masked(scores, first):
    keys = lax.broadcasted_iota(jnp.int32, scores.shape, 0)
    queries = lax.broadcasted_iota(jnp.int32, scores.shape, 1) + first
    return jnp.where(keys <= queries, scores, -1e30)


def attend(q, key, value):
    length = q.shape[0] // 2
    heads, groups = q.shape[1] // HD, key.shape[1] // HD

    def kernel(q_ref, k_ref, v_ref, o_ref, lse_ref):
        for g in range(groups):
            keys = k_ref[:, g * HD : (g + 1) * HD]
            turned = v_ref[:, g * HD : (g + 1) * HD].T
            for j in range(g * heads // groups, (g + 1) * heads // groups):
                for t in range(length // TILE):
                    at = slice(t * TILE, (t + 1) * TILE)
                    reach = (t + 1) * TILE
                    s = nt(keys[:reach], q_ref[at, j * HD : (j + 1) * HD]) * SCALE
                    s = masked(s, t * TILE)
                    peak = jnp.max(s, axis=0, keepdims=True)
                    e = jnp.exp(s - peak)
                    total = jnp.sum(e, axis=0, keepdims=True)
                    lse = peak + jnp.log(total)
                    p = (e * (1.0 / total)).astype(BF)
                    lse_ref[0, j : j + 1, at] = lse
                    o_ref[at, j * HD : (j + 1) * HD] = nn(turned[:, :reach], p).T.astype(BF)

    return call(
        kernel,
        [shaped(q.shape), shaped((2, heads, length), F32)],
        q,
        key,
        value,
        grid=(2,),
        in_specs=[
            pl.BlockSpec((length, q.shape[1]), lambda i: (i, 0)),
            pl.BlockSpec((length, key.shape[1]), lambda i: (i, 0)),
            pl.BlockSpec((length, key.shape[1]), lambda i: (i, 0)),
        ],
        out_specs=[
            pl.BlockSpec((length, q.shape[1]), lambda i: (i, 0)),
            pl.BlockSpec((1, heads, length), lambda i: (i, 0, 0)),
        ],
        us=10,
    )


def attend_back(q, key, value, lse, d_mixed, turns):
    length = q.shape[0] // 2
    heads, groups = q.shape[1] // HD, key.shape[1] // HD
    inner, narrow = q.shape[1], key.shape[1]

    def kernel(q_ref, k_ref, v_ref, lse_ref, do_ref, cos_ref, right_ref, left_ref, out, dq, dk):
        for g in range(groups):
            keys = k_ref[:, g * HD : (g + 1) * HD]
            values = v_ref[:, g * HD : (g + 1) * HD]
            turned = keys.T
            d_key = [jnp.zeros((TILE, HD), F32) for _ in range(length // TILE)]
            d_value = [jnp.zeros((TILE, HD), F32) for _ in range(length // TILE)]
            for j in range(g * heads // groups, (g + 1) * heads // groups):
                for t in range(length // TILE):
                    at = slice(t * TILE, (t + 1) * TILE)
                    reach = (t + 1) * TILE
                    queries = q_ref[at, j * HD : (j + 1) * HD]
                    upstream = do_ref[at, j * HD : (j + 1) * HD]
                    s = masked(nt(keys[:reach], queries) * SCALE, t * TILE)
                    p = jnp.exp(s - lse_ref[0, j : j + 1, at])
                    dp = nt(values[:reach], upstream)
                    centre = jnp.sum(p * dp, axis=0, keepdims=True)
                    ds = (p * (dp - centre)).astype(BF)
                    from_values = nn(p.astype(BF), upstream)
                    from_keys = nn(ds, queries)
                    for i in range(t + 1):
                        rows = slice(i * TILE, (i + 1) * TILE)
                        d_value[i] = d_value[i] + from_values[rows]
                        d_key[i] = d_key[i] + from_keys[rows]
                    dq[at, j * HD : (j + 1) * HD] = nn(turned[:, :reach], ds).T * SCALE
            for i in range(length // TILE):
                rows = slice(i * TILE, (i + 1) * TILE)
                dk[rows, g * HD : (g + 1) * HD] = d_key[i] * SCALE
                first = inner + narrow + g * HD
                out[rows, first : first + HD] = d_value[i].astype(BF)
        cosine, right, left = cos_ref[...], right_ref[...], left_ref[...]
        for t in range(inner // narrow):
            cols = slice(t * narrow, (t + 1) * narrow)
            out[:, cols] = rotated(dq[:, cols], cosine, right, left, -1.0).astype(BF)
        out[:, inner : inner + narrow] = rotated(dk[...], cosine, right, left, -1.0).astype(BF)

    def block(cols):
        return pl.BlockSpec((length, cols), lambda i: (i, 0))

    table = pl.BlockSpec(turns[0].shape, lambda i: (0, 0))
    return call(
        kernel,
        shaped((2 * length, inner + 2 * narrow)),
        q,
        key,
        value,
        lse,
        d_mixed,
        *turns,
        grid=(2,),
        in_specs=[
            block(inner),
            block(narrow),
            block(narrow),
            pl.BlockSpec((1, heads, length), lambda i: (i, 0, 0)),
            block(inner),
            table,
            table,
            table,
        ],
        out_specs=block(inner + 2 * narrow),
        scratch=[pltpu.VMEM((length, inner), F32), pltpu.VMEM((length, narrow), F32)],
        us=17,
    )


def mix(pos, mixed, got, shard):
    tokens, inner = mixed.shape
    width = shard.shape[1]
    rows = shard.shape[0]
    high = got.rows
    low = high - rows // QUADS
    parts = all_parts(got)

    def kernel(pos_ref, mixed_ref, shard_ref, *refs):
        part_refs = refs[: len(parts)]
        other, mine, weight, sems = refs[len(parts) :]
        z, k = pos_ref[0], pos_ref[1]
        copies = start(
            [(shard_ref, weight.at[pl.ds(pl.multiple_of(z * rows, 16), rows), :])]
            + whole_copies(got, part_refs, z, k, weight, rows, low, high),
            sems,
        )
        for copy in copies:
            copy.wait()
        for i in range(tokens // 2 // TILE):
            at = slice(i * TILE, (i + 1) * TILE)
            there = slice(tokens // 2 + i * TILE, tokens // 2 + (i + 1) * TILE)
            other[at, :] = nn(mixed_ref[there, :], weight[...]).astype(BF)
            mine[at, :] = nn(mixed_ref[at, :], weight[...])

    return call(
        kernel,
        [
            shaped((tokens // 2, width)),
            shaped((tokens // 2, width), F32),
            shaped((inner, width)),
        ],
        pos,
        mixed,
        shard,
        *parts,
        in_specs=[SCALARS, WHOLE] + [ANY] * (1 + len(parts)),
        out_specs=[WHOLE] * 3,
        scratch=[pltpu.SemaphoreType.DMA((1 + n_copies(got, low, high),))],
        us=8,
    )


def residual_norm(tokens, mine, received, gain):
    length, width = tokens.shape

    def kernel(x, a, b, gain_ref, hidden, normed):
        h = x[...].astype(F32) + a[...] + b[...].astype(F32)
        hidden[...] = h
        normed[...] = (h * rms(h) * gain_ref[...]).astype(BF)

    block = pl.BlockSpec((TILE, width), lambda i: (i, 0))
    return call(
        kernel,
        [shaped((length, width), F32), shaped((length, width))],
        tokens,
        mine,
        received,
        gain,
        grid=(length // TILE,),
        in_specs=[block, block, block, pl.BlockSpec((1, width), lambda i: (0, 0))],
        out_specs=[block, block],
        us=4,
    )


def norm_back(mine, received, values, residual, gain, rounded):
    length, width = values.shape

    def kernel(a, b, values_ref, residual_ref, gain_ref, grad, gain_grad, *low):
        x = values_ref[...].astype(F32)
        factor = rms(x)
        normed = x * factor
        upstream = a[...] + b[...].astype(F32)
        part = jnp.sum(upstream * normed, axis=0, keepdims=True)

        @pl.when(pl.program_id(0) == 0)
        def _():
            gain_grad[...] = part

        @pl.when(pl.program_id(0) > 0)
        def _():
            gain_grad[...] += part

        scaled = upstream * gain_ref[...]
        inside = scaled - normed * jnp.mean(scaled * normed, axis=-1, keepdims=True)
        total = residual_ref[...].astype(F32) + factor * inside
        grad[...] = total
        if low:
            low[0][...] = total.astype(BF)

    block = pl.BlockSpec((TILE, width), lambda i: (i, 0))
    line = pl.BlockSpec((1, width), lambda i: (0, 0))
    return call(
        kernel,
        [shaped((length, width), F32), shaped((1, width), F32)]
        + [shaped((length, width))] * rounded,
        mine,
        received,
        values,
        residual,
        gain,
        grid=(length // TILE,),
        in_specs=[block] * 4 + [line],
        out_specs=[block, line] + [block] * rounded,
        us=5,
    )


def weight_copies(pos_ref, rel, got, refs, shard_ref, target):
    z, k, c = pos_ref[0], pos_ref[1], pos_ref[2]
    if rel == 0:
        return [(refs[0], target)]
    depth, rows = got.depth, got.rows
    j = k ^ rel
    at = pl.ds(pl.multiple_of(z * rows, 16), rows)
    if shard_ref.shape[0] == rows:
        seg = target.shape[1] // depth
        copies = []
        for s in range(depth):
            col = pl.multiple_of(((s * 2 + c) * QUADS + j) * seg, 128)
            copies.append(
                (shard_ref.at[:, pl.ds(col, seg)], target.at[at, pl.ds(s * seg, seg)])
            )
    else:
        row = pl.multiple_of((c * QUADS + j) * rows, 16)
        copies = [(shard_ref.at[pl.ds(row, rows), :], target.at[at, :])]
    return copies + got.copies(rel, refs, z, target, rows, 0, 0, rows)


def count_copies(rel, got, columns):
    return 1 if rel == 0 else (got.depth if columns else 1) + n_copies(got, 0, got.rows, [rel])


class Weights:
    def __init__(self, shards, gots, columns, rels=range(QUADS)):
        self.shards, self.gots, self.columns, self.rels = shards, gots, columns, rels
        self.operands = list(shards)
        self.places = {}
        for i, got in enumerate(gots):
            for rel in rels:
                arrays = got.arrays(rel)
                self.places[i, rel] = (len(self.operands), len(arrays))
                self.operands += arrays
        self.total = sum(
            count_copies(rel, got, col) for got, col in zip(gots, columns) for rel in rels
        )
        self.scratch = [pltpu.VMEM((len(rels), *got.own.shape), BF) for got in gots]

    def start(self, pos_ref, refs, targets, sems, first):
        begun = []
        for slot, rel in enumerate(self.rels):
            copies = []
            for i, got in enumerate(self.gots):
                at, count = self.places[i, rel]
                copies += weight_copies(
                    pos_ref, rel, got, refs[at : at + count], refs[i], targets[i].at[slot]
                )
            begun.append(start(copies, sems, first))
            first += len(copies)
        return begun


def wait(copies):
    for copy in copies:
        copy.wait()


def ffn_forward(pos, rels, n_two, d_out, shards, gots, deep, whole=False):
    weights = Weights(shards, gots, (True, True, False), rels)
    length, width = n_two[0].shape
    tokens = 2 * length
    cols = gots[0].own.shape[1]
    depth, rows = gots[2].depth, gots[2].rows
    given = [] if deep is None else [deep]
    count = len(weights.operands)
    n = len(rels)
    tile = 2 * TILE

    def kernel(pos_ref, na, nb, ya, yb, *refs):
        operands, refs = refs[:count], refs[count + len(given) :]
        acts, dgus, grads = refs[:n], refs[n : 2 * n], refs[2 * n]
        extra, refs = refs[2 * n + 1 : 2 * n + 1 + 2 * whole], refs[2 * n + 1 + 2 * whole :]
        n_all, y_all, w_gate, w_up, w_down, act, dgu, made, sems = refs[:9]
        first = start(
            [
                (na, n_all.at[pl.ds(0, length), :]),
                (nb, n_all.at[pl.ds(length, length), :]),
                (ya, y_all.at[pl.ds(0, length), :]),
                (yb, y_all.at[pl.ds(length, length), :]),
            ],
            sems,
        )
        begun = weights.start(pos_ref, operands, (w_gate, w_up, w_down), sems, 4)
        written = []
        for slot, rel in enumerate(rels):
            wait(begun[slot])
            for i in range(tokens // tile):
                if slot == 0:
                    wait(first[i::2])
                at = slice(i * tile, (i + 1) * tile)
                normed, grad = n_all[at, :], y_all[at, :]
                gated = nn(normed, w_gate[slot])
                upper = nn(normed, w_up[slot])
                d_act = nt(grad, w_down[slot])
                sig = 1.0 / (1.0 + jnp.exp(-gated))
                silu = gated * sig
                act[slot, at, :] = (silu * upper).astype(BF)
                dgu[slot, at, :cols] = (
                    d_act * upper * sig * (1.0 + gated * (1.0 - sig))
                ).astype(BF)
                dgu[slot, at, cols:] = (d_act * silu).astype(BF)
            if whole and slot == 0:
                turned, sides = refs[9:]
                for s in range(depth):
                    at = slice(s * (width // depth), (s + 1) * (width // depth))
                    turned[at, :] = n_all[:, at].T
                for part in range(2):
                    out = nn(turned[...], dgu[slot, :, part * cols : (part + 1) * cols])
                    for s in range(depth):
                        at = slice(s * (width // depth), (s + 1) * (width // depth))
                        sides[part, s] = out[at].astype(BF)
                    written += start(
                        [(sides.at[part], extra[part])], sems, 4 + weights.total + 3 * n + part
                    )
            at = 4 + weights.total + 3 * slot
            written += start([(act.at[slot], acts[slot]), (dgu.at[slot], dgus[slot])], sems, at)

            def grad(s, _, slot=slot):
                made[slot, s] = tn(act[slot, :, tile_at(s, rows)], y_all[...]).astype(BF)
                return 0

            lax.fori_loop(0, depth, grad, 0)
            written += start([(made.at[slot], grads.at[:, rel])], sems, at + 2)
        wait(written)

    made = call(
        kernel,
        [shaped((tokens, cols))] * n
        + [shaped((tokens, 2 * cols))] * n
        + [shaped((depth, QUADS, rows, width))]
        + [shaped((depth, width // depth, cols))] * (2 * whole),
        pos,
        *n_two,
        *d_out,
        *weights.operands,
        *given,
        in_specs=[SCALARS] + [ANY] * (4 + count + len(given)),
        out_specs=[ANY] * (2 * n + 1 + 2 * whole),
        scratch=[
            pltpu.VMEM((tokens, width), BF),
            pltpu.VMEM((tokens, width), BF),
            *weights.scratch,
            pltpu.VMEM((n, tokens, cols), BF),
            pltpu.VMEM((n, tokens, 2 * cols), BF),
            pltpu.VMEM((n, depth, rows, width), BF),
            pltpu.SemaphoreType.DMA((4 + weights.total + 3 * n + 2,)),
        ]
        + [pltpu.VMEM((width, tokens), BF), pltpu.VMEM((2, depth, width // depth, cols), BF)]
        * whole,
        vmem=56,
        us=3 + 9 * n,
        aliases={5 + count: 2 * n} if given else None,
    )
    return made[:n], made[n : 2 * n], made[2 * n], made[2 * n + 1 :]


def ffn_grads(n_two, dgus, depth):
    length, width = n_two[0].shape
    tokens = 2 * length
    rows = width // depth
    cols = dgus[0].shape[1] // 2
    n = len(dgus)

    def kernel(na, nb, *refs):
        ins, outs, refs = refs[:n], refs[n : 3 * n], refs[3 * n :]
        n_all, dgu, turned, made, sems = refs
        first = start(
            [
                (na, n_all.at[pl.ds(0, length), :]),
                (nb, n_all.at[pl.ds(length, length), :]),
                *[(ins[rel], dgu.at[rel]) for rel in range(n)],
            ],
            sems,
        )
        wait(first[:2])
        for s in range(depth):
            at = slice(s * rows, (s + 1) * rows)
            turned[at, :] = n_all[:, at].T
        written = [[], []]
        for rel in range(n):
            first[2 + rel].wait()
            for part in range(2):
                wait(written[part])
                grads = nn(turned[...], dgu[rel, :, part * cols : (part + 1) * cols])
                for s in range(depth):
                    made[part, s] = grads[s * rows : (s + 1) * rows].astype(BF)
                written[part] = start(
                    [(made.at[part], outs[2 * rel + part])], sems, 2 + n + part
                )
        wait(written[0] + written[1])

    made = call(
        kernel,
        [shaped((depth, rows, cols))] * (2 * n),
        *n_two,
        *dgus,
        in_specs=[ANY] * (2 + n),
        out_specs=[ANY] * (2 * n),
        scratch=[
            pltpu.VMEM((tokens, width), BF),
            pltpu.VMEM((n, tokens, 2 * cols), BF),
            pltpu.VMEM((width, tokens), BF),
            pltpu.VMEM((2, depth, rows, cols), BF),
            pltpu.SemaphoreType.DMA((4 + n,)),
        ],
        us=16,
    )
    return [made[2 * rel : 2 * rel + 2] for rel in range(n)]


def ffn_product(pos, lefts, shards, gots, transposed):
    weights = Weights(shards, gots, (transposed,) * len(gots))
    tokens = lefts[0].shape[0]
    half = tokens // 2
    cols = lefts[0].shape[1] // len(gots)
    width = gots[0].own.shape[0] if transposed else gots[0].own.shape[1]
    count = len(weights.operands)

    def kernel(pos_ref, *refs):
        ins, operands, refs = refs[:QUADS], refs[QUADS : QUADS + count], refs[QUADS + count :]
        other, mine, refs = refs[0], refs[1], refs[2:]
        targets, (left, total, sems) = refs[: len(gots)], refs[len(gots) :]
        first = start([(ins[rel], left.at[rel]) for rel in range(QUADS)], sems)
        begun = weights.start(pos_ref, operands, targets, sems, QUADS)
        for rel in range(QUADS):
            first[rel].wait()
            wait(begun[rel])

            def body(i, _, rel=rel):
                at = tile_at(i, 2 * TILE)
                part = None if rel == 0 else total[at, :]
                for n, target in enumerate(targets):
                    term = (nt if transposed else nn)(
                        left[rel, at, n * cols : (n + 1) * cols], target[rel]
                    )
                    part = term if part is None else part + term
                total[at, :] = part
                return 0

            lax.fori_loop(0, tokens // (2 * TILE), body, 0)
        other[...] = total[half:, :].astype(BF)
        mine[...] = total[:half, :]

    return call(
        kernel,
        [shaped((half, width)), shaped((half, width), F32)],
        pos,
        *lefts,
        *weights.operands,
        in_specs=[SCALARS] + [ANY] * (QUADS + count),
        out_specs=[WHOLE] * 2,
        scratch=[
            *weights.scratch,
            pltpu.VMEM((QUADS, tokens, len(gots) * cols), BF),
            pltpu.VMEM((tokens, width), F32),
            pltpu.SemaphoreType.DMA((QUADS + weights.total,)),
        ],
        vmem=56,
        us=20,
    )


def rows_product(lefts, rights, half, transposed, dtype, us):
    rows = lefts[0].shape[0] // 2
    per = len(rights) // len(lefts)
    width = rights[0].shape[0] if transposed else rights[0].shape[1]
    depth = rights[0].shape[1] if transposed else rights[0].shape[0]
    steps = rows // TILE

    def kernel(*refs):
        left, right, out = refs[: len(lefts)], refs[len(lefts) : -1], refs[-1]
        total = None
        for i, ref in enumerate(right):
            part = left[i // per][:, (i % per) * depth : (i % per + 1) * depth]
            term = (nt if transposed else nn)(part, ref[...])
            total = term if total is None else total + term
        out[...] = total.astype(dtype)

    return call(
        kernel,
        shaped((rows, width), dtype),
        *lefts,
        *rights,
        grid=(steps,),
        in_specs=[
            pl.BlockSpec((TILE, left.shape[1]), lambda i: (i + half * steps, 0)) for left in lefts
        ]
        + [pl.BlockSpec(right.shape, lambda i: (0, 0)) for right in rights],
        out_specs=pl.BlockSpec((TILE, width), lambda i: (i, 0)),
        vmem=56,
        us=us,
    )


def mix_back(low, other, mixed, weight):
    length, width = low.shape
    inner = mixed.shape[1]

    def kernel(a, b, mixed_ref, weight_ref, d_mixed, grad):
        for i in range(2 * length // TILE):
            at = slice(i * TILE, (i + 1) * TILE)
            part = a if i < length // TILE else b
            first = i * TILE % length
            d_mixed[at, :] = nt(part[first : first + TILE, :], weight_ref[...]).astype(BF)

        def body(i, _):
            at = tile_at(i, TILE)
            grad[at, :] = (
                tn(mixed_ref[:length, at], a[...]) + tn(mixed_ref[length:, at], b[...])
            ).astype(BF)
            return 0

        lax.fori_loop(0, inner // TILE, body, 0)

    return call(
        kernel,
        [shaped((2 * length, inner)), shaped((inner, width))],
        low,
        other,
        mixed,
        weight,
        in_specs=[WHOLE] * 4,
        out_specs=[WHOLE] * 2,
        us=10,
    )


def attention_grads(links, pos, normed, d_qkv, grad_out, deep, depth, rows, low):
    width, cols = normed.shape[1], d_qkv.shape[1]
    quarter = rows // QUADS
    small = quarter // 2
    high = quarter - low + small
    more = deep.shape[1] // (2 * depth)

    def kernel(pos_ref, normed_ref, d_ref, out_ref, deep_ref, *refs):
        outs, tile = refs[:-1], refs[-1]
        k = pos_ref[1]

        def body(s, _):
            tile[...] = tn(normed_ref[:, tile_at(s, rows)], d_ref[...]).astype(BF)
            for rel in range(QUADS):
                j = k ^ rel
                first = pl.multiple_of(j * quarter, 16)
                to_low, to_high = outs[2 * rel : 2 * rel + 2]
                to_low[s, :low] = tile[pl.ds(first, low), :]
                to_high[s, : quarter - low] = tile[pl.ds(first + low, quarter - low), :]
                at = pl.multiple_of(s * (rows // 2) + j * small, 16)
                to_high[s, quarter - low : high] = out_ref[pl.ds(at, small), :]
                at = pl.multiple_of(s * more, 16)
                to_low[s, low:] = deep_ref[rel, pl.ds(at, more), :]
                to_high[s, high:] = deep_ref[rel, pl.ds(at + depth * more, more), :]
            return 0

        lax.fori_loop(0, depth, body, 0)

    made = call(
        kernel,
        [shaped((depth, n + more, cols)) for _ in range(QUADS) for n in (low, high)],
        pos,
        normed,
        d_qkv,
        grad_out,
        deep,
        in_specs=[SCALARS] + [WHOLE] * 4,
        out_specs=[WHOLE] * (2 * QUADS),
        scratch=[pltpu.VMEM((rows, cols), BF)],
        us=10,
    )
    return Summed(links, *[made[2 * rel : 2 * rel + 2] for rel in range(QUADS)])


def unpack_columns(pos, mine, other, depth, half):
    cols = mine.shape[2]
    rows = D // depth
    seg = cols // depth
    width = cols * 2 * QUADS
    tile = 128
    steps = rows // tile

    def kernel(pos_ref, a, b, out):
        k, c = pos_ref[1], pos_ref[2]
        for ref, core in ((a, c), (b, 1 - c)):
            for rel in range(QUADS):
                block = core * QUADS + (k ^ rel)
                for s in range(depth):
                    at = pl.multiple_of((s * 2 * QUADS + block) * seg, 128)
                    out[:, pl.ds(at, seg)] = ref[rel, :, s * seg : (s + 1) * seg].astype(F32)

    spec = pl.BlockSpec((QUADS, tile, cols), lambda i: (0, i + half * steps, 0))
    return call(
        kernel,
        shaped((rows, width), F32),
        pos,
        mine,
        other,
        grid=(steps,),
        in_specs=[SCALARS, spec, spec],
        out_specs=pl.BlockSpec((tile, width), lambda i: (i, 0)),
        vmem=60,
        us=4,
    )


def unpack_rows(pos, mine, other, rows, width, first):
    tile = mine.shape[2]

    def kernel(pos_ref, a, b, out):
        k, c = pos_ref[1], pos_ref[2]
        for ref, core in ((a, c), (b, 1 - c)):
            for rel in range(QUADS):
                at = pl.multiple_of((core * QUADS + (k ^ rel)) * rows, 8)
                out[pl.ds(at, rows), :] = ref[rel].astype(F32)

    spec = pl.BlockSpec((QUADS, rows, tile), lambda i: (0, first // rows + i, 0))
    return call(
        kernel,
        shaped((2 * QUADS * rows, width), F32),
        pos,
        mine,
        other,
        grid=(width // tile,),
        in_specs=[SCALARS, spec, spec],
        out_specs=pl.BlockSpec((2 * QUADS * rows, tile), lambda i: (0, i)),
        vmem=60,
        us=5,
    )


def unpack_attention(pos, mine, other, depth, rows, inner, narrow):
    quarter = rows // QUADS
    small = quarter // 2

    def kernel(pos_ref, a, b, *outs):
        k, c = pos_ref[1], pos_ref[2]

        def place(first, second):
            for core, ref in ((0, first), (1, second)):
                for rel in range(QUADS):
                    j = k ^ rel
                    at = pl.ds(pl.multiple_of(j * quarter, 8), quarter)
                    cols = 0
                    for out, width in zip(outs[:3], (inner, narrow, narrow)):
                        seg = width // depth
                        for s in range(depth):
                            to = (2 * s + core) * seg
                            out[at, to : to + seg] = ref[
                                rel, :quarter, cols : cols + seg
                            ].astype(F32)
                            cols += seg
                    at = pl.ds(pl.multiple_of(core * (rows // 2) + j * small, 8), small)
                    outs[3][at, :] = ref[rel, quarter:, :].astype(F32)

        @pl.when(c == 0)
        def _():
            place(a, b)

        @pl.when(c == 1)
        def _():
            place(b, a)

    return call(
        kernel,
        [
            shaped((rows, 2 * inner), F32),
            shaped((rows, 2 * narrow), F32),
            shaped((rows, 2 * narrow), F32),
            shaped((rows, 2 * inner), F32),
        ],
        pos,
        mine,
        other,
        in_specs=[SCALARS] + [WHOLE] * 2,
        out_specs=[WHOLE] * 4,
        us=6,
    )


def on_device(
    reps,
    depth,
    tokens,
    gain_attn,
    w_query,
    w_key,
    w_value,
    w_out,
    gain_ffn,
    w_gate,
    w_up,
    w_down,
    cotangent,
):
    links = Links(reps, depth)
    z = lax.axis_index("fsdp")
    r = lax.axis_index("rep")
    c = r % 2
    k = (r // 2) % QUADS
    pos = jnp.stack([z, k, c]).astype(jnp.int32)
    length = tokens.shape[0]
    rows = w_query.shape[0]
    quarter = rows // QUADS
    small = quarter // 2
    inner = D // 2
    narrow = inner // (HEADS // KV)

    def core_columns(weight):
        split = weight.reshape(rows, depth, 2, weight.shape[1] // (2 * depth))
        return lax.dynamic_index_in_dim(split, c, 2, keepdims=False).reshape(rows, -1)

    shard_qkv = jnp.concatenate([core_columns(i) for i in (w_query, w_key, w_value)], axis=1)
    shard_out = lax.dynamic_slice_in_dim(w_out, c * (rows // 2), rows // 2, 0)
    piece_qkv = lax.dynamic_slice_in_dim(shard_qkv, k * quarter, quarter, 0)
    piece_out = lax.dynamic_slice_in_dim(shard_out, k * small, small, 0)
    seg = w_gate.shape[1] // (depth * 2 * QUADS)
    d_rows = w_down.shape[0] // (2 * QUADS)

    def block_columns(weight):
        return jnp.concatenate(
            [
                lax.dynamic_slice_in_dim(weight, ((s * 2 + c) * QUADS + k) * seg, seg, 1)
                for s in range(depth)
            ],
            axis=1,
        )

    piece_gate, piece_up = block_columns(w_gate), block_columns(w_up)
    piece_down = lax.dynamic_slice_in_dim(w_down, (c * QUADS + k) * d_rows, d_rows, 0)

    gains = jnp.stack([gain_attn, gain_ffn])
    gains = jnp.stack([gains] + [links.shift(gains, by) for by in range(1, depth)])
    gains = jnp.take(gains, (z - jnp.arange(depth)) % depth, axis=0)
    g_one = gains[:, 0].reshape(1, -1).astype(F32)
    g_two = gains[:, 1].reshape(1, -1).astype(F32)
    token_pair = (tokens, links.swap(tokens, 1))
    d_pair = (cotangent, links.swap(cotangent, 1))
    turns = tables(length)

    piece = jnp.concatenate([piece_qkv, piece_out], axis=0)
    early = after(pos, token_pair[1], d_pair[1])
    got_attn = links.spread(piece, 224)
    got_gate = links.spread(piece_gate, 3 * rows // 2)
    got_up = links.spread(after(piece_up, got_attn.own), 3 * rows // 2)
    got_down = links.spread(after(piece_down, got_gate.own), 3 * d_rows // 2)
    got_attn.compact(early)
    got_attn.to_plane()
    got_attn.to_corner()
    got_gate.compact(after(pos, *got_attn.corner, g_one, g_two))
    got_gate.to_plane()
    n_one, q, key, value, wqkv = project(pos, token_pair, g_one, got_attn, shard_qkv, turns)
    got_up.compact(after(pos, q))
    got_up.to_plane()
    got_gate.parts = [after(i, got_up.remote) for i in got_gate.parts]
    got_gate.to_corner()

    mixed, lse = attend(q, key, value)
    got_down.compact(after(pos, lse))
    got_down.to_plane()
    got_up.to_corner()
    got_down.to_corner()
    to_other, mine, wo = mix(pos, mixed, got_attn, shard_out)
    ready = after(to_other, *got_gate.corner, got_up.x, got_up.y, got_down.remote)
    hidden, n_two = residual_norm(tokens, mine, links.swap(ready, 1), g_two)

    n_pair = (n_two, links.swap(n_two, 1))
    shards, gots = (w_gate, w_up, w_down), (got_gate, got_up, got_down)
    acts, dgus, deep, _ = ffn_forward(pos, (0, 1, 2), n_pair, d_pair, shards, gots, None)
    at = after(pos, dgus[-1])
    act, dgu, deep, corner = ffn_forward(at, (3,), n_pair, d_pair, shards, gots, deep, True)
    acts, dgus = [*acts, *act], [*dgus, *dgu]
    deep_sum = links.over_depth(deep)
    half = d_rows // 2
    others = ffn_grads(n_pair, [after(i, corner[0]) for i in dgus[:3]], depth)
    wide = Summed(links, *others, corner)
    lefts = [after(i, wide.own[0]) for i in dgus]
    to_other, mine = ffn_product(pos, lefts, (w_gate, w_up), (got_gate, got_up), True)
    wide.add()
    acts = [after(i, to_other, *wide.added) for i in acts]
    out_other, out_mine = ffn_product(pos, acts, (w_down,), (got_down,), False)
    received = links.swap(to_other, 1)
    mine = after(mine, out_mine, *wide.second)
    d_hidden, grad_g_two, low = norm_back(mine, received, hidden, cotangent, g_two, 1)

    low_pair = low, links.swap(after(low, *wide.added), 1)
    d_mixed, grad_out = mix_back(*low_pair, mixed, wo)
    d_qkv = attend_back(q, key, value, lse, d_mixed, turns)
    deep_sum = after(deep_sum, d_qkv)
    small = attention_grads(links, pos, n_one, d_qkv, grad_out, deep_sum, depth, rows, 80)
    (sums_wide,) = wide.total([small.own[0]])
    late = after(d_qkv, sums_wide)
    sums_wide = links.over_depth(sums_wide)
    to_other = rows_product([late], [wqkv], 1, True, BF, 7)
    mine = rows_product([late], [wqkv], 0, True, F32, 7)
    out_received = links.swap(after(out_other, d_hidden), 1)
    result = (hidden + out_mine + out_received.astype(F32)).astype(BF)
    small.add()
    sums_attn, sums_deep = small.total(more=half // depth)
    sums_deep = sums_deep.reshape(d_rows, -1)
    split = sums_deep.shape[1] // sums_wide.shape[1]
    sums_ffn = jnp.concatenate([sums_wide, *jnp.split(sums_deep, split, axis=1)], axis=0)
    ffn_x, ffn_y = links.both(*[after(sums_ffn, sums_attn)] * 2)
    received = links.swap(after(to_other, mine, result, ffn_x, ffn_y), 1)
    input_grad, grad_g_one = norm_back(mine, received, tokens, d_hidden, g_one, 0)
    gain_sums = jnp.concatenate([grad_g_one, grad_g_two], axis=0)
    sums_attn = links.over_depth(sums_attn)
    cut = sums_ffn.shape[0] // 2
    ffn_corner = links.both(ffn_y[:cut], ffn_x[cut:])

    def stacked(own, along_x, along_y, corner, *earlier):
        mine = jnp.stack([own, along_x, along_y, jnp.concatenate(corner, axis=0)])
        return mine, links.swap(after(mine, *earlier), 1)

    sums_attn = after(sums_attn, received)
    attn_x, attn_y = links.both(sums_attn, sums_attn)
    ffn_pair = stacked(sums_ffn, ffn_x, ffn_y, ffn_corner, attn_x, attn_y, input_grad)
    attn_corner = links.both(attn_y[:80], attn_x[80:])
    attn_pair = stacked(sums_attn, attn_x, attn_y, attn_corner)
    gain_sums = gain_sums + links.swap(after(gain_sums, attn_x, attn_y), 1)
    share_gate = unpack_columns(pos, *ffn_pair, depth, 0)
    gain_sums = gain_sums + links.swap(after(gain_sums, share_gate), 2)
    share_up = unpack_columns(after(pos, share_gate), *ffn_pair, depth, 1)
    gain_sums = gain_sums + links.swap(after(gain_sums, share_up), 4)
    gain_sums = links.cells(gain_sums).reshape(2, depth, rows)
    share_down = unpack_rows(after(pos, share_up), *ffn_pair, d_rows, D, 2 * rows)

    def own_part(at):
        part = lax.dynamic_index_in_dim(gain_sums, at % depth, 1, keepdims=False)
        return after(part, share_down)

    own_gains = own_part(z)
    for by in range(1, depth):
        own_gains = own_gains + links.shift(own_part(z + by), by)
    share_q, share_k, share_v, share_out = unpack_attention(
        after(pos, share_down), *attn_pair, depth, rows, inner, narrow
    )
    return (
        result,
        input_grad,
        own_gains[0],
        share_q,
        share_k,
        share_v,
        share_out,
        own_gains[1],
        share_gate,
        share_up,
        share_down,
    )


def solution(mesh):
    tokens = P(("rep", "fsdp"), None)
    gain, weight = P("fsdp"), P("fsdp", None)
    return jax.shard_map(
        functools.partial(on_device, mesh.shape["rep"], mesh.shape["fsdp"]),
        mesh=mesh,
        in_specs=(tokens, gain, *[weight] * 4, gain, *[weight] * 3, tokens),
        out_specs=(tokens, tokens, gain, *[weight] * 4, gain, *[weight] * 3),
        check_vma=False,
    )
```
